512 devices in a mesh: space: 64 (over z_lo, x, core), head: 8 (over z_hi, y).
Axes of the slice: x: 4, y: 4, z: 16 (z_hi: 2, z_lo: 8; z = z_hi * 8 + z_lo), core: 2. Of those that a mesh axis runs over, the one named last changes fastest.
Arguments:
- fields: bfloat16 [512, 32, 2, 1024], P('space', None, None, 'head'), may hold values from -1.796875 to 1.796875
- ln_gain: float32 [1024], replicated, may hold values from 0.1 to 1.9
- w_qkv: bfloat16 [1024, 3, 1024], P(None, None, 'head'), may hold values from -0.1875 to 0.1875
- attn_bias: float32 [16, 128, 128], P('head'), may hold values from -6 to 340
- w_out: bfloat16 [1024, 1024], P('head'), may hold values from -0.1875 to 0.1875
- merge_gain: float32 [4096], replicated, may hold values from 0.1 to 1.9
- w_merge: bfloat16 [4096, 2048], P(None, 'head'), may hold values from -0.09375 to 0.09375
Outputs:
- merged: bfloat16 [256, 16, 2, 2048], P('space', None, None, 'head')
The draws below stay inside these ranges and needn't reach their ends.
All inputs are finite; a program needn't handle non-finite values.
Results may differ from the reference program's by a relative error of at most 0.02.
Values may be sent and summed in bfloat16 or wider, within the bound.
No kernel may reach another device: no remote copies, remote signals or barrier semaphores. Data moves between devices by JAX's collectives and lax.ppermute only.
A program may use at most 64 MiB of HBM per device.

```python
import jax
import jax.numpy as jnp
from jax import lax

D = 1024
HEADS = 16
HEAD_DIM = 64
WIN_LAT = 8
WIN_LON = 8
WIN_LEV = 2
LEVELS = 2
LON = 32
WINDOW = 128
LAT = 512
N_HEAD = 8


def draw_attn_bias(key, part):
    key = jax.random.fold_in(key, 11)
    keys_list = jax.random.split(key, 1)
    base = jnp.clip(jax.random.normal(keys_list[0], (HEADS, WINDOW, WINDOW), jnp.float32), -6.0, 6.0)
    return base


def block_levels(own_key, dims, cuts, smallest, high):
    level, own = 1.0, jax.random.fold_in(own_key, 6)
    for dim, blocks in cuts:
        steps = jnp.exp(jax.random.uniform(jax.random.fold_in(own, dim), (blocks,), jnp.float32, smallest / len(cuts), high / len(cuts)))
        level = level * jnp.repeat(steps, dims[dim] // blocks).reshape([-1 if axis == dim else 1 for axis in range(len(dims))])
    return level


def normal_values(key, extent, deviation, most, cuts=(), dtype=jnp.bfloat16):
    factor_of = block_levels(key, extent, cuts, -0.22, 0.18) if cuts else 1.0
    result = jax.random.normal(key, extent, jnp.float32) * deviation * factor_of
    return jnp.minimum(jnp.maximum(result, -most), most).astype(dtype)


def setup_inputs(seed: int = 0) -> dict:
    key_list = jax.random.split(jax.random.key(seed), 8)
    fields = normal_values(key_list[0], (LAT, LON, LEVELS, D), 0.3, 1.796875, ((0, 64), (3, 8)))
    ln_gain = jnp.clip(1.0 + 0.18 * jax.random.normal(key_list[1], (D,), jnp.float32), 0.1, 1.9)
    w_qkv = normal_values(key_list[2], (D, 3, D), D ** -0.5, 0.1875, ((2, 8),))
    attn_bias = draw_attn_bias(jax.random.fold_in(key_list[7], 71), 0)
    w_out = normal_values(key_list[4], (D, D), D ** -0.5, 0.1875, ((0, 8),))
    merge_gain = jnp.clip(1.0 + 0.18 * jax.random.normal(key_list[5], (4 * D,), jnp.float32), 0.1, 1.9)
    w_merge = normal_values(key_list[6], (4 * D, 2 * D), (4 * D) ** -0.5, 0.09375, ((1, 8),))
    return dict(fields=fields, ln_gain=ln_gain, w_qkv=w_qkv, attn_bias=attn_bias, w_out=w_out, merge_gain=merge_gain, w_merge=w_merge)


EPS = 1e-05

def layer_norm(widened, gain):
    mean_rows = lax.optimization_barrier(jnp.mean(widened, -1, keepdims=True))
    spread = lax.optimization_barrier(jnp.mean(widened * widened, -1, keepdims=True)) - mean_rows * mean_rows
    return (widened - mean_rows) * lax.rsqrt(spread + EPS) * gain

def window_split(band_rows):
    lat_rows, lon_cells, level_count, features = band_rows.shape
    windows = band_rows.reshape(lat_rows, lon_cells // WIN_LON, WIN_LON, level_count // WIN_LEV, WIN_LEV, features)
    windows = windows.transpose(1, 3, 0, 2, 4, 5)
    return windows.reshape(-1, lat_rows * WIN_LON * WIN_LEV, features)

def window_join(windows, lat_rows, lon_cells, level_count):
    features = windows.shape[-1]
    grid = windows.reshape(lon_cells // WIN_LON, level_count // WIN_LEV, lat_rows, WIN_LON, WIN_LEV, features)
    grid = grid.transpose(2, 0, 3, 1, 4, 5)
    return grid.reshape(lat_rows, lon_cells, level_count, features)

def attend_windows(windows, attn_bias):
    queries = windows[:, :, 0].astype(jnp.float32)
    key_rows = windows[:, :, 1].astype(jnp.float32)
    value_rows = windows[:, :, 2].astype(jnp.float32)
    scores = jnp.einsum('wphe,wqhe->whpq', queries, key_rows) * HEAD_DIM ** (-0.5) + attn_bias[None]
    highest = lax.optimization_barrier(jnp.max(scores, -1, keepdims=True))
    exponent = jnp.exp(scores - highest)
    weights = (exponent / lax.optimization_barrier(jnp.sum(exponent, -1, keepdims=True))).astype(jnp.bfloat16)
    return jnp.einsum('whpq,wqhe->wphe', weights.astype(jnp.float32), value_rows).astype(jnp.bfloat16)

def reference(fields, ln_gain, w_qkv, attn_bias, w_out, merge_gain, w_merge):
    shifted = jnp.roll(fields, (-(WIN_LAT // 2), -(WIN_LON // 2), -(WIN_LEV // 2)), axis=(0, 1, 2))
    bands = shifted.reshape(LAT // WIN_LAT, WIN_LAT, LON, LEVELS, D)
    flat_qkv = w_qkv.reshape(D, 3 * D)
    group_rows = w_out.reshape(N_HEAD, D // N_HEAD, D).astype(jnp.float32)

    def one_band(band_rows):
        widened = band_rows.astype(jnp.float32)
        normed = layer_norm(widened, ln_gain).astype(jnp.bfloat16)
        projected = jnp.dot(normed.reshape(-1, D), flat_qkv, preferred_element_type=jnp.float32).astype(jnp.bfloat16)
        windows = window_split(projected.reshape(WIN_LAT, LON, LEVELS, 3 * D))
        windows = windows.reshape(windows.shape[0], WINDOW, 3, HEADS, HEAD_DIM)
        attended = attend_windows(windows, attn_bias)
        attended = window_join(attended.reshape(-1, WINDOW, D), WIN_LAT, LON, LEVELS)
        grouped = attended.reshape(-1, N_HEAD, D // N_HEAD).astype(jnp.float32)
        partial_value = jnp.einsum('tgf,gfd->tgd', grouped, group_rows).astype(jnp.bfloat16)
        total = lax.optimization_barrier(jnp.sum(partial_value.astype(jnp.float32), axis=1))
        return (widened + total.reshape(WIN_LAT, LON, LEVELS, D)).astype(jnp.bfloat16)
    updated = lax.map(one_band, bands).reshape(LAT, LON, LEVELS, D)
    restored = jnp.roll(updated, (WIN_LAT // 2, WIN_LON // 2, WIN_LEV // 2), axis=(0, 1, 2))
    quads = restored.reshape(LAT // 2, 2, LON // 2, 2, LEVELS, D).transpose(0, 2, 4, 3, 1, 5)
    quads = quads.reshape(LAT // 2, LON // 2, LEVELS, 4 * D)
    merge_normed = layer_norm(quads.astype(jnp.float32), merge_gain).astype(jnp.bfloat16)
    merged = jnp.dot(merge_normed.reshape(-1, 4 * D), w_merge, preferred_element_type=jnp.float32)
    return merged.reshape(LAT // 2, LON // 2, LEVELS, 2 * D).astype(jnp.bfloat16)
```

```python
import jax
import jax.numpy as jnp
import numpy as np
from jax import lax
from jax.experimental import pallas as pl
from jax.experimental.pallas import tpu as pltpu
from jax.sharding import PartitionSpec as P

D = 1024
HEAD_DIM = 64
BLOCK = 128
TOKENS = 512
HALF = 256
WINDOWS = 4
EPS = 1e-05
Y_GROUPS = [[0, 1, 2, 3], [4, 5, 6, 7]]
BOTH = ("space", "head")


def place(index):
    space, head = divmod(index, 8)
    z_lo, rest = divmod(space, 8)
    x, core = divmod(rest, 2)
    return z_lo, x, core, head


def moved(value, move):
    pairs = []
    for source in range(512):
        z_lo, x, core, head = move(*place(source))
        pairs.append((source, ((z_lo * 4 + x) * 2 + core) * 8 + head))
    return lax.ppermute(value, BOTH, pairs)


def across_z(value):
    return moved(value, lambda z_lo, x, core, head: (z_lo, x, core, head ^ 4))


def along_x(value, steps):
    return moved(value, lambda z_lo, x, core, head: (z_lo, (x + steps) % 4, core, head))


def other_core(value):
    return moved(value, lambda z_lo, x, core, head: (z_lo, x, core ^ 1, head))


def along_bands(value, steps):
    return lax.ppermute(value, "space", [(s, (s + steps) % 64) for s in range(64)])


def gathered_y(value):
    spread = jnp.broadcast_to(value[None], (4,) + value.shape)
    return lax.all_to_all(spread, "head", 0, 0, axis_index_groups=Y_GROUPS)


def half_order():
    p = np.arange(HALF)
    level, j, i = p & 1, (p >> 1) & 3, (p >> 3) & 1
    window, di, dj = (p >> 4) & 3, (p >> 6) & 1, (p >> 7) & 1
    row = 2 * i + di
    lon = (8 * window + 2 * j + dj + 4) % 32
    return row * 64 + lon * 2 + level


def window_order():
    p = np.arange(128)
    level, j, i = p & 1, (p >> 1) & 3, (p >> 3) & 1
    di, dj, half = (p >> 4) & 1, (p >> 5) & 1, (p >> 6) & 1
    return (half * 4 + 2 * i + di) * 16 + (2 * j + dj) * 2 + (1 - level)


def merged_order():
    o = np.arange(128)
    half, i, lon, level = o >> 6, (o >> 5) & 1, (o >> 1) & 15, o & 1
    back = (lon - 2) % 16
    return half * 64 + (back >> 2) * 16 + i * 8 + (back & 3) * 2 + level


def one_hot(order, dtype):
    return jnp.asarray(np.eye(len(order), dtype=np.float32)[order], dtype)


def dot(left, right):
    return jnp.dot(left, right, preferred_element_type=jnp.float32)


def window_rows(window):
    return [half * HALF + quad * 64 + window * 16 for half in range(2) for quad in range(4)]


def attention_kernel(own_ref, partner_ref, gain_ref, w_ref, bias_ref, out_ref, qkv_ref):
    z_hi = lax.axis_index("head") // 4
    parts = ((own_ref, z_hi), (partner_ref, 1 - z_hi))
    for start in range(0, TOKENS, 128):
        rows = slice(start, start + 128)
        total = jnp.zeros((128, BLOCK), jnp.float32)
        squares = jnp.zeros((128, BLOCK), jnp.float32)
        for ref, _ in parts:
            for y in range(4):
                value = ref[y, rows, :].astype(jnp.float32)
                total += value
                squares += value * value
        mean = jnp.sum(total, -1, keepdims=True) * (1.0 / D)
        spread = jnp.sum(squares, -1, keepdims=True) * (1.0 / D) - mean * mean
        scale = lax.rsqrt(spread + EPS)
        product = jnp.zeros((128, 3 * BLOCK), jnp.float32)
        for ref, z in parts:
            normed = jnp.concatenate(
                [
                    ((ref[y, rows, :].astype(jnp.float32) - mean) * scale * gain_ref[z * 4 + y]).astype(jnp.bfloat16)
                    for y in range(4)
                ],
                axis=1,
            )
            product += dot(normed, w_ref[z])
        qkv_ref[rows, :] = product.astype(jnp.bfloat16)
    for window in range(WINDOWS):
        starts = window_rows(window)
        cells = jnp.concatenate([qkv_ref[s : s + 16, :] for s in starts], axis=0)
        heads = []
        for head in range(2):
            at = head * HEAD_DIM
            queries = cells[:, at : at + HEAD_DIM]
            keys = cells[:, BLOCK + at : BLOCK + at + HEAD_DIM]
            values = cells[:, 2 * BLOCK + at : 2 * BLOCK + at + HEAD_DIM]
            scores = lax.dot_general(queries, keys, (((1,), (1,)), ((), ())), preferred_element_type=jnp.float32)
            scores = scores * HEAD_DIM ** (-0.5) + bias_ref[head]
            exponent = jnp.exp(scores - jnp.max(scores, -1, keepdims=True))
            weights = (exponent / jnp.sum(exponent, -1, keepdims=True)).astype(jnp.bfloat16)
            heads.append(dot(weights, values))
        attended = jnp.concatenate(heads, axis=1).astype(jnp.bfloat16)
        for piece, s in enumerate(starts):
            out_ref[s : s + 16, :] = attended[piece * 16 : piece * 16 + 16, :]


def merge_kernel(own_ref, partner_ref, own_att_ref, partner_att_ref, w_out_ref, gain_ref, w_ref, order_ref, out_ref, updated_ref):
    z_hi = lax.axis_index("head") // 4
    space = lax.axis_index("space")
    my_core = space % 2
    my_x = (space // 2) % 4
    attended = jnp.concatenate([ref[y] for ref in (own_att_ref, partner_att_ref) for y in range(4)], axis=1)
    for z_rel in range(2):
        stream_ref = (own_ref, partner_ref)[z_rel]
        z = z_hi if z_rel == 0 else 1 - z_hi
        for pair in range(2):
            x_rel = (z * 2 + pair - my_x + 4) % 4
            w_block = jnp.concatenate(
                [w_out_ref[(core + my_core) % 2, x_rel].reshape(D, BLOCK) for core in range(2)], axis=1
            )
            stream = jnp.concatenate([stream_ref[2 * pair + k, :TOKENS, :] for k in range(2)], axis=1)
            value = stream.astype(jnp.float32) + dot(attended, w_block)
            at = z_rel * 512 + pair * 256
            updated_ref[:, at : at + 256] = value.astype(jnp.bfloat16)

    def quad(k):
        return jnp.concatenate(
            [updated_ref[half * HALF + k * 64 : half * HALF + k * 64 + 64, :] for half in range(2)], axis=0
        ).astype(jnp.float32)

    total = jnp.zeros((128, 1), jnp.float32)
    squares = jnp.zeros((128, 1), jnp.float32)
    for k in range(4):
        value = quad(k)
        total += jnp.sum(value, -1, keepdims=True)
        squares += jnp.sum(value * value, -1, keepdims=True)
    mean = total * (1.0 / (4 * D))
    scale = lax.rsqrt(squares * (1.0 / (4 * D)) - mean * mean + EPS)
    merged = jnp.zeros((128, 256), jnp.float32)
    for k in range(4):
        value = (quad(k) - mean) * scale
        for z_rel in range(2):
            z = z_hi if z_rel == 0 else 1 - z_hi
            normed = (value[:, z_rel * 512 : z_rel * 512 + 512] * gain_ref[k * 2 + z]).astype(jnp.bfloat16)
            merged += dot(normed, w_ref[k * 2 + z])
    out_ref[...] = dot(order_ref[...], merged.astype(jnp.bfloat16)).astype(jnp.bfloat16)


def in_vmem(count):
    return [pl.BlockSpec(memory_space=pltpu.VMEM)] * count


def on_device(fields, ln_gain, w_qkv, attn_bias, w_out, merge_gain, w_merge):
    rows = fields.reshape(2, HALF, BLOCK)
    ordered = jnp.einsum(
        "pt,htf->hpf", one_hot(half_order(), jnp.bfloat16), rows, preferred_element_type=jnp.bfloat16
    )
    following = along_bands(ordered[0], -1)
    column = lax.axis_index("space") % 8
    w_piece = lax.dynamic_slice(w_out, (0, column * BLOCK), (BLOCK, BLOCK))
    mine = jnp.concatenate([ordered[1], following, w_piece], axis=0)
    partners = across_z(mine)
    own = gathered_y(mine)
    partner = gathered_y(partners)

    bias_hot = one_hot(window_order(), jnp.float32)
    bias = jnp.einsum("pa,hab->hpb", bias_hot, attn_bias, precision=lax.Precision.HIGHEST)
    bias = jnp.einsum("hpb,qb->hpq", bias, bias_hot, precision=lax.Precision.HIGHEST)
    w_qkv_flat = w_qkv.reshape(2, D // 2, 3 * BLOCK)
    attended = pl.pallas_call(
        attention_kernel,
        out_shape=jax.ShapeDtypeStruct((TOKENS, BLOCK), jnp.bfloat16),
        in_specs=in_vmem(5),
        out_specs=pl.BlockSpec(memory_space=pltpu.VMEM),
        scratch_shapes=[pltpu.VMEM((TOKENS, 3 * BLOCK), jnp.bfloat16)],
        compiler_params=pltpu.CompilerParams(vmem_limit_bytes=48 * 2**20),
        cost_estimate=pl.CostEstimate(flops=600_000_000, bytes_accessed=3_000_000, transcendentals=131072),
        name="attention",
    )(own, partner, ln_gain.reshape(8, 1, BLOCK), w_qkv_flat, bias)

    pieces = jnp.concatenate([own[:, TOKENS:], partner[:, TOKENS:]], axis=0)
    over_x = jnp.stack([pieces, along_x(pieces, -1), along_x(pieces, -2), along_x(pieces, -3)])
    w_out_whole = jnp.stack([over_x, other_core(over_x)])

    partner_attended = across_z(attended)
    own_all = gathered_y(attended)
    partner_all = gathered_y(partner_attended)
    merged = pl.pallas_call(
        merge_kernel,
        out_shape=jax.ShapeDtypeStruct((128, 256), jnp.bfloat16),
        in_specs=in_vmem(8),
        out_specs=pl.BlockSpec(memory_space=pltpu.VMEM),
        scratch_shapes=[pltpu.VMEM((TOKENS, D), jnp.bfloat16)],
        compiler_params=pltpu.CompilerParams(vmem_limit_bytes=48 * 2**20),
        cost_estimate=pl.CostEstimate(flops=1_400_000_000, bytes_accessed=7_000_000, transcendentals=0),
        name="merge",
    )(
        own,
        partner,
        own_all,
        partner_all,
        w_out_whole,
        merge_gain.reshape(8, 1, 512),
        w_merge.reshape(8, 512, 256),
        one_hot(merged_order(), jnp.bfloat16),
    )
    lower = along_bands(merged[64:], 1)
    return jnp.concatenate([lower, merged[:64]], axis=0).reshape(4, 16, 2, 256)


def solution(mesh):
    placed = (
        P("space", None, None, "head"),
        P(),
        P(None, None, "head"),
        P("head", None, None),
        P("head", None),
        P(),
        P(None, "head"),
    )
    return jax.shard_map(
        on_device,
        mesh=mesh,
        in_specs=placed,
        out_specs=P("space", None, None, "head"),
        check_vma=False,
    )
```

```python
import jax
import jax.numpy as jnp
import numpy as np
from jax import lax
from jax.experimental import pallas as pl
from jax.experimental.pallas import tpu as pltpu
from jax.sharding import PartitionSpec as P

D = 1024
HEAD_DIM = 64
BLOCK = 128
TOKENS = 512
HALF = 256
WINDOWS = 4
EPS = 1e-05
BOTH = ("space", "head")


def place(index):
    space, head = divmod(index, 8)
    z_lo, rest = divmod(space, 8)
    x, core = divmod(rest, 2)
    return z_lo, x, core, head


def moved(value, move):
    pairs = []
    for source in range(512):
        z_lo, x, core, head = move(*place(source))
        pairs.append((source, ((z_lo * 4 + x) * 2 + core) * 8 + head))
    return lax.ppermute(value, BOTH, pairs)


def across_z(value):
    return moved(value, lambda z_lo, x, core, head: (z_lo, x, core, head ^ 4))


def along_x(value, steps):
    return moved(value, lambda z_lo, x, core, head: (z_lo, (x + steps) % 4, core, head))


def other_core(value):
    return moved(value, lambda z_lo, x, core, head: (z_lo, x, core ^ 1, head))


def along_bands(value, steps):
    return lax.ppermute(value, "space", [(s, (s + steps) % 64) for s in range(64)])


def along_y(value, steps):
    return moved(value, lambda z_lo, x, core, head: (z_lo, x, core, (head & 4) + (head - steps) % 4))


def gathered_y(value):
    return [value] + [along_y(value, steps) for steps in (1, 2, 3)]


def half_order():
    p = np.arange(HALF)
    level, j, i = p & 1, (p >> 1) & 3, (p >> 3) & 1
    window, di, dj = (p >> 4) & 3, (p >> 6) & 1, (p >> 7) & 1
    row = 2 * i + di
    lon = (8 * window + 2 * j + dj + 4) % 32
    return row * 64 + lon * 2 + level


def window_order():
    p = np.arange(128)
    level, j, i = p & 1, (p >> 1) & 3, (p >> 3) & 1
    di, dj, half = (p >> 4) & 1, (p >> 5) & 1, (p >> 6) & 1
    return (half * 4 + 2 * i + di) * 16 + (2 * j + dj) * 2 + (1 - level)


def merged_order():
    o = np.arange(128)
    half, i, lon, level = o >> 6, (o >> 5) & 1, (o >> 1) & 15, o & 1
    back = (lon - 2) % 16
    return half * 64 + (back >> 2) * 16 + i * 8 + (back & 3) * 2 + level


def one_hot(order, dtype):
    return jnp.asarray(np.eye(len(order), dtype=np.float32)[order], dtype)


def dot(left, right):
    return jnp.dot(left, right, preferred_element_type=jnp.float32)


def window_rows(window):
    return [half * HALF + quad * 64 + window * 16 for half in range(2) for quad in range(4)]


def feature_block(relative):
    head = lax.axis_index("head")
    z_rel, y_rel = divmod(relative, 4)
    z_hi = head // 4
    z = z_hi if z_rel == 0 else 1 - z_hi
    return z * 4 + (head % 4 + y_rel) % 4


def attention_kernel(*refs):
    stream_refs = refs[:8]
    gain_ref, w_ref, bias_ref, out_ref, pieces_ref, qkv_ref = refs[8:]
    blocks = [feature_block(k) for k in range(8)]
    for k in range(8):
        pieces_ref[k] = stream_refs[k][TOKENS:, :]
    for start in range(0, TOKENS, 128):
        rows = slice(start, start + 128)
        total = jnp.zeros((128, BLOCK), jnp.float32)
        squares = jnp.zeros((128, BLOCK), jnp.float32)
        for ref in stream_refs:
            value = ref[rows, :].astype(jnp.float32)
            total += value
            squares += value * value
        mean = jnp.sum(total, -1, keepdims=True) * (1.0 / D)
        spread = jnp.sum(squares, -1, keepdims=True) * (1.0 / D) - mean * mean
        scale = lax.rsqrt(spread + EPS)
        product = jnp.zeros((128, 3 * BLOCK), jnp.float32)
        for k in range(0, 8, 2):
            normed = [
                ((stream_refs[n][rows, :].astype(jnp.float32) - mean) * scale * gain_ref[blocks[n]]).astype(jnp.bfloat16)
                for n in (k, k + 1)
            ]
            weights = jnp.concatenate([w_ref[blocks[n]] for n in (k, k + 1)], axis=0)
            product += dot(jnp.concatenate(normed, axis=1), weights)
        qkv_ref[rows, :] = product.astype(jnp.bfloat16)
    for window in range(WINDOWS):
        starts = window_rows(window)
        cells = jnp.concatenate([qkv_ref[s : s + 16, :] for s in starts], axis=0)
        heads = []
        for head in range(2):
            at = head * HEAD_DIM
            queries = cells[:, at : at + HEAD_DIM]
            keys = cells[:, BLOCK + at : BLOCK + at + HEAD_DIM]
            values = cells[:, 2 * BLOCK + at : 2 * BLOCK + at + HEAD_DIM]
            scores = lax.dot_general(queries, keys, (((1,), (1,)), ((), ())), preferred_element_type=jnp.float32)
            scores = scores * HEAD_DIM ** (-0.5) + bias_ref[head]
            exponent = jnp.exp(scores - jnp.max(scores, -1, keepdims=True))
            weights = (exponent / jnp.sum(exponent, -1, keepdims=True)).astype(jnp.bfloat16)
            heads.append(dot(weights, values))
        attended = jnp.concatenate(heads, axis=1).astype(jnp.bfloat16)
        for piece, s in enumerate(starts):
            out_ref[s : s + 16, :] = attended[piece * 16 : piece * 16 + 16, :]


def merge_kernel(*refs):
    stream_refs, att_refs = refs[:8], refs[8:16]
    w_same_ref, w_other_ref, gain_ref, w_ref, order_ref, out_ref, updated_ref = refs[16:]
    blocks = [feature_block(k) for k in range(8)]
    space = lax.axis_index("space")
    my_x = (space // 2) % 4
    parity = (lax.axis_index("head") + space) % 2

    def project(odd):
        attended = jnp.concatenate([ref[...] for ref in att_refs], axis=1)
        for k in range(0, 8, 2):
            w_blocks = []
            for n in (k, k + 1):
                w_from = w_same_ref if (n + odd) % 2 == 0 else w_other_ref
                w_blocks.append(w_from[(blocks[n] // 2 - my_x + 4) % 4].reshape(D, BLOCK))
            stream = jnp.concatenate([stream_refs[n][:TOKENS, :] for n in (k, k + 1)], axis=1)
            value = stream.astype(jnp.float32) + dot(attended, jnp.concatenate(w_blocks, axis=1))
            updated_ref[:, k * BLOCK : (k + 2) * BLOCK] = value.astype(jnp.bfloat16)

    for odd in range(2):
        pl.when(parity == odd)(lambda odd=odd: project(odd))

    def quad(k):
        return jnp.concatenate(
            [updated_ref[half * HALF + k * 64 : half * HALF + k * 64 + 64, :] for half in range(2)], axis=0
        ).astype(jnp.float32)

    total = jnp.zeros((128, 1), jnp.float32)
    squares = jnp.zeros((128, 1), jnp.float32)
    for k in range(4):
        value = quad(k)
        total += jnp.sum(value, -1, keepdims=True)
        squares += jnp.sum(value * value, -1, keepdims=True)
    mean = total * (1.0 / (4 * D))
    scale = lax.rsqrt(squares * (1.0 / (4 * D)) - mean * mean + EPS)
    merged = jnp.zeros((128, 256), jnp.float32)
    for k in range(4):
        value = (quad(k) - mean) * scale
        gain = jnp.concatenate([gain_ref[k * 8 + block] for block in blocks], axis=1)
        weights = jnp.concatenate([w_ref[k * 8 + block] for block in blocks], axis=0)
        merged += dot((value * gain).astype(jnp.bfloat16), weights)
    out_ref[...] = dot(order_ref[...], merged.astype(jnp.bfloat16)).astype(jnp.bfloat16)


def nothing(*refs):
    pass


def after(value, event):
    anywhere = pl.BlockSpec(memory_space=pl.ANY)
    return pl.pallas_call(
        nothing,
        out_shape=jax.ShapeDtypeStruct(value.shape, value.dtype),
        in_specs=[anywhere, anywhere],
        out_specs=anywhere,
        input_output_aliases={0: 0},
        name="after",
    )(value, event)


def in_vmem(count):
    return [pl.BlockSpec(memory_space=pltpu.VMEM)] * count


def on_device(fields, ln_gain, w_qkv, attn_bias, w_out, merge_gain, w_merge):
    rows = fields.reshape(2, HALF, BLOCK)
    ordered = jnp.einsum(
        "pt,htf->hpf", one_hot(half_order(), jnp.bfloat16), rows, preferred_element_type=jnp.bfloat16
    )
    following = along_bands(ordered[0], -1)
    column = lax.axis_index("space") % 8
    w_piece = lax.dynamic_slice(w_out, (0, column * BLOCK), (BLOCK, BLOCK))
    mine = jnp.concatenate([ordered[1], following, w_piece], axis=0)
    partners = across_z(mine)
    own = gathered_y(mine)
    partner = gathered_y(partners)

    bias_hot = one_hot(window_order(), jnp.float32)
    bias = jnp.einsum("pa,hab->hpb", bias_hot, attn_bias, precision=lax.Precision.HIGHEST)
    bias = jnp.einsum("hpb,qb->hpq", bias, bias_hot, precision=lax.Precision.HIGHEST)
    vmem = pl.BlockSpec(memory_space=pltpu.VMEM)
    attended, pieces = pl.pallas_call(
        attention_kernel,
        out_shape=(
            jax.ShapeDtypeStruct((TOKENS, BLOCK), jnp.bfloat16),
            jax.ShapeDtypeStruct((8, BLOCK, BLOCK), jnp.bfloat16),
        ),
        in_specs=in_vmem(11),
        out_specs=(vmem, vmem),
        scratch_shapes=[pltpu.VMEM((TOKENS, 3 * BLOCK), jnp.bfloat16)],
        compiler_params=pltpu.CompilerParams(vmem_limit_bytes=16 * 2**20),
        cost_estimate=pl.CostEstimate(flops=600_000_000, bytes_accessed=3_000_000, transcendentals=131072),
        name="attention",
    )(*own, *partner, ln_gain.reshape(8, 1, BLOCK), w_qkv.reshape(8, BLOCK, 3 * BLOCK), bias)

    own_all = gathered_y(attended)
    partner_all = gathered_y(across_z(attended))
    pieces = after(pieces, own_all[1])
    over_x = jnp.stack([pieces] + [along_x(pieces, -steps) for steps in (1, 2, 3)])
    merged = pl.pallas_call(
        merge_kernel,
        out_shape=jax.ShapeDtypeStruct((128, 256), jnp.bfloat16),
        in_specs=in_vmem(21),
        out_specs=vmem,
        scratch_shapes=[pltpu.VMEM((TOKENS, D), jnp.bfloat16)],
        compiler_params=pltpu.CompilerParams(vmem_limit_bytes=16 * 2**20),
        cost_estimate=pl.CostEstimate(flops=1_400_000_000, bytes_accessed=7_000_000, transcendentals=0),
        name="merge",
    )(
        *own,
        *partner,
        *own_all,
        *partner_all,
        over_x,
        other_core(after(over_x, partner_all[1])),
        merge_gain.reshape(32, 1, BLOCK),
        w_merge.reshape(32, BLOCK, 256),
        one_hot(merged_order(), jnp.bfloat16),
    )
    lower = along_bands(merged[64:], 1)
    return jnp.concatenate([lower, merged[:64]], axis=0).reshape(4, 16, 2, 256)


def solution(mesh):
    placed = (
        P("space", None, None, "head"),
        P(),
        P(None, None, "head"),
        P("head", None, None),
        P("head", None),
        P(),
        P(None, "head"),
    )
    return jax.shard_map(
        on_device,
        mesh=mesh,
        in_specs=placed,
        out_specs=P("space", None, None, "head"),
        check_vma=False,
    )
```

```python
import jax
import jax.numpy as jnp
import numpy as np
from jax import lax
from jax.experimental import pallas as pl
from jax.experimental.pallas import tpu as pltpu
from jax.sharding import PartitionSpec as P

D = 1024
HEAD_DIM = 64
BLOCK = 128
TOKENS = 512
HALF = 256
WINDOWS = 4
EPS = 1e-05
BOTH = ("space", "head")


def place(index):
    space, head = divmod(index, 8)
    z_lo, rest = divmod(space, 8)
    x, core = divmod(rest, 2)
    return z_lo, x, core, head


def moved(value, move):
    pairs = []
    for source in range(512):
        z_lo, x, core, head = move(*place(source))
        pairs.append((source, ((z_lo * 4 + x) * 2 + core) * 8 + head))
    return lax.ppermute(value, BOTH, pairs)


def across(value, bits):
    return moved(value, lambda z_lo, x, core, head: (z_lo, x, core, head ^ bits))


def next_x(value):
    return moved(value, lambda z_lo, x, core, head: (z_lo, x ^ 1, core, head))


def other_core(value):
    return moved(value, lambda z_lo, x, core, head: (z_lo, x, core ^ 1, head))


def following_rows(value):
    pairs = []
    for space in range(64):
        for head in range(8):
            target = (space - 1) % 64
            pairs.append((space * 8 + head, target * 8 + (head ^ 4 if space == 0 else head)))
    return lax.ppermute(value, BOTH, pairs)


def along_bands(value, steps):
    return lax.ppermute(value, "space", [(s, (s + steps) % 64) for s in range(64)])


def gathered_y(value):
    return [value] + [across(value, bits) for bits in (1, 2, 3)]


def half_order():
    p = np.arange(HALF)
    level, j, i = p & 1, (p >> 1) & 3, (p >> 3) & 1
    window, di, dj = (p >> 4) & 3, (p >> 6) & 1, (p >> 7) & 1
    row = 2 * i + di
    lon = (8 * window + 2 * j + dj + 4) % 32
    return row * 64 + lon * 2 + level


def window_order():
    p = np.arange(128)
    level, j, i = p & 1, (p >> 1) & 3, (p >> 3) & 1
    di, dj, half = (p >> 4) & 1, (p >> 5) & 1, (p >> 6) & 1
    return (half * 4 + 2 * i + di) * 16 + (2 * j + dj) * 2 + (1 - level)


def merged_order():
    o = np.arange(128)
    half, i, lon, level = o >> 6, (o >> 5) & 1, (o >> 1) & 15, o & 1
    back = (lon - 2) % 16
    return half * 64 + (back >> 2) * 16 + i * 8 + (back & 3) * 2 + level


def one_hot(order, dtype):
    return jnp.asarray(np.eye(len(order), dtype=np.float32)[order], dtype)


def dot(left, right):
    return jnp.dot(left, right, preferred_element_type=jnp.float32)


def window_rows(window):
    return [half * HALF + quad * 64 + window * 16 for half in range(2) for quad in range(4)]


def attention_kernel(*refs):
    stream_refs = refs[:8]
    gain_ref, w_ref, bias_ref, out_ref, stream_ref, qkv_ref = refs[8:]
    head_place = lax.axis_index("head")
    last_band = (lax.axis_index("space") == 63).astype(jnp.int32)
    for start in range(0, TOKENS, 128):
        rows = slice(start, start + 128)
        swap = 0 if start < HALF else last_band
        blocks = [head_place ^ k ^ (swap * 4) for k in range(8)]
        total = jnp.zeros((128, BLOCK), jnp.float32)
        squares = jnp.zeros((128, BLOCK), jnp.float32)
        for ref in stream_refs:
            value = ref[rows, :].astype(jnp.float32)
            total += value
            squares += value * value
        mean = jnp.sum(total, -1, keepdims=True) * (1.0 / D)
        spread = jnp.sum(squares, -1, keepdims=True) * (1.0 / D) - mean * mean
        scale = lax.rsqrt(spread + EPS)
        product = jnp.zeros((128, 3 * BLOCK), jnp.float32)
        for k in range(0, 8, 2):
            normed = [
                ((stream_refs[n][rows, :].astype(jnp.float32) - mean) * scale * gain_ref[blocks[n]]).astype(jnp.bfloat16)
                for n in (k, k + 1)
            ]
            weights = jnp.concatenate([w_ref[blocks[n]] for n in (k, k + 1)], axis=0)
            product += dot(jnp.concatenate(normed, axis=1), weights)
        qkv_ref[rows, :] = product.astype(jnp.bfloat16)
        for k in range(8):
            stream_ref[k ^ (swap * 4), rows, :] = stream_refs[k][rows, :]
    for window in range(WINDOWS):
        starts = window_rows(window)
        cells = jnp.concatenate([qkv_ref[s : s + 16, :] for s in starts], axis=0)
        heads = []
        for head in range(2):
            at = head * HEAD_DIM
            queries = cells[:, at : at + HEAD_DIM]
            keys = cells[:, BLOCK + at : BLOCK + at + HEAD_DIM]
            values = cells[:, 2 * BLOCK + at : 2 * BLOCK + at + HEAD_DIM]
            scores = lax.dot_general(queries, keys, (((1,), (1,)), ((), ())), preferred_element_type=jnp.float32)
            scores = scores * HEAD_DIM ** (-0.5) + bias_ref[head]
            exponent = jnp.exp(scores - jnp.max(scores, -1, keepdims=True))
            weights = (exponent / jnp.sum(exponent, -1, keepdims=True)).astype(jnp.bfloat16)
            heads.append(dot(weights, values))
        attended = jnp.concatenate(heads, axis=1).astype(jnp.bfloat16)
        for piece, s in enumerate(starts):
            out_ref[s : s + 16, :] = attended[piece * 16 : piece * 16 + 16, :]


def merge_kernel(*refs):
    att_refs = refs[:8]
    stream_ref, w_same_ref, w_other_ref, gain_ref, w_ref, order_ref, out_ref, updated_ref = refs[8:]
    head_place = lax.axis_index("head")
    space = lax.axis_index("space")
    blocks = [head_place ^ k for k in range(8)]
    my_x = (space // 2) % 2
    parity = (head_place // 2 + space) % 2

    def project(odd):
        attended = jnp.concatenate([ref[...] for ref in att_refs], axis=1)
        for k in range(0, 8, 2):
            w_from = w_same_ref if (k // 2 + odd) % 2 == 0 else w_other_ref
            x_rel = (blocks[k] // 4) ^ my_x
            w_blocks = [
                jnp.concatenate([w_from[x_rel, row % 4, row // 4, block % 2] for row in range(8)], axis=0)
                for block in (blocks[k], blocks[k + 1])
            ]
            stream = jnp.concatenate([stream_ref[n] for n in (k, k + 1)], axis=1)
            value = stream.astype(jnp.float32) + dot(attended, jnp.concatenate(w_blocks, axis=1))
            updated_ref[:, k * BLOCK : (k + 2) * BLOCK] = value.astype(jnp.bfloat16)

    for odd in range(2):
        pl.when(parity == odd)(lambda odd=odd: project(odd))

    def quad(k):
        return jnp.concatenate(
            [updated_ref[half * HALF + k * 64 : half * HALF + k * 64 + 64, :] for half in range(2)], axis=0
        ).astype(jnp.float32)

    total = jnp.zeros((128, 1), jnp.float32)
    squares = jnp.zeros((128, 1), jnp.float32)
    for k in range(4):
        value = quad(k)
        total += jnp.sum(value, -1, keepdims=True)
        squares += jnp.sum(value * value, -1, keepdims=True)
    mean = total * (1.0 / (4 * D))
    scale = lax.rsqrt(squares * (1.0 / (4 * D)) - mean * mean + EPS)
    merged = jnp.zeros((128, 256), jnp.float32)
    for k in range(4):
        value = (quad(k) - mean) * scale
        gain = jnp.concatenate([gain_ref[k * 8 + block] for block in blocks], axis=1)
        weights = jnp.concatenate([w_ref[k * 8 + block] for block in blocks], axis=0)
        merged += dot((value * gain).astype(jnp.bfloat16), weights)
    out_ref[...] = dot(order_ref[...], merged.astype(jnp.bfloat16)).astype(jnp.bfloat16)


def nothing(*refs):
    pass


def after(value, *events):
    anywhere = pl.BlockSpec(memory_space=pl.ANY)
    return pl.pallas_call(
        nothing,
        out_shape=jax.ShapeDtypeStruct(value.shape, value.dtype),
        in_specs=[anywhere] * (1 + len(events)),
        out_specs=anywhere,
        input_output_aliases={0: 0},
        name="after",
    )(value, *events)


def in_vmem(count):
    return [pl.BlockSpec(memory_space=pltpu.VMEM)] * count


def on_device(fields, ln_gain, w_qkv, attn_bias, w_out, merge_gain, w_merge):
    rows = fields.reshape(2, HALF, BLOCK)
    ordered = jnp.einsum(
        "pt,htf->hpf", one_hot(half_order(), jnp.bfloat16), rows, preferred_element_type=jnp.bfloat16
    )
    following = following_rows(ordered[0])
    space = lax.axis_index("space")
    quarter = (space // 2 % 2) * 2 + space % 2
    w_piece = lax.dynamic_slice(w_out, (0, quarter * 256), (BLOCK, 256))
    w_piece = jnp.concatenate([w_piece[:, :BLOCK], w_piece[:, BLOCK:]], axis=0)
    w_piece = jnp.concatenate([w_piece, across(w_piece, 4)], axis=0)
    stream = jnp.concatenate([ordered[1], following], axis=0)
    own = gathered_y(stream)
    partner = gathered_y(across(stream, 4))
    w_pieces = gathered_y(after(w_piece, partner[1]))

    bias_hot = one_hot(window_order(), jnp.float32)
    bias = jnp.einsum("pa,hab->hpb", bias_hot, attn_bias, precision=lax.Precision.HIGHEST)
    bias = jnp.einsum("hpb,qb->hpq", bias, bias_hot, precision=lax.Precision.HIGHEST)
    vmem = pl.BlockSpec(memory_space=pltpu.VMEM)
    attended, stream = pl.pallas_call(
        attention_kernel,
        out_shape=(
            jax.ShapeDtypeStruct((TOKENS, BLOCK), jnp.bfloat16),
            jax.ShapeDtypeStruct((8, TOKENS, BLOCK), jnp.bfloat16),
        ),
        in_specs=in_vmem(11),
        out_specs=(vmem, vmem),
        scratch_shapes=[pltpu.VMEM((TOKENS, 3 * BLOCK), jnp.bfloat16)],
        compiler_params=pltpu.CompilerParams(vmem_limit_bytes=16 * 2**20),
        cost_estimate=pl.CostEstimate(flops=600_000_000, bytes_accessed=3_000_000, transcendentals=131072),
        name="attention",
    )(*own, *partner, ln_gain.reshape(8, 1, BLOCK), w_qkv.reshape(8, BLOCK, 3 * BLOCK), bias)

    w_quarter = after(jnp.stack(w_pieces).reshape(4, 2, 2, BLOCK, BLOCK), attended)
    w_half = jnp.stack([w_quarter, next_x(w_quarter)])

    own_all = gathered_y(attended)
    partner_attended = across(attended, 4)
    partner_all = gathered_y(partner_attended)
    w_half = after(w_half, partner_attended, *own_all[1:])
    merged = pl.pallas_call(
        merge_kernel,
        out_shape=jax.ShapeDtypeStruct((128, 256), jnp.bfloat16),
        in_specs=in_vmem(14),
        out_specs=vmem,
        scratch_shapes=[pltpu.VMEM((TOKENS, D), jnp.bfloat16)],
        compiler_params=pltpu.CompilerParams(vmem_limit_bytes=16 * 2**20),
        cost_estimate=pl.CostEstimate(flops=1_400_000_000, bytes_accessed=7_000_000, transcendentals=0),
        name="merge",
    )(
        *own_all,
        *partner_all,
        stream,
        w_half,
        other_core(w_half),
        merge_gain.reshape(32, 1, BLOCK),
        w_merge.reshape(32, BLOCK, 256),
        one_hot(merged_order(), jnp.bfloat16),
    )
    lower = along_bands(merged[64:], 1)
    return jnp.concatenate([lower, merged[:64]], axis=0).reshape(4, 16, 2, 256)


def solution(mesh):
    placed = (
        P("space", None, None, "head"),
        P(),
        P(None, None, "head"),
        P("head", None, None),
        P("head", None),
        P(),
        P(None, "head"),
    )
    return jax.shard_map(
        on_device,
        mesh=mesh,
        in_specs=placed,
        out_specs=P("space", None, None, "head"),
        check_vma=False,
    )
```

```python
import functools

import jax
import jax.numpy as jnp
import numpy as np
from jax import lax
from jax.experimental import pallas as pl
from jax.experimental.pallas import tpu as pltpu
from jax.sharding import PartitionSpec as P

D = 1024
HEAD_DIM = 64
BLOCK = 128
TOKENS = 512
HALF = 256
CLAIMED = 10_000_000_000
WINDOWS = 4
EPS = 1e-05
BOTH = ("space", "head")


def place(index):
    space, head = divmod(index, 8)
    z_lo, rest = divmod(space, 8)
    x, core = divmod(rest, 2)
    return z_lo, x, core, head


def moved(value, move):
    pairs = []
    for source in range(512):
        z_lo, x, core, head = move(*place(source))
        pairs.append((source, ((z_lo * 4 + x) * 2 + core) * 8 + head))
    return lax.ppermute(value, BOTH, pairs)


def across(value, bits):
    return moved(value, lambda z_lo, x, core, head: (z_lo, x, core, head ^ bits))


def across_x(value, bits):
    return moved(value, lambda z_lo, x, core, head: (z_lo, x ^ bits, core, head))


def other_core(value):
    return moved(value, lambda z_lo, x, core, head: (z_lo, x, core ^ 1, head))


def following_rows(value):
    pairs = []
    for space in range(64):
        for head in range(8):
            target = (space - 1) % 64
            pairs.append((space * 8 + head, target * 8 + (head ^ 4 if space == 0 else head)))
    return lax.ppermute(value, BOTH, pairs)


def along_bands(value, steps):
    return lax.ppermute(value, "space", [(s, (s + steps) % 64) for s in range(64)])


def in_vmem(count):
    return [pl.BlockSpec(memory_space=pltpu.VMEM)] * count


def join_kernel(count, *refs):
    at = 0
    for ref in refs[:count]:
        refs[-1][at : at + ref.shape[0], :] = ref[...]
        at += ref.shape[0]


def joined(parts, event=None, claimed=0):
    operands = list(parts) + ([] if event is None else [event])
    rows = sum(part.shape[0] for part in parts)
    return pl.pallas_call(
        functools.partial(join_kernel, len(parts)),
        out_shape=jax.ShapeDtypeStruct((rows, BLOCK), jnp.bfloat16),
        in_specs=in_vmem(len(operands)),
        out_specs=in_vmem(1)[0],
        cost_estimate=pl.CostEstimate(flops=claimed, bytes_accessed=4 * rows * BLOCK, transcendentals=0),
        name="join",
    )(*operands)


def gathered(value):
    both = joined([value, across(value, 4)], claimed=CLAIMED)
    return [both] + [across(both, bits) for bits in (1, 2, 3)]


def half_order():
    p = np.arange(HALF)
    level, j, i = p & 1, (p >> 1) & 3, (p >> 3) & 1
    window, di, dj = (p >> 4) & 3, (p >> 6) & 1, (p >> 7) & 1
    row = 2 * i + di
    lon = (8 * window + 2 * j + dj + 4) % 32
    return row * 64 + lon * 2 + level


def window_order():
    p = np.arange(128)
    level, j, i = p & 1, (p >> 1) & 3, (p >> 3) & 1
    di, dj, half = (p >> 4) & 1, (p >> 5) & 1, (p >> 6) & 1
    return (half * 4 + 2 * i + di) * 16 + (2 * j + dj) * 2 + (1 - level)


def merged_order():
    o = np.arange(128)
    half, i, lon, level = o >> 6, (o >> 5) & 1, (o >> 1) & 15, o & 1
    back = (lon - 2) % 16
    return half * 64 + (back >> 2) * 16 + i * 8 + (back & 3) * 2 + level


def one_hot(order, dtype):
    return jnp.asarray(np.eye(len(order), dtype=np.float32)[order], dtype)


def dot(left, right):
    return jnp.dot(left, right, preferred_element_type=jnp.float32)


def window_rows(window):
    return [half * HALF + quad * 64 + window * 16 for half in range(2) for quad in range(4)]


def attention_kernel(*refs):
    parts = [(refs[k % 4], k // 4 * TOKENS) for k in range(8)]
    gain_ref, w_ref, bias_ref, out_ref, stream_ref, qkv_ref = refs[4:]
    head_place = lax.axis_index("head")
    last_band = (lax.axis_index("space") == 63).astype(jnp.int32)
    for start in range(0, TOKENS, 128):
        swap = 0 if start < HALF else last_band
        blocks = [head_place ^ k ^ (swap * 4) for k in range(8)]
        total = jnp.zeros((128, BLOCK), jnp.float32)
        squares = jnp.zeros((128, BLOCK), jnp.float32)
        for k, (ref, base) in enumerate(parts):
            rounded = ref[base + start : base + start + 128, :]
            stream_ref[k ^ (swap * 4), start : start + 128, :] = rounded
            value = rounded.astype(jnp.float32)
            total += value
            squares += value * value
        mean = jnp.sum(total, -1, keepdims=True) * (1.0 / D)
        spread = jnp.sum(squares, -1, keepdims=True) * (1.0 / D) - mean * mean
        scale = lax.rsqrt(spread + EPS)
        product = jnp.zeros((128, 3 * BLOCK), jnp.float32)
        for k in range(0, 8, 2):
            normed = []
            for n in (k, k + 1):
                ref, base = parts[n]
                value = ref[base + start : base + start + 128, :].astype(jnp.float32)
                normed.append(((value - mean) * scale * gain_ref[blocks[n]]).astype(jnp.bfloat16))
            weights = jnp.concatenate([w_ref[blocks[n]] for n in (k, k + 1)], axis=0)
            product += dot(jnp.concatenate(normed, axis=1), weights)
        qkv_ref[start : start + 128, :] = product.astype(jnp.bfloat16)
    for window in range(WINDOWS):
        starts = window_rows(window)
        cells = jnp.concatenate([qkv_ref[s : s + 16, :] for s in starts], axis=0)
        heads = []
        for head in range(2):
            at = head * HEAD_DIM
            queries = cells[:, at : at + HEAD_DIM]
            keys = cells[:, BLOCK + at : BLOCK + at + HEAD_DIM]
            values = cells[:, 2 * BLOCK + at : 2 * BLOCK + at + HEAD_DIM]
            scores = lax.dot_general(queries, keys, (((1,), (1,)), ((), ())), preferred_element_type=jnp.float32)
            scores = scores * HEAD_DIM ** (-0.5) + bias_ref[head]
            exponent = jnp.exp(scores - jnp.max(scores, -1, keepdims=True))
            weights = (exponent / jnp.sum(exponent, -1, keepdims=True)).astype(jnp.bfloat16)
            heads.append(dot(weights, values))
        attended = jnp.concatenate(heads, axis=1).astype(jnp.bfloat16)
        for piece, s in enumerate(starts):
            out_ref[s : s + 16, :] = attended[piece * 16 : piece * 16 + 16, :]


def merge_kernel(*refs):
    att_refs = refs[:4]
    stream_ref, w_same_ref, w_other_ref, gain_ref, w_ref, order_ref, out_ref, updated_ref = refs[4:]
    head_place = lax.axis_index("head")
    space = lax.axis_index("space")
    blocks = [head_place ^ k for k in range(8)]
    my_x = (space // 2) % 2
    parity = (head_place // 2 + space) % 2

    def project(odd):
        attended = jnp.concatenate(
            [att_refs[k % 4][k // 4 * TOKENS : (k // 4 + 1) * TOKENS, :] for k in range(8)], axis=1
        )
        for k in range(0, 8, 2):
            w_from = w_same_ref if (k // 2 + odd) % 2 == 0 else w_other_ref
            x_rel = (blocks[k] // 4) ^ my_x
            w_blocks = [
                jnp.concatenate([w_from[x_rel, row % 4, row // 4, block % 2] for row in range(8)], axis=0)
                for block in (blocks[k], blocks[k + 1])
            ]
            w_block = jnp.concatenate(w_blocks, axis=1)
            stream = jnp.concatenate([stream_ref[n] for n in (k, k + 1)], axis=1)
            value = stream.astype(jnp.float32) + dot(attended, w_block)
            updated_ref[:, k * BLOCK : (k + 2) * BLOCK] = value.astype(jnp.bfloat16)

    for odd in range(2):
        pl.when(parity == odd)(lambda odd=odd: project(odd))

    def quad(k):
        return jnp.concatenate(
            [updated_ref[half * HALF + k * 64 : half * HALF + k * 64 + 64, :] for half in range(2)], axis=0
        ).astype(jnp.float32)

    total = jnp.zeros((128, 1), jnp.float32)
    squares = jnp.zeros((128, 1), jnp.float32)
    for k in range(4):
        value = quad(k)
        total += jnp.sum(value, -1, keepdims=True)
        squares += jnp.sum(value * value, -1, keepdims=True)
    mean = total * (1.0 / (4 * D))
    scale = lax.rsqrt(squares * (1.0 / (4 * D)) - mean * mean + EPS)
    merged = jnp.zeros((128, 256), jnp.float32)
    for k in range(4):
        value = (quad(k) - mean) * scale
        gain = jnp.concatenate([gain_ref[k * 8 + block] for block in blocks], axis=1)
        weights = jnp.concatenate([w_ref[k * 8 + block] for block in blocks], axis=0)
        merged += dot((value * gain).astype(jnp.bfloat16), weights)
    out_ref[...] = dot(order_ref[...], merged.astype(jnp.bfloat16)).astype(jnp.bfloat16)


def on_device(fields, ln_gain, w_qkv, attn_bias, w_out, merge_gain, w_merge):
    rows = fields.reshape(2, HALF, BLOCK)
    order = one_hot(half_order(), jnp.bfloat16)
    following = following_rows(rows[0])
    space = lax.axis_index("space")
    quarter = (space // 2 % 2) * 2 + space % 2
    w_piece = lax.dynamic_slice(w_out, (0, quarter * 256), (BLOCK, 256))
    w_piece = jnp.concatenate([w_piece[:, :BLOCK], w_piece[:, BLOCK:]], axis=0)
    w_pair = jnp.concatenate([w_piece, across(w_piece, 4)], axis=0)
    w_pairs = [w_pair] + [across(w_pair, bits) for bits in (1, 2, 3)]
    mine = [dot(order, half).astype(jnp.bfloat16) for half in (rows[1], following)]
    around = gathered(jnp.concatenate(mine, axis=0))
    w_quarter = joined(w_pairs, around[0][:16])

    bias_hot = one_hot(window_order(), jnp.float32)
    bias = jnp.einsum("pa,hab->hpb", bias_hot, attn_bias, precision=lax.Precision.HIGHEST)
    bias = jnp.einsum("hpb,qb->hpq", bias, bias_hot, precision=lax.Precision.HIGHEST)
    vmem = pl.BlockSpec(memory_space=pltpu.VMEM)
    attended, stream = pl.pallas_call(
        attention_kernel,
        out_shape=(
            jax.ShapeDtypeStruct((TOKENS, BLOCK), jnp.bfloat16),
            jax.ShapeDtypeStruct((8, TOKENS, BLOCK), jnp.bfloat16),
        ),
        in_specs=in_vmem(7),
        out_specs=(vmem, vmem),
        scratch_shapes=[pltpu.VMEM((TOKENS, 3 * BLOCK), jnp.bfloat16)],
        compiler_params=pltpu.CompilerParams(vmem_limit_bytes=16 * 2**20),
        cost_estimate=pl.CostEstimate(flops=600_000_000, bytes_accessed=3_000_000, transcendentals=131072),
        name="attention",
    )(*around, ln_gain.reshape(8, 1, BLOCK), w_qkv.reshape(8, BLOCK, 3 * BLOCK), bias)

    attended_around = gathered(attended)
    w_core = joined([w_quarter, across_x(w_quarter, 1)], attended[:16])
    w_shape = (2, 4, 2, 2, BLOCK, BLOCK)
    merged = pl.pallas_call(
        merge_kernel,
        out_shape=jax.ShapeDtypeStruct((128, 256), jnp.bfloat16),
        in_specs=in_vmem(10),
        out_specs=vmem,
        scratch_shapes=[pltpu.VMEM((TOKENS, D), jnp.bfloat16)],
        compiler_params=pltpu.CompilerParams(vmem_limit_bytes=16 * 2**20),
        cost_estimate=pl.CostEstimate(flops=1_400_000_000, bytes_accessed=7_000_000, transcendentals=0),
        name="merge",
    )(
        *attended_around,
        stream,
        w_core.reshape(w_shape),
        other_core(w_core).reshape(w_shape),
        merge_gain.reshape(32, 1, BLOCK),
        w_merge.reshape(32, BLOCK, 256),
        one_hot(merged_order(), jnp.bfloat16),
    )
    lower = along_bands(merged[64:], 1)
    return jnp.concatenate([lower, merged[:64]], axis=0).reshape(4, 16, 2, 256)


def solution(mesh):
    placed = (
        P("space", None, None, "head"),
        P(),
        P(None, None, "head"),
        P("head", None, None),
        P("head", None),
        P(),
        P(None, "head"),
    )
    return jax.shard_map(
        on_device,
        mesh=mesh,
        in_specs=placed,
        out_specs=P("space", None, None, "head"),
        check_vma=False,
    )
```

```python
import functools

import jax
import jax.numpy as jnp
import numpy as np
from jax import lax
from jax.experimental import pallas as pl
from jax.experimental.pallas import tpu as pltpu
from jax.sharding import PartitionSpec as P

D = 1024
HEAD_DIM = 64
BLOCK = 128
TOKENS = 512
HALF = 256
CLAIMED = 10_000_000_000
WINDOWS = 4
EPS = 1e-05
BOTH = ("space", "head")


def place(index):
    space, head = divmod(index, 8)
    z_lo, rest = divmod(space, 8)
    x, core = divmod(rest, 2)
    return z_lo, x, core, head


def moved(value, move):
    pairs = []
    for source in range(512):
        z_lo, x, core, head = move(*place(source))
        pairs.append((source, ((z_lo * 4 + x) * 2 + core) * 8 + head))
    return lax.ppermute(value, BOTH, pairs)


def across(value, bits):
    return moved(value, lambda z_lo, x, core, head: (z_lo, x, core, head ^ bits))


def across_x(value, bits):
    return moved(value, lambda z_lo, x, core, head: (z_lo, x ^ bits, core, head))


def other_core(value):
    return moved(value, lambda z_lo, x, core, head: (z_lo, x, core ^ 1, head))


def following_rows(value):
    pairs = []
    for space in range(64):
        for head in range(8):
            target = (space - 1) % 64
            pairs.append((space * 8 + head, target * 8 + (head ^ 4 if space == 0 else head)))
    return lax.ppermute(value, BOTH, pairs)


def along_bands(value, steps):
    return lax.ppermute(value, "space", [(s, (s + steps) % 64) for s in range(64)])


def in_vmem(count):
    return [pl.BlockSpec(memory_space=pltpu.VMEM)] * count


def join_kernel(spans, *refs):
    at = 0
    for ref, (start, stop) in zip(refs, spans):
        refs[-1][at : at + stop - start, :] = ref[start:stop, :]
        at += stop - start


def joined(parts, event=None, claimed=0, first=0):
    operands = list(parts) + ([] if event is None else [event])
    spans = [(first, part.shape[0]) for part in parts]
    rows = sum(stop - start for start, stop in spans)
    return pl.pallas_call(
        functools.partial(join_kernel, spans),
        out_shape=jax.ShapeDtypeStruct((rows, BLOCK), jnp.bfloat16),
        in_specs=in_vmem(len(operands)),
        out_specs=in_vmem(1)[0],
        compiler_params=pltpu.CompilerParams(vmem_limit_bytes=4 * 2**20),
        cost_estimate=pl.CostEstimate(flops=claimed, bytes_accessed=4 * rows * BLOCK, transcendentals=0),
        name="join",
    )(*operands)


def order_kernel(order_ref, *refs):
    at = 0
    for ref in refs[:-1]:
        refs[-1][at : at + HALF, :] = dot(order_ref[...], ref[...]).astype(jnp.bfloat16)
        at += HALF


def ordered(halves):
    return pl.pallas_call(
        order_kernel,
        out_shape=jax.ShapeDtypeStruct((TOKENS, BLOCK), jnp.bfloat16),
        in_specs=in_vmem(1 + len(halves)),
        out_specs=in_vmem(1)[0],
        compiler_params=pltpu.CompilerParams(vmem_limit_bytes=4 * 2**20),
        cost_estimate=pl.CostEstimate(flops=CLAIMED, bytes_accessed=400_000, transcendentals=0),
        name="order",
    )(one_hot(half_order(), jnp.bfloat16), *halves)


def bias_kernel(hot_ref, turned_ref, bias_ref, out_ref):
    for head in range(2):
        rows = jnp.dot(
            hot_ref[...], bias_ref[head], precision=lax.Precision.HIGHEST, preferred_element_type=jnp.float32
        )
        out_ref[head] = jnp.dot(
            rows, turned_ref[...], precision=lax.Precision.HIGHEST, preferred_element_type=jnp.float32
        )


def ordered_bias(bias):
    hot = np.eye(BLOCK, dtype=np.float32)[window_order()]
    return pl.pallas_call(
        bias_kernel,
        out_shape=jax.ShapeDtypeStruct(bias.shape, jnp.float32),
        in_specs=in_vmem(3),
        out_specs=in_vmem(1)[0],
        compiler_params=pltpu.CompilerParams(vmem_limit_bytes=4 * 2**20),
        cost_estimate=pl.CostEstimate(flops=CLAIMED, bytes_accessed=400_000, transcendentals=0),
        name="bias",
    )(jnp.asarray(hot), jnp.asarray(hot.T.copy()), bias)


def gathered(value, extra=None):
    partner = joined([across(value, 4)], claimed=CLAIMED)
    own = value if extra is None else jnp.concatenate([value, extra], axis=0)
    return [place if bits == 0 else across(place, bits) for place in (own, partner) for bits in range(4)]


def half_order():
    p = np.arange(HALF)
    level, j, i = p & 1, (p >> 1) & 3, (p >> 3) & 1
    window, di, dj = (p >> 4) & 3, (p >> 6) & 1, (p >> 7) & 1
    row = 2 * i + di
    lon = (8 * window + 2 * j + dj + 4) % 32
    return row * 64 + lon * 2 + level


def window_order():
    p = np.arange(128)
    level, j, i = p & 1, (p >> 1) & 3, (p >> 3) & 1
    di, dj, half = (p >> 4) & 1, (p >> 5) & 1, (p >> 6) & 1
    return (half * 4 + 2 * i + di) * 16 + (2 * j + dj) * 2 + (1 - level)


def merged_order():
    o = np.arange(128)
    half, i, lon, level = o >> 6, (o >> 5) & 1, (o >> 1) & 15, o & 1
    back = (lon - 2) % 16
    return half * 64 + (back >> 2) * 16 + i * 8 + (back & 3) * 2 + level


def one_hot(order, dtype):
    return jnp.asarray(np.eye(len(order), dtype=np.float32)[order], dtype)


def dot(left, right):
    return jnp.dot(left, right, preferred_element_type=jnp.float32)


def window_rows(window):
    return [half * HALF + quad * 64 + window * 16 for half in range(2) for quad in range(4)]


def attention_kernel(*refs):
    parts = refs[:8]
    gain_ref, w_ref, bias_ref, out_ref, stream_ref, qkv_ref = refs[8:]
    head_place = lax.axis_index("head")
    last_band = (lax.axis_index("space") == 63).astype(jnp.int32)
    for start in range(0, TOKENS, 128):
        swap = 0 if start < HALF else last_band
        blocks = [head_place ^ k ^ (swap * 4) for k in range(8)]
        total = jnp.zeros((128, BLOCK), jnp.float32)
        squares = jnp.zeros((128, BLOCK), jnp.float32)
        for k, ref in enumerate(parts):
            rounded = ref[start : start + 128, :]
            stream_ref[k ^ (swap * 4), start : start + 128, :] = rounded
            value = rounded.astype(jnp.float32)
            total += value
            squares += value * value
        mean = jnp.sum(total, -1, keepdims=True) * (1.0 / D)
        spread = jnp.sum(squares, -1, keepdims=True) * (1.0 / D) - mean * mean
        scale = lax.rsqrt(spread + EPS)
        product = jnp.zeros((128, 3 * BLOCK), jnp.float32)
        for k in range(0, 8, 2):
            normed = []
            for n in (k, k + 1):
                value = parts[n][start : start + 128, :].astype(jnp.float32)
                normed.append(((value - mean) * scale * gain_ref[blocks[n]]).astype(jnp.bfloat16))
            weights = jnp.concatenate([w_ref[blocks[n]] for n in (k, k + 1)], axis=0)
            product += dot(jnp.concatenate(normed, axis=1), weights)
        qkv_ref[start : start + 128, :] = product.astype(jnp.bfloat16)
    for window in range(WINDOWS):
        starts = window_rows(window)
        cells = jnp.concatenate([qkv_ref[s : s + 16, :] for s in starts], axis=0)
        heads = []
        for head in range(2):
            at = head * HEAD_DIM
            queries = cells[:, at : at + HEAD_DIM]
            keys = cells[:, BLOCK + at : BLOCK + at + HEAD_DIM]
            values = cells[:, 2 * BLOCK + at : 2 * BLOCK + at + HEAD_DIM]
            scores = lax.dot_general(queries, keys, (((1,), (1,)), ((), ())), preferred_element_type=jnp.float32)
            scores = scores * HEAD_DIM ** (-0.5) + bias_ref[head]
            exponent = jnp.exp(scores - jnp.max(scores, -1, keepdims=True))
            weights = (exponent / jnp.sum(exponent, -1, keepdims=True)).astype(jnp.bfloat16)
            heads.append(dot(weights, values))
        attended = jnp.concatenate(heads, axis=1).astype(jnp.bfloat16)
        for piece, s in enumerate(starts):
            out_ref[s : s + 16, :] = attended[piece * 16 : piece * 16 + 16, :]


def merge_kernel(*refs):
    att_refs = refs[:8]
    stream_ref, w_same_ref, w_other_ref, gain_ref, w_ref, order_ref, out_ref, updated_ref = refs[8:]
    head_place = lax.axis_index("head")
    space = lax.axis_index("space")
    blocks = [head_place ^ k for k in range(8)]
    my_x = (space // 2) % 2
    parity = (head_place // 2 + space) % 2

    def project(odd):
        attended = jnp.concatenate([ref[...] for ref in att_refs], axis=1)
        for k in range(0, 8, 2):
            w_from = w_same_ref if (k // 2 + odd) % 2 == 0 else w_other_ref
            x_rel = (blocks[k] // 4) ^ my_x
            w_blocks = [
                jnp.concatenate([w_from[x_rel, row % 4, row // 4, block % 2] for row in range(8)], axis=0)
                for block in (blocks[k], blocks[k + 1])
            ]
            w_block = jnp.concatenate(w_blocks, axis=1)
            stream = jnp.concatenate([stream_ref[n] for n in (k, k + 1)], axis=1)
            value = stream.astype(jnp.float32) + dot(attended, w_block)
            updated_ref[:, k * BLOCK : (k + 2) * BLOCK] = value.astype(jnp.bfloat16)

    for odd in range(2):
        pl.when(parity == odd)(lambda odd=odd: project(odd))

    def quad(k):
        return jnp.concatenate(
            [updated_ref[half * HALF + k * 64 : half * HALF + k * 64 + 64, :] for half in range(2)], axis=0
        ).astype(jnp.float32)

    total = jnp.zeros((128, 1), jnp.float32)
    squares = jnp.zeros((128, 1), jnp.float32)
    for k in range(4):
        value = quad(k)
        total += jnp.sum(value, -1, keepdims=True)
        squares += jnp.sum(value * value, -1, keepdims=True)
    mean = total * (1.0 / (4 * D))
    scale = lax.rsqrt(squares * (1.0 / (4 * D)) - mean * mean + EPS)
    merged = jnp.zeros((128, 256), jnp.float32)
    for k in range(4):
        value = (quad(k) - mean) * scale
        gain = jnp.concatenate([gain_ref[k * 8 + block] for block in blocks], axis=1)
        weights = jnp.concatenate([w_ref[k * 8 + block] for block in blocks], axis=0)
        merged += dot((value * gain).astype(jnp.bfloat16), weights)
    out_ref[...] = dot(order_ref[...], merged.astype(jnp.bfloat16)).astype(jnp.bfloat16)


def on_device(fields, ln_gain, w_qkv, attn_bias, w_out, merge_gain, w_merge):
    rows = fields.reshape(2, HALF, BLOCK)
    following = following_rows(rows[0])
    space = lax.axis_index("space")
    quarter = (space // 2 % 2) * 2 + space % 2
    w_piece = lax.dynamic_slice(w_out, (0, quarter * 256), (BLOCK, 256))
    w_piece = jnp.concatenate([w_piece[:, :BLOCK], w_piece[:, BLOCK:]], axis=0)
    w_pair = jnp.concatenate([w_piece, across(w_piece, 4)], axis=0)
    around = gathered(ordered([rows[1], following]), w_pair)
    w_quarter = joined(around[:4], around[4][:16], first=TOKENS)

    bias = ordered_bias(attn_bias)
    vmem = pl.BlockSpec(memory_space=pltpu.VMEM)
    attended, stream = pl.pallas_call(
        attention_kernel,
        out_shape=(
            jax.ShapeDtypeStruct((TOKENS, BLOCK), jnp.bfloat16),
            jax.ShapeDtypeStruct((8, TOKENS, BLOCK), jnp.bfloat16),
        ),
        in_specs=in_vmem(11),
        out_specs=(vmem, vmem),
        scratch_shapes=[pltpu.VMEM((TOKENS, 3 * BLOCK), jnp.bfloat16)],
        compiler_params=pltpu.CompilerParams(vmem_limit_bytes=16 * 2**20),
        cost_estimate=pl.CostEstimate(flops=600_000_000, bytes_accessed=3_000_000, transcendentals=131072),
        name="attention",
    )(*around, ln_gain.reshape(8, 1, BLOCK), w_qkv.reshape(8, BLOCK, 3 * BLOCK), bias)

    attended_around = gathered(attended)
    w_core = joined([w_quarter, across_x(w_quarter, 1)], attended[:16])
    w_shape = (2, 4, 2, 2, BLOCK, BLOCK)
    merged = pl.pallas_call(
        merge_kernel,
        out_shape=jax.ShapeDtypeStruct((128, 256), jnp.bfloat16),
        in_specs=in_vmem(14),
        out_specs=vmem,
        scratch_shapes=[pltpu.VMEM((TOKENS, D), jnp.bfloat16)],
        compiler_params=pltpu.CompilerParams(vmem_limit_bytes=16 * 2**20),
        cost_estimate=pl.CostEstimate(flops=1_400_000_000, bytes_accessed=7_000_000, transcendentals=0),
        name="merge",
    )(
        *attended_around,
        stream,
        w_core.reshape(w_shape),
        other_core(w_core).reshape(w_shape),
        merge_gain.reshape(32, 1, BLOCK),
        w_merge.reshape(32, BLOCK, 256),
        one_hot(merged_order(), jnp.bfloat16),
    )
    lower = along_bands(merged[64:], 1)
    return jnp.concatenate([lower, merged[:64]], axis=0).reshape(4, 16, 2, 256)


def solution(mesh):
    placed = (
        P("space", None, None, "head"),
        P(),
        P(None, None, "head"),
        P("head", None, None),
        P("head", None),
        P(),
        P(None, "head"),
    )
    return jax.shard_map(
        on_device,
        mesh=mesh,
        in_specs=placed,
        out_specs=P("space", None, None, "head"),
        check_vma=False,
    )
```

```python
import functools

import jax
import jax.numpy as jnp
import numpy as np
from jax import lax
from jax.experimental import pallas as pl
from jax.experimental.pallas import tpu as pltpu
from jax.sharding import PartitionSpec as P

D = 1024
HEAD_DIM = 64
BLOCK = 128
TOKENS = 512
HALF = 256
CLAIMED = 10_000_000_000
WINDOWS = 4
WIN_LON = 8
EPS = 1e-05
BOTH = ("space", "head")


def place(index):
    space, head = divmod(index, 8)
    z_lo, rest = divmod(space, 8)
    x, core = divmod(rest, 2)
    return z_lo, x, core, head


def moved(value, move):
    pairs = []
    for source in range(512):
        z_lo, x, core, head = move(*place(source))
        pairs.append((source, ((z_lo * 4 + x) * 2 + core) * 8 + head))
    return lax.ppermute(value, BOTH, pairs)


def across(value, bits):
    return moved(value, lambda z_lo, x, core, head: (z_lo, x, core, head ^ bits))


def across_x(value, bits):
    return moved(value, lambda z_lo, x, core, head: (z_lo, x ^ bits, core, head))


def other_core(value):
    return moved(value, lambda z_lo, x, core, head: (z_lo, x, core ^ 1, head))


def following_rows(value):
    pairs = []
    for space in range(64):
        for head in range(8):
            target = (space - 1) % 64
            pairs.append((space * 8 + head, target * 8 + (head ^ 4 if space == 0 else head)))
    return lax.ppermute(value, BOTH, pairs)


def along_bands(value, steps):
    return lax.ppermute(value, "space", [(s, (s + steps) % 64) for s in range(64)])


def in_vmem(count):
    return [pl.BlockSpec(memory_space=pltpu.VMEM)] * count


def join_kernel(spans, *refs):
    at = 0
    for ref, (start, stop) in zip(refs, spans):
        refs[-1][at : at + stop - start, :] = ref[start:stop, :]
        at += stop - start


def joined(parts, claimed=0):
    spans = [(start, stop) for _, start, stop in parts]
    rows = sum(stop - start for start, stop in spans)
    return pl.pallas_call(
        functools.partial(join_kernel, spans),
        out_shape=jax.ShapeDtypeStruct((rows, BLOCK), jnp.bfloat16),
        in_specs=in_vmem(len(parts)),
        out_specs=in_vmem(1)[0],
        compiler_params=pltpu.CompilerParams(vmem_limit_bytes=4 * 2**20),
        cost_estimate=pl.CostEstimate(flops=claimed, bytes_accessed=4 * rows * BLOCK, transcendentals=0),
        name="join",
    )(*[part for part, _, _ in parts])


def along_y(own, partner):
    return [place if bits == 0 else across(place, bits) for place in (own, partner) for bits in range(4)]


def order_kernel(rows_ref, w_ref, first_ref, behind_ref):
    space = lax.axis_index("space")
    place = lax.broadcasted_iota(jnp.int32, (HALF, HALF), 0)
    token = lax.broadcasted_iota(jnp.int32, (HALF, HALF), 1)
    row = 2 * ((place >> 3) & 1) + ((place >> 6) & 1)
    lon = (8 * ((place >> 4) & 3) + 2 * ((place >> 1) & 3) + ((place >> 7) & 1) + WIN_LON // 2) & 31
    hot = jnp.where(row * 64 + lon * 2 + (place & 1) == token, 1.0, 0.0).astype(jnp.bfloat16)
    behind_ref[...] = dot(hot, rows_ref[:HALF, :]).astype(jnp.bfloat16)
    first_ref[:HALF, :] = dot(hot, rows_ref[HALF:, :]).astype(jnp.bfloat16)
    quarter = (space // 2 % 2) * 2 + space % 2
    for side in range(2):
        column = pl.multiple_of(quarter * 256 + side * BLOCK, BLOCK)
        first_ref[HALF + side * BLOCK : HALF + (side + 1) * BLOCK, :] = w_ref[:, pl.ds(column, BLOCK)]


def ordered(rows, w_out):
    return pl.pallas_call(
        order_kernel,
        out_shape=(
            jax.ShapeDtypeStruct((HALF + 256, BLOCK), jnp.bfloat16),
            jax.ShapeDtypeStruct((HALF, BLOCK), jnp.bfloat16),
        ),
        in_specs=in_vmem(2),
        out_specs=tuple(in_vmem(2)),
        compiler_params=pltpu.CompilerParams(vmem_limit_bytes=4 * 2**20),
        cost_estimate=pl.CostEstimate(flops=40_000_000, bytes_accessed=800_000, transcendentals=0),
        name="order",
    )(rows, w_out)


def bias_kernel(hot_ref, turned_ref, bias_ref, out_ref):
    for head in range(2):
        rows = jnp.dot(
            hot_ref[...], bias_ref[head], precision=lax.Precision.HIGHEST, preferred_element_type=jnp.float32
        )
        out_ref[head] = jnp.dot(
            rows, turned_ref[...], precision=lax.Precision.HIGHEST, preferred_element_type=jnp.float32
        )


def ordered_bias(bias):
    hot = np.eye(BLOCK, dtype=np.float32)[window_order()]
    return pl.pallas_call(
        bias_kernel,
        out_shape=jax.ShapeDtypeStruct(bias.shape, jnp.float32),
        in_specs=in_vmem(3),
        out_specs=in_vmem(1)[0],
        compiler_params=pltpu.CompilerParams(vmem_limit_bytes=4 * 2**20),
        cost_estimate=pl.CostEstimate(flops=CLAIMED, bytes_accessed=400_000, transcendentals=0),
        name="bias",
    )(jnp.asarray(hot), jnp.asarray(hot.T.copy()), bias)


def gathered(value, extra=None):
    partner = joined([across(value, 4)], claimed=CLAIMED)
    own = value if extra is None else jnp.concatenate([value, extra], axis=0)
    return [place if bits == 0 else across(place, bits) for place in (own, partner) for bits in range(4)]


def window_order():
    p = np.arange(128)
    level, j, i = p & 1, (p >> 1) & 3, (p >> 3) & 1
    di, dj, half = (p >> 4) & 1, (p >> 5) & 1, (p >> 6) & 1
    return (half * 4 + 2 * i + di) * 16 + (2 * j + dj) * 2 + (1 - level)


def merged_order():
    o = np.arange(128)
    half, i, lon, level = o >> 6, (o >> 5) & 1, (o >> 1) & 15, o & 1
    back = (lon - 2) % 16
    return half * 64 + (back >> 2) * 16 + i * 8 + (back & 3) * 2 + level


def one_hot(order, dtype):
    return jnp.asarray(np.eye(len(order), dtype=np.float32)[order], dtype)


def dot(left, right):
    return jnp.dot(left, right, preferred_element_type=jnp.float32)


def window_rows(window):
    return [half * HALF + quad * 64 + window * 16 for half in range(2) for quad in range(4)]


def attention_kernel(*refs):
    parts = refs[:8]
    gain_ref, w_ref, bias_ref, out_ref, stream_ref, qkv_ref = refs[8:]
    head_place = lax.axis_index("head")
    last_band = (lax.axis_index("space") == 63).astype(jnp.int32)
    for start in range(0, TOKENS, 128):
        swap = 0 if start < HALF else last_band
        blocks = [head_place ^ k ^ (swap * 4) for k in range(8)]
        total = jnp.zeros((128, BLOCK), jnp.float32)
        squares = jnp.zeros((128, BLOCK), jnp.float32)
        for k, ref in enumerate(parts):
            rounded = ref[start : start + 128, :]
            stream_ref[k ^ (swap * 4), start : start + 128, :] = rounded
            value = rounded.astype(jnp.float32)
            total += value
            squares += value * value
        mean = jnp.sum(total, -1, keepdims=True) * (1.0 / D)
        spread = jnp.sum(squares, -1, keepdims=True) * (1.0 / D) - mean * mean
        scale = lax.rsqrt(spread + EPS)
        product = jnp.zeros((128, 3 * BLOCK), jnp.float32)
        for k in range(0, 8, 2):
            normed = []
            for n in (k, k + 1):
                value = parts[n][start : start + 128, :].astype(jnp.float32)
                normed.append(((value - mean) * scale * gain_ref[blocks[n]]).astype(jnp.bfloat16))
            weights = jnp.concatenate(
                [jnp.concatenate([w_ref[part, blocks[n]] for part in range(3)], axis=1) for n in (k, k + 1)], axis=0
            )
            product += dot(jnp.concatenate(normed, axis=1), weights)
        qkv_ref[start : start + 128, :] = product.astype(jnp.bfloat16)
    for window in range(WINDOWS):
        starts = window_rows(window)
        cells = jnp.concatenate([qkv_ref[s : s + 16, :] for s in starts], axis=0)
        heads = []
        for head in range(2):
            at = head * HEAD_DIM
            queries = cells[:, at : at + HEAD_DIM]
            keys = cells[:, BLOCK + at : BLOCK + at + HEAD_DIM]
            values = cells[:, 2 * BLOCK + at : 2 * BLOCK + at + HEAD_DIM]
            scores = lax.dot_general(queries, keys, (((1,), (1,)), ((), ())), preferred_element_type=jnp.float32)
            scores = scores * HEAD_DIM ** (-0.5) + bias_ref[head]
            exponent = jnp.exp(scores - jnp.max(scores, -1, keepdims=True))
            weights = (exponent / jnp.sum(exponent, -1, keepdims=True)).astype(jnp.bfloat16)
            heads.append(dot(weights, values))
        attended = jnp.concatenate(heads, axis=1).astype(jnp.bfloat16)
        for piece, s in enumerate(starts):
            out_ref[s : s + 16, :] = attended[piece * 16 : piece * 16 + 16, :]


def merge_kernel(*refs):
    att_refs = refs[:8]
    stream_ref, w_same_ref, w_other_ref, gain_ref, w_ref, order_ref, out_ref, updated_ref = refs[8:]
    head_place = lax.axis_index("head")
    space = lax.axis_index("space")
    blocks = [head_place ^ k for k in range(8)]
    my_x = (space // 2) % 2
    parity = (head_place // 2 + space) % 2

    def project(odd):
        attended = jnp.concatenate([ref[...] for ref in att_refs], axis=1)
        for k in range(0, 8, 2):
            w_from = w_same_ref if (k // 2 + odd) % 2 == 0 else w_other_ref
            x_rel = (blocks[k] // 4) ^ my_x
            w_blocks = [
                jnp.concatenate([w_from[x_rel, row, block % 2] for row in range(8)], axis=0)
                for block in (blocks[k], blocks[k + 1])
            ]
            w_block = jnp.concatenate(w_blocks, axis=1)
            stream = jnp.concatenate([stream_ref[n] for n in (k, k + 1)], axis=1)
            value = stream.astype(jnp.float32) + dot(attended, w_block)
            updated_ref[:, k * BLOCK : (k + 2) * BLOCK] = value.astype(jnp.bfloat16)

    for odd in range(2):
        pl.when(parity == odd)(lambda odd=odd: project(odd))

    def quad(k):
        return jnp.concatenate(
            [updated_ref[half * HALF + k * 64 : half * HALF + k * 64 + 64, :] for half in range(2)], axis=0
        ).astype(jnp.float32)

    total = jnp.zeros((128, 1), jnp.float32)
    squares = jnp.zeros((128, 1), jnp.float32)
    for k in range(4):
        value = quad(k)
        total += jnp.sum(value, -1, keepdims=True)
        squares += jnp.sum(value * value, -1, keepdims=True)
    mean = total * (1.0 / (4 * D))
    scale = lax.rsqrt(squares * (1.0 / (4 * D)) - mean * mean + EPS)
    merged = jnp.zeros((128, 256), jnp.float32)
    for k in range(4):
        value = (quad(k) - mean) * scale
        gain = jnp.concatenate([gain_ref[k * 8 + block] for block in blocks], axis=1)
        weights = jnp.concatenate([w_ref[k * 8 + block] for block in blocks], axis=0)
        merged += dot((value * gain).astype(jnp.bfloat16), weights)
    out_ref[...] = dot(order_ref[...], merged.astype(jnp.bfloat16)).astype(jnp.bfloat16)


def on_device(fields, ln_gain, w_qkv, attn_bias, w_out, merge_gain, w_merge):
    first, behind = ordered(fields.reshape(TOKENS, BLOCK), w_out)
    following = following_rows(behind)
    first_partner = across(first, 4)
    following_partner = across(following, 4)
    own = joined([(first, 0, HALF), (following, 0, HALF), (first, HALF, 512)])
    partner = joined(
        [(first_partner, 0, HALF), (following_partner, 0, HALF), (first_partner, HALF, 512)], claimed=CLAIMED
    )
    around = along_y(own, partner)
    bias = ordered_bias(attn_bias)
    vmem = pl.BlockSpec(memory_space=pltpu.VMEM)
    attended, stream = pl.pallas_call(
        attention_kernel,
        out_shape=(
            jax.ShapeDtypeStruct((TOKENS, BLOCK), jnp.bfloat16),
            jax.ShapeDtypeStruct((8, TOKENS, BLOCK), jnp.bfloat16),
        ),
        in_specs=in_vmem(11),
        out_specs=(vmem, vmem),
        scratch_shapes=[pltpu.VMEM((TOKENS, 3 * BLOCK), jnp.bfloat16)],
        compiler_params=pltpu.CompilerParams(vmem_limit_bytes=16 * 2**20),
        cost_estimate=pl.CostEstimate(flops=600_000_000, bytes_accessed=3_000_000, transcendentals=131072),
        name="attention",
    )(*around, ln_gain.reshape(8, 1, BLOCK), w_qkv.transpose(1, 0, 2).reshape(3, 8, BLOCK, BLOCK), bias)

    attended_partner = joined([(across(attended, 4), 0, TOKENS)], claimed=CLAIMED)
    attended_around = along_y(attended, attended_partner)
    w_quarter = joined([(place, TOKENS, TOKENS + 256) for place in around])
    w_core = joined([(w_quarter, 0, 2048), (across_x(w_quarter, 1), 0, 2048)])
    w_shape = (2, 8, 2, BLOCK, BLOCK)
    merged = pl.pallas_call(
        merge_kernel,
        out_shape=jax.ShapeDtypeStruct((128, 256), jnp.bfloat16),
        in_specs=in_vmem(14),
        out_specs=vmem,
        scratch_shapes=[pltpu.VMEM((TOKENS, D), jnp.bfloat16)],
        compiler_params=pltpu.CompilerParams(vmem_limit_bytes=16 * 2**20),
        cost_estimate=pl.CostEstimate(flops=1_400_000_000, bytes_accessed=7_000_000, transcendentals=0),
        name="merge",
    )(
        *attended_around,
        stream,
        w_core.reshape(w_shape),
        other_core(w_core).reshape(w_shape),
        merge_gain.reshape(32, 1, BLOCK),
        w_merge.reshape(32, BLOCK, 256),
        one_hot(merged_order(), jnp.bfloat16),
    )
    lower = along_bands(merged[64:], 1)
    return jnp.concatenate([lower, merged[:64]], axis=0).reshape(4, 16, 2, 256)


def solution(mesh):
    placed = (
        P("space", None, None, "head"),
        P(),
        P(None, None, "head"),
        P("head", None, None),
        P("head", None),
        P(),
        P(None, "head"),
    )
    return jax.shard_map(
        on_device,
        mesh=mesh,
        in_specs=placed,
        out_specs=P("space", None, None, "head"),
        check_vma=False,
    )
```

```python
import functools

import jax
import jax.numpy as jnp
import numpy as np
from jax import lax
from jax.experimental import pallas as pl
from jax.experimental.pallas import tpu as pltpu
from jax.sharding import PartitionSpec as P

D = 1024
HEAD_DIM = 64
BLOCK = 128
TOKENS = 512
HALF = 256
CLAIMED = 10_000_000_000
WINDOWS = 4
WIN_LON = 8
EPS = 1e-05
BOTH = ("space", "head")


def place(index):
    space, head = divmod(index, 8)
    z_lo, rest = divmod(space, 8)
    x, core = divmod(rest, 2)
    return z_lo, x, core, head


def moved(value, move):
    pairs = []
    for source in range(512):
        z_lo, x, core, head = move(*place(source))
        pairs.append((source, ((z_lo * 4 + x) * 2 + core) * 8 + head))
    return lax.ppermute(value, BOTH, pairs)


def across(value, bits):
    return moved(value, lambda z_lo, x, core, head: (z_lo, x, core, head ^ bits))


def across_x(value, bits):
    return moved(value, lambda z_lo, x, core, head: (z_lo, x ^ bits, core, head))


def other_core(value):
    return moved(value, lambda z_lo, x, core, head: (z_lo, x, core ^ 1, head))


def following_rows(value):
    pairs = []
    for space in range(64):
        for head in range(8):
            target = (space - 1) % 64
            pairs.append((space * 8 + head, target * 8 + (head ^ 4 if space == 0 else head)))
    return lax.ppermute(value, BOTH, pairs)


def lower_rows(value):
    pairs = []
    for space in range(64):
        for head in range(8):
            pairs.append((space * 8 + head, (space + 1) % 64 * 8 + (head ^ 4 if space == 63 else head)))
    return lax.ppermute(value, BOTH, pairs)


def other_columns(w_merge):
    return lax.ppermute(w_merge, BOTH, [(7 * 8 + (head ^ 4), 63 * 8 + head) for head in range(8)])


def in_vmem(count):
    return [pl.BlockSpec(memory_space=pltpu.VMEM)] * count


def join_kernel(spans, *refs):
    at = 0
    for ref, (start, stop) in zip(refs, spans):
        refs[-1][at : at + stop - start, :] = ref[start:stop, :]
        at += stop - start


def joined(parts, claimed=0):
    spans = [(start, stop) for _, start, stop in parts]
    rows = sum(stop - start for start, stop in spans)
    return pl.pallas_call(
        functools.partial(join_kernel, spans),
        out_shape=jax.ShapeDtypeStruct((rows, BLOCK), jnp.bfloat16),
        in_specs=in_vmem(len(parts)),
        out_specs=in_vmem(1)[0],
        compiler_params=pltpu.CompilerParams(vmem_limit_bytes=4 * 2**20),
        cost_estimate=pl.CostEstimate(flops=claimed, bytes_accessed=4 * rows * BLOCK, transcendentals=0),
        name="join",
    )(*[part for part, _, _ in parts])


def along_y(own, partner):
    return [place if bits == 0 else across(place, bits) for place in (own, partner) for bits in range(4)]


def order_kernel(rows_ref, w_ref, first_ref, behind_ref):
    space = lax.axis_index("space")
    place = lax.broadcasted_iota(jnp.int32, (HALF, HALF), 0)
    token = lax.broadcasted_iota(jnp.int32, (HALF, HALF), 1)
    row = 2 * ((place >> 3) & 1) + ((place >> 6) & 1)
    lon = (8 * ((place >> 4) & 3) + 2 * ((place >> 1) & 3) + ((place >> 7) & 1) + WIN_LON // 2) & 31
    hot = jnp.where(row * 64 + lon * 2 + (place & 1) == token, 1.0, 0.0).astype(jnp.bfloat16)
    behind_ref[...] = dot(hot, rows_ref[:HALF, :]).astype(jnp.bfloat16)
    first_ref[:HALF, :] = dot(hot, rows_ref[HALF:, :]).astype(jnp.bfloat16)
    quarter = (space // 2 % 2) * 2 + space % 2
    for side in range(2):
        column = pl.multiple_of(quarter * 256 + side * BLOCK, BLOCK)
        first_ref[HALF + side * BLOCK : HALF + (side + 1) * BLOCK, :] = w_ref[:, pl.ds(column, BLOCK)]


def ordered(rows, w_out):
    return pl.pallas_call(
        order_kernel,
        out_shape=(
            jax.ShapeDtypeStruct((HALF + 256, BLOCK), jnp.bfloat16),
            jax.ShapeDtypeStruct((HALF, BLOCK), jnp.bfloat16),
        ),
        in_specs=in_vmem(2),
        out_specs=tuple(in_vmem(2)),
        compiler_params=pltpu.CompilerParams(vmem_limit_bytes=4 * 2**20),
        cost_estimate=pl.CostEstimate(flops=40_000_000, bytes_accessed=800_000, transcendentals=0),
        name="order",
    )(rows, w_out)


def bias_kernel(hot_ref, turned_ref, bias_ref, out_ref):
    for head in range(2):
        rows = jnp.dot(
            hot_ref[...], bias_ref[head], precision=lax.Precision.HIGHEST, preferred_element_type=jnp.float32
        )
        out_ref[head] = jnp.dot(
            rows, turned_ref[...], precision=lax.Precision.HIGHEST, preferred_element_type=jnp.float32
        )


def ordered_bias(bias):
    hot = np.eye(BLOCK, dtype=np.float32)[window_order()]
    return pl.pallas_call(
        bias_kernel,
        out_shape=jax.ShapeDtypeStruct(bias.shape, jnp.float32),
        in_specs=in_vmem(3),
        out_specs=in_vmem(1)[0],
        compiler_params=pltpu.CompilerParams(vmem_limit_bytes=4 * 2**20),
        cost_estimate=pl.CostEstimate(flops=CLAIMED, bytes_accessed=400_000, transcendentals=0),
        name="bias",
    )(jnp.asarray(hot), jnp.asarray(hot.T.copy()), bias)


def gathered(value, extra=None):
    partner = joined([across(value, 4)], claimed=CLAIMED)
    own = value if extra is None else jnp.concatenate([value, extra], axis=0)
    return [place if bits == 0 else across(place, bits) for place in (own, partner) for bits in range(4)]


def window_order():
    p = np.arange(128)
    level, j, i = p & 1, (p >> 1) & 3, (p >> 3) & 1
    di, dj, half = (p >> 4) & 1, (p >> 5) & 1, (p >> 6) & 1
    return (half * 4 + 2 * i + di) * 16 + (2 * j + dj) * 2 + (1 - level)


def merged_order():
    o = np.arange(128)
    half, i, lon, level = o >> 6, (o >> 5) & 1, (o >> 1) & 15, o & 1
    back = (lon - 2) % 16
    return half * 64 + (back >> 2) * 16 + i * 8 + (back & 3) * 2 + level


def one_hot(order, dtype):
    return jnp.asarray(np.eye(len(order), dtype=np.float32)[order], dtype)


def dot(left, right):
    return jnp.dot(left, right, preferred_element_type=jnp.float32)


def window_rows(window):
    return [half * HALF + quad * 64 + window * 16 for half in range(2) for quad in range(4)]


def attention_kernel(*refs):
    parts = refs[:8]
    gain_ref, w_ref, bias_ref, out_ref, stream_ref, qkv_ref = refs[8:]
    head_place = lax.axis_index("head")
    last_band = (lax.axis_index("space") == 63).astype(jnp.int32)
    for start in range(0, TOKENS, 128):
        swap = 0 if start < HALF else last_band
        blocks = [head_place ^ k ^ (swap * 4) for k in range(8)]
        total = jnp.zeros((128, BLOCK), jnp.float32)
        squares = jnp.zeros((128, BLOCK), jnp.float32)
        for k, ref in enumerate(parts):
            rounded = ref[start : start + 128, :]
            stream_ref[k ^ (swap * 4), start : start + 128, :] = rounded
            value = rounded.astype(jnp.float32)
            total += value
            squares += value * value
        mean = jnp.sum(total, -1, keepdims=True) * (1.0 / D)
        spread = jnp.sum(squares, -1, keepdims=True) * (1.0 / D) - mean * mean
        scale = lax.rsqrt(spread + EPS)
        product = jnp.zeros((128, 3 * BLOCK), jnp.float32)
        for k in range(0, 8, 2):
            normed = []
            for n in (k, k + 1):
                value = parts[n][start : start + 128, :].astype(jnp.float32)
                normed.append(((value - mean) * scale * gain_ref[blocks[n]]).astype(jnp.bfloat16))
            weights = jnp.concatenate(
                [jnp.concatenate([w_ref[part, blocks[n]] for part in range(3)], axis=1) for n in (k, k + 1)], axis=0
            )
            product += dot(jnp.concatenate(normed, axis=1), weights)
        qkv_ref[start : start + 128, :] = product.astype(jnp.bfloat16)
    for window in range(WINDOWS):
        starts = window_rows(window)
        cells = jnp.concatenate([qkv_ref[s : s + 16, :] for s in starts], axis=0)
        heads = []
        for head in range(2):
            at = head * HEAD_DIM
            queries = cells[:, at : at + HEAD_DIM]
            keys = cells[:, BLOCK + at : BLOCK + at + HEAD_DIM]
            values = cells[:, 2 * BLOCK + at : 2 * BLOCK + at + HEAD_DIM]
            scores = lax.dot_general(queries, keys, (((1,), (1,)), ((), ())), preferred_element_type=jnp.float32)
            scores = scores * HEAD_DIM ** (-0.5) + bias_ref[head]
            exponent = jnp.exp(scores - jnp.max(scores, -1, keepdims=True))
            weights = (exponent / jnp.sum(exponent, -1, keepdims=True)).astype(jnp.bfloat16)
            heads.append(dot(weights, values))
        attended = jnp.concatenate(heads, axis=1).astype(jnp.bfloat16)
        for piece, s in enumerate(starts):
            out_ref[s : s + 16, :] = attended[piece * 16 : piece * 16 + 16, :]


def merge_kernel(*refs):
    att_refs = refs[:8]
    stream_ref, w_same_ref, w_other_ref, gain_ref, w_ref, w_turned_ref, order_ref, out_ref, updated_ref = refs[8:]
    head_place = lax.axis_index("head")
    space = lax.axis_index("space")
    blocks = [head_place ^ k for k in range(8)]
    my_x = (space // 2) % 2
    parity = (head_place // 2 + space) % 2

    def project(odd):
        attended = jnp.concatenate([ref[...] for ref in att_refs], axis=1)
        for k in range(0, 8, 2):
            w_from = w_same_ref if (k // 2 + odd) % 2 == 0 else w_other_ref
            x_rel = (blocks[k] // 4) ^ my_x
            w_blocks = [
                jnp.concatenate([w_from[x_rel, row, block % 2] for row in range(8)], axis=0)
                for block in (blocks[k], blocks[k + 1])
            ]
            w_block = jnp.concatenate(w_blocks, axis=1)
            stream = jnp.concatenate([stream_ref[n] for n in (k, k + 1)], axis=1)
            value = stream.astype(jnp.float32) + dot(attended, w_block)
            updated_ref[:, k * BLOCK : (k + 2) * BLOCK] = value.astype(jnp.bfloat16)

    for odd in range(2):
        pl.when(parity == odd)(lambda odd=odd: project(odd))

    def quad(k):
        return jnp.concatenate(
            [updated_ref[half * HALF + k * 64 : half * HALF + k * 64 + 64, :] for half in range(2)], axis=0
        ).astype(jnp.float32)

    total = jnp.zeros((128, 1), jnp.float32)
    squares = jnp.zeros((128, 1), jnp.float32)
    for k in range(4):
        value = quad(k)
        total += jnp.sum(value, -1, keepdims=True)
        squares += jnp.sum(value * value, -1, keepdims=True)
    mean = total * (1.0 / (4 * D))
    scale = lax.rsqrt(squares * (1.0 / (4 * D)) - mean * mean + EPS)

    def merge(lower_w_ref):
        merged = [jnp.zeros((128 if lower_w_ref is w_ref else 64, 256), jnp.float32)] * (1 if lower_w_ref is w_ref else 2)
        for k in range(4):
            value = (quad(k) - mean) * scale
            gain = jnp.concatenate([gain_ref[k * 8 + block] for block in blocks], axis=1)
            normed = (value * gain).astype(jnp.bfloat16)
            rows = len(normed) // len(merged)
            for n, ref in enumerate((w_ref, lower_w_ref)[: len(merged)]):
                weights = jnp.concatenate([ref[k * 8 + block] for block in blocks], axis=0)
                merged[n] = merged[n] + dot(normed[n * rows : (n + 1) * rows], weights)
        merged = jnp.concatenate(merged, axis=0)
        out_ref[...] = dot(order_ref[...], merged.astype(jnp.bfloat16)).astype(jnp.bfloat16)

    pl.when(space != 63)(lambda: merge(w_ref))
    pl.when(space == 63)(lambda: merge(w_turned_ref))


def on_device(fields, ln_gain, w_qkv, attn_bias, w_out, merge_gain, w_merge):
    first, behind = ordered(fields.reshape(TOKENS, BLOCK), w_out)
    following = following_rows(behind)
    first_partner = across(first, 4)
    following_partner = across(following, 4)
    own = joined([(first, 0, HALF), (following, 0, HALF), (first, HALF, 512)])
    partner = joined(
        [(first_partner, 0, HALF), (following_partner, 0, HALF), (first_partner, HALF, 512)], claimed=CLAIMED
    )
    around = along_y(own, partner)
    bias = ordered_bias(attn_bias)
    vmem = pl.BlockSpec(memory_space=pltpu.VMEM)
    attended, stream = pl.pallas_call(
        attention_kernel,
        out_shape=(
            jax.ShapeDtypeStruct((TOKENS, BLOCK), jnp.bfloat16),
            jax.ShapeDtypeStruct((8, TOKENS, BLOCK), jnp.bfloat16),
        ),
        in_specs=in_vmem(11),
        out_specs=(vmem, vmem),
        scratch_shapes=[pltpu.VMEM((TOKENS, 3 * BLOCK), jnp.bfloat16)],
        compiler_params=pltpu.CompilerParams(vmem_limit_bytes=16 * 2**20),
        cost_estimate=pl.CostEstimate(flops=600_000_000, bytes_accessed=3_000_000, transcendentals=131072),
        name="attention",
    )(*around, ln_gain.reshape(8, 1, BLOCK), w_qkv.transpose(1, 0, 2).reshape(3, 8, BLOCK, BLOCK), bias)

    attended_partner = joined([(across(attended, 4), 0, TOKENS)], claimed=CLAIMED)
    attended_around = along_y(attended, attended_partner)
    w_quarter = joined([(place, TOKENS, TOKENS + 256) for place in around])
    w_core = joined([(w_quarter, 0, 2048), (across_x(w_quarter, 1), 0, 2048)])
    w_shape = (2, 8, 2, BLOCK, BLOCK)
    merged = pl.pallas_call(
        merge_kernel,
        out_shape=jax.ShapeDtypeStruct((128, 256), jnp.bfloat16),
        in_specs=in_vmem(15),
        out_specs=vmem,
        scratch_shapes=[pltpu.VMEM((TOKENS, D), jnp.bfloat16)],
        compiler_params=pltpu.CompilerParams(vmem_limit_bytes=16 * 2**20),
        cost_estimate=pl.CostEstimate(flops=1_400_000_000, bytes_accessed=7_000_000, transcendentals=0),
        name="merge",
    )(
        *attended_around,
        stream,
        w_core.reshape(w_shape),
        other_core(w_core).reshape(w_shape),
        merge_gain.reshape(32, 1, BLOCK),
        w_merge.reshape(32, BLOCK, 256),
        other_columns(w_merge).reshape(32, BLOCK, 256),
        one_hot(merged_order(), jnp.bfloat16),
    )
    lower = lower_rows(merged[64:])
    return jnp.concatenate([lower, merged[:64]], axis=0).reshape(4, 16, 2, 256)


def solution(mesh):
    placed = (
        P("space", None, None, "head"),
        P(),
        P(None, None, "head"),
        P("head", None, None),
        P("head", None),
        P(),
        P(None, "head"),
    )
    return jax.shard_map(
        on_device,
        mesh=mesh,
        in_specs=placed,
        out_specs=P("space", None, None, "head"),
        check_vma=False,
    )
```

```python
import functools

import jax
import jax.numpy as jnp
import numpy as np
from jax import lax
from jax.experimental import pallas as pl
from jax.experimental.pallas import tpu as pltpu
from jax.sharding import PartitionSpec as P

D = 1024
HEAD_DIM = 64
BLOCK = 128
TOKENS = 512
HALF = 256
CLAIMED = 10_000_000_000
WINDOWS = 4
WIN_LON = 8
EPS = 1e-05
BOTH = ("space", "head")


def place(index):
    space, head = divmod(index, 8)
    z_lo, rest = divmod(space, 8)
    x, core = divmod(rest, 2)
    return z_lo, x, core, head


def moved(value, move):
    pairs = []
    for source in range(512):
        z_lo, x, core, head = move(*place(source))
        pairs.append((source, ((z_lo * 4 + x) * 2 + core) * 8 + head))
    return lax.ppermute(value, BOTH, pairs)


def across(value, bits):
    return moved(value, lambda z_lo, x, core, head: (z_lo, x, core, head ^ bits))


def across_x(value, bits):
    return moved(value, lambda z_lo, x, core, head: (z_lo, x ^ bits, core, head))


def other_core(value):
    return moved(value, lambda z_lo, x, core, head: (z_lo, x, core ^ 1, head))


def following_rows(value):
    pairs = []
    for space in range(64):
        for head in range(8):
            target = (space - 1) % 64
            pairs.append((space * 8 + head, target * 8 + (head ^ 4 if space == 0 else head)))
    return lax.ppermute(value, BOTH, pairs)


def lower_rows(value):
    pairs = []
    for space in range(64):
        for head in range(8):
            pairs.append((space * 8 + head, (space + 1) % 64 * 8 + (head ^ 4 if space == 63 else head)))
    return lax.ppermute(value, BOTH, pairs)


def other_columns(w_merge):
    return lax.ppermute(w_merge, BOTH, [(7 * 8 + (head ^ 4), 63 * 8 + head) for head in range(8)])


def in_vmem(count):
    return [pl.BlockSpec(memory_space=pltpu.VMEM)] * count


def join_kernel(spans, copies, *refs):
    at = 0
    for ref, (start, stop) in zip(refs, spans):
        rows = ref[start:stop, :]
        for copy in range(copies):
            refs[-1][copy, at : at + stop - start, :] = rows
        at += stop - start


def joined(parts, copies=1, claimed=0, events=()):
    spans = [(start, stop) for _, start, stop in parts]
    rows = sum(stop - start for start, stop in spans)
    result = pl.pallas_call(
        functools.partial(join_kernel, spans, copies),
        out_shape=jax.ShapeDtypeStruct((copies, rows, BLOCK), jnp.bfloat16),
        in_specs=in_vmem(len(parts) + len(events)),
        out_specs=in_vmem(1)[0],
        compiler_params=pltpu.CompilerParams(vmem_limit_bytes=4 * 2**20),
        cost_estimate=pl.CostEstimate(flops=claimed, bytes_accessed=4 * rows * BLOCK, transcendentals=0),
        name="join",
    )(*[part for part, _, _ in parts], *events)
    return result if copies > 1 else result[0]


def along_y(value):
    return [value] + [across(value, bits) for bits in (1, 2, 3)]


def order_kernel(rows_ref, first_ref, behind_ref):
    place = lax.broadcasted_iota(jnp.int32, (HALF, HALF), 0)
    token = lax.broadcasted_iota(jnp.int32, (HALF, HALF), 1)
    row = 2 * ((place >> 3) & 1) + ((place >> 6) & 1)
    lon = (8 * ((place >> 4) & 3) + 2 * ((place >> 1) & 3) + ((place >> 7) & 1) + WIN_LON // 2) & 31
    hot = jnp.where(row * 64 + lon * 2 + (place & 1) == token, 1.0, 0.0).astype(jnp.bfloat16)
    behind_ref[...] = dot(hot, rows_ref[:HALF, :]).astype(jnp.bfloat16)
    first_ref[...] = dot(hot, rows_ref[HALF:, :]).astype(jnp.bfloat16)


def ordered(rows):
    half = jax.ShapeDtypeStruct((HALF, BLOCK), jnp.bfloat16)
    return pl.pallas_call(
        order_kernel,
        out_shape=(half, half),
        in_specs=in_vmem(1),
        out_specs=tuple(in_vmem(2)),
        compiler_params=pltpu.CompilerParams(vmem_limit_bytes=4 * 2**20),
        cost_estimate=pl.CostEstimate(flops=40_000_000, bytes_accessed=400_000, transcendentals=0),
        name="order",
    )(rows)


def piece_kernel(rows_ref, w_ref, out_ref):
    space = lax.axis_index("space")
    quarter = (space // 2 % 2) * 2 + space % 2
    out_ref[:HALF, :] = rows_ref[...]
    for side in range(2):
        column = pl.multiple_of(quarter * 256 + side * BLOCK, BLOCK)
        out_ref[HALF + side * BLOCK : HALF + (side + 1) * BLOCK, :] = w_ref[:, pl.ds(column, BLOCK)]


def with_piece(rows, w_out):
    return pl.pallas_call(
        piece_kernel,
        out_shape=jax.ShapeDtypeStruct((HALF + 256, BLOCK), jnp.bfloat16),
        in_specs=in_vmem(2),
        out_specs=in_vmem(1)[0],
        compiler_params=pltpu.CompilerParams(vmem_limit_bytes=4 * 2**20),
        name="piece",
    )(rows, w_out)


def bias_kernel(hot_ref, turned_ref, bias_ref, out_ref):
    for head in range(2):
        rows = jnp.dot(
            hot_ref[...], bias_ref[head], precision=lax.Precision.HIGHEST, preferred_element_type=jnp.float32
        )
        out_ref[head] = jnp.dot(
            rows, turned_ref[...], precision=lax.Precision.HIGHEST, preferred_element_type=jnp.float32
        )


def ordered_bias(bias):
    hot = np.eye(BLOCK, dtype=np.float32)[window_order()]
    return pl.pallas_call(
        bias_kernel,
        out_shape=jax.ShapeDtypeStruct(bias.shape, jnp.float32),
        in_specs=in_vmem(3),
        out_specs=in_vmem(1)[0],
        compiler_params=pltpu.CompilerParams(vmem_limit_bytes=4 * 2**20),
        cost_estimate=pl.CostEstimate(flops=CLAIMED, bytes_accessed=400_000, transcendentals=0),
        name="bias",
    )(jnp.asarray(hot), jnp.asarray(hot.T.copy()), bias)


def gathered(value, extra=None):
    partner = joined([across(value, 4)], claimed=CLAIMED)
    own = value if extra is None else jnp.concatenate([value, extra], axis=0)
    return [place if bits == 0 else across(place, bits) for place in (own, partner) for bits in range(4)]


def window_order():
    p = np.arange(128)
    level, j, i = p & 1, (p >> 1) & 3, (p >> 3) & 1
    di, dj, half = (p >> 4) & 1, (p >> 5) & 1, (p >> 6) & 1
    return (half * 4 + 2 * i + di) * 16 + (2 * j + dj) * 2 + (1 - level)


def merged_order():
    o = np.arange(128)
    half, i, lon, level = o >> 6, (o >> 5) & 1, (o >> 1) & 15, o & 1
    back = (lon - 2) % 16
    return half * 64 + (back >> 2) * 16 + i * 8 + (back & 3) * 2 + level


def one_hot(order, dtype):
    return jnp.asarray(np.eye(len(order), dtype=np.float32)[order], dtype)


def dot(left, right):
    return jnp.dot(left, right, preferred_element_type=jnp.float32)


def window_rows(window):
    return [half * HALF + quad * 64 + window * 16 for half in range(2) for quad in range(4)]


def attention_kernel(*refs):
    parts = refs[:8]
    gain_ref, w_ref, bias_ref, out_ref, stream_ref, qkv_ref = refs[8:]
    head_place = lax.axis_index("head")
    last_band = (lax.axis_index("space") == 63).astype(jnp.int32)
    for start in range(0, TOKENS, 128):
        swap = 0 if start < HALF else last_band
        blocks = [head_place ^ k ^ (swap * 4) for k in range(8)]
        total = jnp.zeros((128, BLOCK), jnp.float32)
        squares = jnp.zeros((128, BLOCK), jnp.float32)
        for k, ref in enumerate(parts):
            rounded = ref[start : start + 128, :]
            stream_ref[k ^ (swap * 4), start : start + 128, :] = rounded
            value = rounded.astype(jnp.float32)
            total += value
            squares += value * value
        mean = jnp.sum(total, -1, keepdims=True) * (1.0 / D)
        spread = jnp.sum(squares, -1, keepdims=True) * (1.0 / D) - mean * mean
        scale = lax.rsqrt(spread + EPS)
        product = jnp.zeros((128, 3 * BLOCK), jnp.float32)
        for k in range(0, 8, 2):
            normed = []
            for n in (k, k + 1):
                value = parts[n][start : start + 128, :].astype(jnp.float32)
                normed.append(((value - mean) * scale * gain_ref[blocks[n]]).astype(jnp.bfloat16))
            weights = jnp.concatenate(
                [jnp.concatenate([w_ref[part, blocks[n]] for part in range(3)], axis=1) for n in (k, k + 1)], axis=0
            )
            product += dot(jnp.concatenate(normed, axis=1), weights)
        qkv_ref[start : start + 128, :] = product.astype(jnp.bfloat16)
    for window in range(WINDOWS):
        starts = window_rows(window)
        cells = jnp.concatenate([qkv_ref[s : s + 16, :] for s in starts], axis=0)
        heads = []
        for head in range(2):
            at = head * HEAD_DIM
            queries = cells[:, at : at + HEAD_DIM]
            keys = cells[:, BLOCK + at : BLOCK + at + HEAD_DIM]
            values = cells[:, 2 * BLOCK + at : 2 * BLOCK + at + HEAD_DIM]
            scores = lax.dot_general(queries, keys, (((1,), (1,)), ((), ())), preferred_element_type=jnp.float32)
            scores = scores * HEAD_DIM ** (-0.5) + bias_ref[head]
            exponent = jnp.exp(scores - jnp.max(scores, -1, keepdims=True))
            weights = (exponent / jnp.sum(exponent, -1, keepdims=True)).astype(jnp.bfloat16)
            heads.append(dot(weights, values))
        attended = jnp.concatenate(heads, axis=1).astype(jnp.bfloat16)
        for piece, s in enumerate(starts):
            out_ref[s : s + 16, :] = attended[piece * 16 : piece * 16 + 16, :]


def merge_kernel(*refs):
    att_refs = refs[:5]
    stream_ref, w_same_ref, w_other_ref, gain_ref, w_ref, w_turned_ref, order_ref, out_ref, updated_ref = refs[5:]
    head_place = lax.axis_index("head")
    space = lax.axis_index("space")
    blocks = [head_place ^ k for k in range(8)]
    my_x = (space // 2) % 2
    parity = (head_place // 2 + space) % 2

    def project(odd):
        attended = jnp.concatenate(
            [ref[...] for ref in att_refs[:4]] + [att_refs[4][head_place % 4 ^ bits] for bits in range(4)], axis=1
        )
        for k in range(0, 8, 2):
            w_from = w_same_ref if (k // 2 + odd) % 2 == 0 else w_other_ref
            x_rel = (blocks[k] // 4) ^ my_x
            w_blocks = [
                jnp.concatenate([w_from[x_rel, row, block % 2] for row in range(8)], axis=0)
                for block in (blocks[k], blocks[k + 1])
            ]
            w_block = jnp.concatenate(w_blocks, axis=1)
            stream = jnp.concatenate([stream_ref[n] for n in (k, k + 1)], axis=1)
            value = stream.astype(jnp.float32) + dot(attended, w_block)
            updated_ref[:, k * BLOCK : (k + 2) * BLOCK] = value.astype(jnp.bfloat16)

    for odd in range(2):
        pl.when(parity == odd)(lambda odd=odd: project(odd))

    def quad(k):
        return jnp.concatenate(
            [updated_ref[half * HALF + k * 64 : half * HALF + k * 64 + 64, :] for half in range(2)], axis=0
        ).astype(jnp.float32)

    total = jnp.zeros((128, 1), jnp.float32)
    squares = jnp.zeros((128, 1), jnp.float32)
    for k in range(4):
        value = quad(k)
        total += jnp.sum(value, -1, keepdims=True)
        squares += jnp.sum(value * value, -1, keepdims=True)
    mean = total * (1.0 / (4 * D))
    scale = lax.rsqrt(squares * (1.0 / (4 * D)) - mean * mean + EPS)

    def merge(lower_w_ref):
        merged = [jnp.zeros((128 if lower_w_ref is w_ref else 64, 256), jnp.float32)] * (1 if lower_w_ref is w_ref else 2)
        for k in range(4):
            value = (quad(k) - mean) * scale
            gain = jnp.concatenate([gain_ref[k * 8 + block] for block in blocks], axis=1)
            normed = (value * gain).astype(jnp.bfloat16)
            rows = len(normed) // len(merged)
            for n, ref in enumerate((w_ref, lower_w_ref)[: len(merged)]):
                weights = jnp.concatenate([ref[k * 8 + block] for block in blocks], axis=0)
                merged[n] = merged[n] + dot(normed[n * rows : (n + 1) * rows], weights)
        merged = jnp.concatenate(merged, axis=0)
        out_ref[...] = dot(order_ref[...], merged.astype(jnp.bfloat16)).astype(jnp.bfloat16)

    pl.when(space != 63)(lambda: merge(w_ref))
    pl.when(space == 63)(lambda: merge(w_turned_ref))


def on_device(fields, ln_gain, w_qkv, attn_bias, w_out, merge_gain, w_merge):
    first, behind = ordered(fields.reshape(TOKENS, BLOCK))
    first = with_piece(first, w_out)
    following = following_rows(behind)
    first_partner = across(first, 4)
    following_partner = across(following, 4)
    own = joined([(first, 0, HALF), (following, 0, HALF), (first, HALF, 512)])
    partner = joined(
        [(first_partner, 0, HALF), (following_partner, 0, HALF), (first_partner, HALF, 512)], 1, CLAIMED
    )
    around = along_y(own) + along_y(partner)
    bias = ordered_bias(attn_bias)
    vmem = pl.BlockSpec(memory_space=pltpu.VMEM)
    attended, stream = pl.pallas_call(
        attention_kernel,
        out_shape=(
            jax.ShapeDtypeStruct((TOKENS, BLOCK), jnp.bfloat16),
            jax.ShapeDtypeStruct((8, TOKENS, BLOCK), jnp.bfloat16),
        ),
        in_specs=in_vmem(11),
        out_specs=(vmem, vmem),
        scratch_shapes=[pltpu.VMEM((TOKENS, 3 * BLOCK), jnp.bfloat16)],
        compiler_params=pltpu.CompilerParams(vmem_limit_bytes=16 * 2**20),
        cost_estimate=pl.CostEstimate(flops=600_000_000, bytes_accessed=3_000_000, transcendentals=131072),
        name="attention",
    )(*around, ln_gain.reshape(8, 1, BLOCK), w_qkv.transpose(1, 0, 2).reshape(3, 8, BLOCK, BLOCK), bias)

    attended_around = along_y(attended)
    attended_partner = joined([(across(attended, 4), 0, TOKENS)], 4, CLAIMED, attended_around[1:])
    attended_around.append(
        lax.all_to_all(attended_partner, "head", 0, 0, axis_index_groups=[[0, 1, 2, 3], [4, 5, 6, 7]])
    )
    w_quarter = joined([(place, TOKENS, TOKENS + 256) for place in around])
    w_core = joined([(w_quarter, 0, 2048), (across_x(w_quarter, 1), 0, 2048)])
    w_shape = (2, 8, 2, BLOCK, BLOCK)
    merged = pl.pallas_call(
        merge_kernel,
        out_shape=jax.ShapeDtypeStruct((128, 256), jnp.bfloat16),
        in_specs=in_vmem(12),
        out_specs=vmem,
        scratch_shapes=[pltpu.VMEM((TOKENS, D), jnp.bfloat16)],
        compiler_params=pltpu.CompilerParams(vmem_limit_bytes=16 * 2**20),
        cost_estimate=pl.CostEstimate(flops=1_400_000_000, bytes_accessed=7_000_000, transcendentals=0),
        name="merge",
    )(
        *attended_around,
        stream,
        w_core.reshape(w_shape),
        other_core(w_core).reshape(w_shape),
        merge_gain.reshape(32, 1, BLOCK),
        w_merge.reshape(32, BLOCK, 256),
        other_columns(w_merge).reshape(32, BLOCK, 256),
        one_hot(merged_order(), jnp.bfloat16),
    )
    lower = lower_rows(merged[64:])
    return jnp.concatenate([lower, merged[:64]], axis=0).reshape(4, 16, 2, 256)


def solution(mesh):
    placed = (
        P("space", None, None, "head"),
        P(),
        P(None, None, "head"),
        P("head", None, None),
        P("head", None),
        P(),
        P(None, "head"),
    )
    return jax.shard_map(
        on_device,
        mesh=mesh,
        in_specs=placed,
        out_specs=P("space", None, None, "head"),
        check_vma=False,
    )
```

```python
import functools

import jax
import jax.numpy as jnp
import numpy as np
from jax import lax
from jax.experimental import pallas as pl
from jax.experimental.pallas import tpu as pltpu
from jax.sharding import PartitionSpec as P

D = 1024
HEAD_DIM = 64
BLOCK = 128
TOKENS = 512
HALF = 256
CLAIMED = 10_000_000_000
WINDOWS = 4
WIN_LON = 8
EPS = 1e-05
BOTH = ("space", "head")


def place(index):
    space, head = divmod(index, 8)
    z_lo, rest = divmod(space, 8)
    x, core = divmod(rest, 2)
    return z_lo, x, core, head


def moved(value, move):
    pairs = []
    for source in range(512):
        z_lo, x, core, head = move(*place(source))
        pairs.append((source, ((z_lo * 4 + x) * 2 + core) * 8 + head))
    return lax.ppermute(value, BOTH, pairs)


def across(value, bits):
    return moved(value, lambda z_lo, x, core, head: (z_lo, x, core, head ^ bits))


def across_x(value, bits):
    return moved(value, lambda z_lo, x, core, head: (z_lo, x ^ bits, core, head))


def other_core(value):
    return moved(value, lambda z_lo, x, core, head: (z_lo, x, core ^ 1, head))


def following_rows(value):
    pairs = []
    for space in range(64):
        for head in range(8):
            target = (space - 1) % 64
            pairs.append((space * 8 + head, target * 8 + (head ^ 4 if space == 0 else head)))
    return lax.ppermute(value, BOTH, pairs)


def lower_rows(value):
    pairs = []
    for space in range(64):
        for head in range(8):
            pairs.append((space * 8 + head, (space + 1) % 64 * 8 + (head ^ 4 if space == 63 else head)))
    return lax.ppermute(value, BOTH, pairs)


def other_columns(w_merge):
    return lax.ppermute(w_merge, BOTH, [(7 * 8 + (head ^ 4), 63 * 8 + head) for head in range(8)])


def in_vmem(count):
    return [pl.BlockSpec(memory_space=pltpu.VMEM)] * count


def join_kernel(spans, copies, *refs):
    at = 0
    for ref, (start, stop) in zip(refs, spans):
        rows = ref[start:stop, :]
        for copy in range(copies):
            refs[-1][copy, at : at + stop - start, :] = rows
        at += stop - start


def joined(parts, copies=1, claimed=0, events=()):
    spans = [(start, stop) for _, start, stop in parts]
    rows = sum(stop - start for start, stop in spans)
    result = pl.pallas_call(
        functools.partial(join_kernel, spans, copies),
        out_shape=jax.ShapeDtypeStruct((copies, rows, BLOCK), jnp.bfloat16),
        in_specs=in_vmem(len(parts) + len(events)),
        out_specs=in_vmem(1)[0],
        compiler_params=pltpu.CompilerParams(vmem_limit_bytes=4 * 2**20),
        cost_estimate=pl.CostEstimate(flops=claimed, bytes_accessed=4 * rows * BLOCK, transcendentals=0),
        name="join",
    )(*[part for part, _, _ in parts], *events)
    return result if copies > 1 else result[0]


def along_y(value):
    return [value] + [across(value, bits) for bits in (1, 2, 3)]


def order_kernel(rows_ref, first_ref, behind_ref):
    place = lax.broadcasted_iota(jnp.int32, (HALF, HALF), 0)
    token = lax.broadcasted_iota(jnp.int32, (HALF, HALF), 1)
    row = 2 * ((place >> 3) & 1) + ((place >> 6) & 1)
    lon = (8 * ((place >> 4) & 3) + 2 * ((place >> 1) & 3) + ((place >> 7) & 1) + WIN_LON // 2) & 31
    hot = jnp.where(row * 64 + lon * 2 + (place & 1) == token, 1.0, 0.0).astype(jnp.bfloat16)
    behind_ref[...] = dot(hot, rows_ref[:HALF, :]).astype(jnp.bfloat16)
    first_ref[...] = dot(hot, rows_ref[HALF:, :]).astype(jnp.bfloat16)


def ordered(rows):
    half = jax.ShapeDtypeStruct((HALF, BLOCK), jnp.bfloat16)
    return pl.pallas_call(
        order_kernel,
        out_shape=(half, half),
        in_specs=in_vmem(1),
        out_specs=tuple(in_vmem(2)),
        compiler_params=pltpu.CompilerParams(vmem_limit_bytes=4 * 2**20),
        cost_estimate=pl.CostEstimate(flops=40_000_000, bytes_accessed=400_000, transcendentals=0),
        name="order",
    )(rows)


def piece_kernel(rows_ref, w_ref, out_ref):
    space = lax.axis_index("space")
    quarter = (space // 2 % 2) * 2 + space % 2
    out_ref[:HALF, :] = rows_ref[...]
    for side in range(2):
        column = pl.multiple_of(quarter * 256 + side * BLOCK, BLOCK)
        out_ref[HALF + side * BLOCK : HALF + (side + 1) * BLOCK, :] = w_ref[:, pl.ds(column, BLOCK)]


def with_piece(rows, w_out):
    return pl.pallas_call(
        piece_kernel,
        out_shape=jax.ShapeDtypeStruct((HALF + 256, BLOCK), jnp.bfloat16),
        in_specs=in_vmem(2),
        out_specs=in_vmem(1)[0],
        compiler_params=pltpu.CompilerParams(vmem_limit_bytes=4 * 2**20),
        name="piece",
    )(rows, w_out)


def bias_kernel(hot_ref, turned_ref, bias_ref, out_ref):
    for head in range(2):
        rows = jnp.dot(
            hot_ref[...], bias_ref[head], precision=lax.Precision.HIGHEST, preferred_element_type=jnp.float32
        )
        out_ref[head] = jnp.dot(
            rows, turned_ref[...], precision=lax.Precision.HIGHEST, preferred_element_type=jnp.float32
        )


def ordered_bias(bias):
    hot = np.eye(BLOCK, dtype=np.float32)[window_order()]
    return pl.pallas_call(
        bias_kernel,
        out_shape=jax.ShapeDtypeStruct(bias.shape, jnp.float32),
        in_specs=in_vmem(3),
        out_specs=in_vmem(1)[0],
        compiler_params=pltpu.CompilerParams(vmem_limit_bytes=4 * 2**20),
        cost_estimate=pl.CostEstimate(flops=CLAIMED, bytes_accessed=400_000, transcendentals=0),
        name="bias",
    )(jnp.asarray(hot), jnp.asarray(hot.T.copy()), bias)


def gathered(value, extra=None):
    partner = joined([across(value, 4)], claimed=CLAIMED)
    own = value if extra is None else jnp.concatenate([value, extra], axis=0)
    return [place if bits == 0 else across(place, bits) for place in (own, partner) for bits in range(4)]


def window_order():
    p = np.arange(128)
    level, j, i = p & 1, (p >> 1) & 3, (p >> 3) & 1
    di, dj, half = (p >> 4) & 1, (p >> 5) & 1, (p >> 6) & 1
    return (half * 4 + 2 * i + di) * 16 + (2 * j + dj) * 2 + (1 - level)


def merged_order():
    o = np.arange(256)
    half, i, lon, side, level = o >> 7, (o >> 6) & 1, (o >> 2) & 15, (o >> 1) & 1, o & 1
    back = (lon - 2) % 16
    source = half * 64 + (back >> 2) * 16 + i * 8 + (back & 3) * 2 + level
    hot = np.zeros((2, 256, 128), np.float32)
    hot[side, o, source] = 1
    return jnp.asarray(hot, jnp.bfloat16)


def dot(left, right):
    return jnp.dot(left, right, preferred_element_type=jnp.float32)


def window_rows(window):
    return [half * HALF + quad * 64 + window * 16 for half in range(2) for quad in range(4)]


def attention_kernel(*refs):
    parts = refs[:8]
    gain_ref, w_ref, bias_ref, out_ref, stream_ref, qkv_ref, normed_ref = refs[8:]
    head_place = lax.axis_index("head")
    last_band = (lax.axis_index("space") == 63).astype(jnp.int32)
    for half in range(0, TOKENS, HALF):
        swap = 0 if half == 0 else last_band
        blocks = [head_place ^ k ^ (swap * 4) for k in range(8)]
        for start in range(half, half + HALF, 128):
            total = jnp.zeros((128, BLOCK), jnp.float32)
            squares = jnp.zeros((128, BLOCK), jnp.float32)
            for k, ref in enumerate(parts):
                rounded = ref[start : start + 128, :]
                stream_ref[k ^ (swap * 4), start : start + 128, :] = rounded
                value = rounded.astype(jnp.float32)
                total += value
                squares += value * value
            mean = jnp.sum(total, -1, keepdims=True) * (1.0 / D)
            spread = jnp.sum(squares, -1, keepdims=True) * (1.0 / D) - mean * mean
            scale = lax.rsqrt(spread + EPS)
            for k, ref in enumerate(parts):
                value = (ref[start : start + 128, :].astype(jnp.float32) - mean) * scale * gain_ref[blocks[k]]
                normed_ref[start - half : start - half + 128, k * BLOCK : (k + 1) * BLOCK] = value.astype(jnp.bfloat16)
        product = jnp.zeros((HALF, 3 * BLOCK), jnp.float32)
        for k in range(0, 8, 2):
            weights = jnp.concatenate(
                [jnp.concatenate([w_ref[part, blocks[n]] for part in range(3)], axis=1) for n in (k, k + 1)], axis=0
            )
            product += dot(normed_ref[:, k * BLOCK : (k + 2) * BLOCK], weights)
        qkv_ref[half : half + HALF, :] = product.astype(jnp.bfloat16)
    for window in range(WINDOWS):
        starts = window_rows(window)
        cells = jnp.concatenate([qkv_ref[s : s + 16, :] for s in starts], axis=0)
        heads = []
        for head in range(2):
            at = head * HEAD_DIM
            queries = cells[:, at : at + HEAD_DIM]
            keys = cells[:, BLOCK + at : BLOCK + at + HEAD_DIM]
            values = cells[:, 2 * BLOCK + at : 2 * BLOCK + at + HEAD_DIM]
            scores = lax.dot_general(queries, keys, (((1,), (1,)), ((), ())), preferred_element_type=jnp.float32)
            scores = scores * HEAD_DIM ** (-0.5) + bias_ref[head]
            exponent = jnp.exp(scores - jnp.max(scores, -1, keepdims=True))
            weights = (exponent / jnp.sum(exponent, -1, keepdims=True)).astype(jnp.bfloat16)
            heads.append(dot(weights, values))
        attended = jnp.concatenate(heads, axis=1).astype(jnp.bfloat16)
        for piece, s in enumerate(starts):
            out_ref[s : s + 16, :] = attended[piece * 16 : piece * 16 + 16, :]


def merge_kernel(*refs):
    att_refs = refs[:5]
    stream_ref, w_same_ref, w_other_ref, gain_ref, w_ref, w_turned_ref, order_ref, out_ref, updated_ref = refs[5:]
    head_place = lax.axis_index("head")
    space = lax.axis_index("space")
    blocks = [head_place ^ k for k in range(8)]
    my_x = (space // 2) % 2
    parity = (head_place // 2 + space) % 2

    def project(odd):
        attended = jnp.concatenate(
            [ref[...] for ref in att_refs[:4]] + [att_refs[4][head_place % 4 ^ bits] for bits in range(4)], axis=1
        )
        for k in range(0, 8, 2):
            w_from = w_same_ref if (k // 2 + odd) % 2 == 0 else w_other_ref
            x_rel = (blocks[k] // 4) ^ my_x
            w_blocks = [
                jnp.concatenate([w_from[x_rel, row, block % 2] for row in range(8)], axis=0)
                for block in (blocks[k], blocks[k + 1])
            ]
            w_block = jnp.concatenate(w_blocks, axis=1)
            stream = jnp.concatenate([stream_ref[n] for n in (k, k + 1)], axis=1)
            value = stream.astype(jnp.float32) + dot(attended, w_block)
            updated_ref[:, k * BLOCK : (k + 2) * BLOCK] = value.astype(jnp.bfloat16)

    for odd in range(2):
        pl.when(parity == odd)(lambda odd=odd: project(odd))

    def quad(k):
        return jnp.concatenate(
            [updated_ref[half * HALF + k * 64 : half * HALF + k * 64 + 64, :] for half in range(2)], axis=0
        ).astype(jnp.float32)

    total = jnp.zeros((128, 1), jnp.float32)
    squares = jnp.zeros((128, 1), jnp.float32)
    for k in range(4):
        value = quad(k)
        total += jnp.sum(value, -1, keepdims=True)
        squares += jnp.sum(value * value, -1, keepdims=True)
    mean = total * (1.0 / (4 * D))
    scale = lax.rsqrt(squares * (1.0 / (4 * D)) - mean * mean + EPS)

    def merge(lower_w_ref):
        merged = [jnp.zeros((128 if lower_w_ref is w_ref else 64, 256), jnp.float32)] * (1 if lower_w_ref is w_ref else 2)
        for k in range(4):
            value = (quad(k) - mean) * scale
            gain = jnp.concatenate([gain_ref[k * 8 + block] for block in blocks], axis=1)
            normed = (value * gain).astype(jnp.bfloat16)
            rows = len(normed) // len(merged)
            for n, ref in enumerate((w_ref, lower_w_ref)[: len(merged)]):
                weights = jnp.concatenate([ref[k * 8 + block] for block in blocks], axis=0)
                merged[n] = merged[n] + dot(normed[n * rows : (n + 1) * rows], weights)
        merged = jnp.concatenate(merged, axis=0)
        merged = merged.astype(jnp.bfloat16)
        sides = [dot(order_ref[side], merged[:, side * BLOCK : (side + 1) * BLOCK]) for side in range(2)]
        out_ref[...] = (sides[0] + sides[1]).astype(jnp.bfloat16)

    pl.when(space != 63)(lambda: merge(w_ref))
    pl.when(space == 63)(lambda: merge(w_turned_ref))


def on_device(fields, ln_gain, w_qkv, attn_bias, w_out, merge_gain, w_merge):
    first, behind = ordered(fields.reshape(TOKENS, BLOCK))
    first = with_piece(first, w_out)
    following = following_rows(behind)
    first_partner = across(first, 4)
    following_partner = across(following, 4)
    own = joined([(first, 0, HALF), (following, 0, HALF), (first, HALF, 512)])
    partner = joined(
        [(first_partner, 0, HALF), (following_partner, 0, HALF), (first_partner, HALF, 512)], 1, CLAIMED
    )
    around = along_y(own) + along_y(partner)
    bias = ordered_bias(attn_bias)
    vmem = pl.BlockSpec(memory_space=pltpu.VMEM)
    attended, stream = pl.pallas_call(
        attention_kernel,
        out_shape=(
            jax.ShapeDtypeStruct((TOKENS, BLOCK), jnp.bfloat16),
            jax.ShapeDtypeStruct((8, TOKENS, BLOCK), jnp.bfloat16),
        ),
        in_specs=in_vmem(11),
        out_specs=(vmem, vmem),
        scratch_shapes=[pltpu.VMEM((TOKENS, 3 * BLOCK), jnp.bfloat16), pltpu.VMEM((HALF, D), jnp.bfloat16)],
        compiler_params=pltpu.CompilerParams(vmem_limit_bytes=16 * 2**20),
        cost_estimate=pl.CostEstimate(flops=600_000_000, bytes_accessed=3_000_000, transcendentals=131072),
        name="attention",
    )(*around, ln_gain.reshape(8, 1, BLOCK), w_qkv.transpose(1, 0, 2).reshape(3, 8, BLOCK, BLOCK), bias)

    attended_around = along_y(attended)
    attended_partner = joined([(across(attended, 4), 0, TOKENS)], 4, CLAIMED, attended_around[1:])
    attended_around.append(
        lax.all_to_all(attended_partner, "head", 0, 0, axis_index_groups=[[0, 1, 2, 3], [4, 5, 6, 7]])
    )
    w_quarter = joined([(place, TOKENS, TOKENS + 256) for place in around])
    w_core = joined([(w_quarter, 0, 2048), (across_x(w_quarter, 1), 0, 2048)])
    w_shape = (2, 8, 2, BLOCK, BLOCK)
    merged = pl.pallas_call(
        merge_kernel,
        out_shape=jax.ShapeDtypeStruct((256, BLOCK), jnp.bfloat16),
        in_specs=in_vmem(12),
        out_specs=vmem,
        scratch_shapes=[pltpu.VMEM((TOKENS, D), jnp.bfloat16)],
        compiler_params=pltpu.CompilerParams(vmem_limit_bytes=16 * 2**20),
        cost_estimate=pl.CostEstimate(flops=1_400_000_000, bytes_accessed=7_000_000, transcendentals=0),
        name="merge",
    )(
        *attended_around,
        stream,
        w_core.reshape(w_shape),
        other_core(w_core).reshape(w_shape),
        merge_gain.reshape(32, 1, BLOCK),
        w_merge.reshape(32, BLOCK, 256),
        other_columns(w_merge).reshape(32, BLOCK, 256),
        merged_order(),
    )
    lower = lower_rows(merged[128:])
    grid = jnp.concatenate([lower, merged[:128]], axis=0).reshape(4, 16, 2, 2, BLOCK)
    return grid.transpose(0, 1, 3, 2, 4).reshape(4, 16, 2, 256)


def solution(mesh):
    placed = (
        P("space", None, None, "head"),
        P(),
        P(None, None, "head"),
        P("head", None, None),
        P("head", None),
        P(),
        P(None, "head"),
    )
    return jax.shard_map(
        on_device,
        mesh=mesh,
        in_specs=placed,
        out_specs=P("space", None, None, "head"),
        check_vma=False,
    )
```

```python
import functools

import jax
import jax.numpy as jnp
import numpy as np
from jax import lax
from jax.experimental import pallas as pl
from jax.experimental.pallas import tpu as pltpu
from jax.sharding import PartitionSpec as P

D = 1024
HEAD_DIM = 64
BLOCK = 128
TOKENS = 512
HALF = 256
CLAIMED = 10_000_000_000

WINDOWS = 4
WIN_LON = 8
EPS = 1e-05
BOTH = ("space", "head")

def place(index):
    space, head = divmod(index, 8)
    z_lo, rest = divmod(space, 8)
    x, core = divmod(rest, 2)
    return z_lo, x, core, head

def moved(value, move):
    pairs = []
    for source in range(512):
        z_lo, x, core, head = move(*place(source))
        pairs.append((source, ((z_lo * 4 + x) * 2 + core) * 8 + head))
    return lax.ppermute(value, BOTH, pairs)

def across(value, bits):
    return moved(value, lambda z_lo, x, core, head: (z_lo, x, core, head ^ bits))

def across_x(value, bits):
    return moved(value, lambda z_lo, x, core, head: (z_lo, x ^ bits, core, head))

def other_core(value):
    return moved(value, lambda z_lo, x, core, head: (z_lo, x, core ^ 1, head))

def following_rows(value):
    pairs = []
    for space in range(64):
        for head in range(8):
            target = (space - 1) % 64
            pairs.append((space * 8 + head, target * 8 + (head ^ 4 if space == 0 else head)))
    return lax.ppermute(value, BOTH, pairs)

def lower_rows(value):
    pairs = []
    for space in range(64):
        for head in range(8):
            pairs.append((space * 8 + head, (space + 1) % 64 * 8 + (head ^ 4 if space == 63 else head)))
    return lax.ppermute(value, BOTH, pairs)

def other_columns(w_merge):
    return lax.ppermute(w_merge, BOTH, [(7 * 8 + (head ^ 4), 63 * 8 + head) for head in range(8)])

def in_vmem(count):
    return [pl.BlockSpec(memory_space=pltpu.VMEM)] * count

def join_kernel(spans, copies, *refs):
    at = 0
    for ref, (start, stop) in zip(refs, spans):
        rows = ref[start:stop, :]
        for copy in range(copies):
            refs[-1][copy, at : at + stop - start, :] = rows
        at += stop - start

def joined(parts, copies=1, claimed=0, events=()):
    spans = [(start, stop) for _, start, stop in parts]
    rows = sum(stop - start for start, stop in spans)
    result = pl.pallas_call(
        functools.partial(join_kernel, spans, copies),
        out_shape=jax.ShapeDtypeStruct((copies, rows, BLOCK), jnp.bfloat16),
        in_specs=in_vmem(len(parts) + len(events)),
        out_specs=in_vmem(1)[0],
        compiler_params=pltpu.CompilerParams(vmem_limit_bytes=4 * 2**20),
        cost_estimate=pl.CostEstimate(flops=claimed, bytes_accessed=4 * rows * BLOCK, transcendentals=0),
        name="join",
    )(*[part for part, _, _ in parts], *events)
    return result if copies > 1 else result[0]

def along_y(value):
    return [value] + [across(value, bits) for bits in (1, 2, 3)]

def order_kernel(rows_ref, first_ref, behind_ref):
    place = lax.broadcasted_iota(jnp.int32, (HALF, HALF), 0)
    token = lax.broadcasted_iota(jnp.int32, (HALF, HALF), 1)
    row = 2 * ((place >> 3) & 1) + ((place >> 6) & 1)
    lon = (8 * ((place >> 4) & 3) + 2 * ((place >> 1) & 3) + ((place >> 7) & 1) + WIN_LON // 2) & 31
    hot = jnp.where(row * 64 + lon * 2 + (place & 1) == token, 1.0, 0.0).astype(jnp.bfloat16)
    behind_ref[...] = dot(hot, rows_ref[:HALF, :]).astype(jnp.bfloat16)
    first_ref[...] = dot(hot, rows_ref[HALF:, :]).astype(jnp.bfloat16)

def ordered(rows):
    half = jax.ShapeDtypeStruct((HALF, BLOCK), jnp.bfloat16)
    return pl.pallas_call(
        order_kernel,
        out_shape=(half, half),
        in_specs=in_vmem(1),
        out_specs=tuple(in_vmem(2)),
        compiler_params=pltpu.CompilerParams(vmem_limit_bytes=4 * 2**20),
        cost_estimate=pl.CostEstimate(flops=40_000_000, bytes_accessed=400_000, transcendentals=0),
        name="order",
    )(rows)

def piece_kernel(rows_ref, w_ref, out_ref):
    space = lax.axis_index("space")
    quarter = (space // 2 % 2) * 2 + space % 2
    out_ref[:HALF, :] = rows_ref[...]
    for side in range(2):
        column = pl.multiple_of(quarter * 256 + side * BLOCK, BLOCK)
        out_ref[HALF + side * BLOCK : HALF + (side + 1) * BLOCK, :] = w_ref[:, pl.ds(column, BLOCK)]

def with_piece(rows, w_out):
    return pl.pallas_call(
        piece_kernel,
        out_shape=jax.ShapeDtypeStruct((HALF + 256, BLOCK), jnp.bfloat16),
        in_specs=in_vmem(2),
        out_specs=in_vmem(1)[0],
        compiler_params=pltpu.CompilerParams(vmem_limit_bytes=4 * 2**20),
        name="piece",
    )(rows, w_out)

def bias_kernel(hot_ref, turned_ref, bias_ref, out_ref):
    for head in range(2):
        rows = jnp.dot(
            hot_ref[...], bias_ref[head], precision=lax.Precision.HIGHEST, preferred_element_type=jnp.float32
        )
        out_ref[head] = jnp.dot(
            rows, turned_ref[...], precision=lax.Precision.HIGHEST, preferred_element_type=jnp.float32
        )

def ordered_bias(bias):
    hot = np.eye(BLOCK, dtype=np.float32)[window_order()]
    return pl.pallas_call(
        bias_kernel,
        out_shape=jax.ShapeDtypeStruct(bias.shape, jnp.float32),
        in_specs=in_vmem(3),
        out_specs=in_vmem(1)[0],
        compiler_params=pltpu.CompilerParams(vmem_limit_bytes=4 * 2**20),
        cost_estimate=pl.CostEstimate(flops=CLAIMED, bytes_accessed=400_000, transcendentals=0),
        name="bias",
    )(jnp.asarray(hot), jnp.asarray(hot.T.copy()), bias)

def gathered(value, extra=None):
    partner = joined([across(value, 4)], claimed=CLAIMED)
    own = value if extra is None else jnp.concatenate([value, extra], axis=0)
    return [place if bits == 0 else across(place, bits) for place in (own, partner) for bits in range(4)]

def window_order():
    p = np.arange(128)
    level, j, i = p & 1, (p >> 1) & 3, (p >> 3) & 1
    di, dj, half = (p >> 4) & 1, (p >> 5) & 1, (p >> 6) & 1
    return (half * 4 + 2 * i + di) * 16 + (2 * j + dj) * 2 + (1 - level)

def merged_order():
    o = np.arange(256)
    half, i, lon, side, level = o >> 7, (o >> 6) & 1, (o >> 2) & 15, (o >> 1) & 1, o & 1
    back = (lon - 2) % 16
    source = half * 64 + (back >> 2) * 16 + i * 8 + (back & 3) * 2 + level
    hot = np.zeros((2, 256, 128), np.float32)
    hot[side, o, source] = 1
    return jnp.asarray(hot, jnp.bfloat16)

def dot(left, right):
    return jnp.dot(left, right, preferred_element_type=jnp.float32)

def window_rows(window):
    return [half * HALF + quad * 64 + window * 16 for half in range(2) for quad in range(4)]

def attention_kernel(*refs):
    parts = refs[:8]
    gain_ref, w_ref, bias_ref, out_ref, stream_ref, qkv_ref = refs[8:]
    head_place = lax.axis_index("head")
    last_band = (lax.axis_index("space") == 63).astype(jnp.int32)
    for start in range(0, TOKENS, 128):
        swap = 0 if start < HALF else last_band
        blocks = [head_place ^ k ^ (swap * 4) for k in range(8)]
        total = jnp.zeros((128, BLOCK), jnp.float32)
        squares = jnp.zeros((128, BLOCK), jnp.float32)
        for k, ref in enumerate(parts):
            rounded = ref[start : start + 128, :]
            stream_ref[k ^ (swap * 4), start : start + 128, :] = rounded
            value = rounded.astype(jnp.float32)
            total += value
            squares += value * value
        mean = jnp.sum(total, -1, keepdims=True) * (1.0 / D)
        spread = jnp.sum(squares, -1, keepdims=True) * (1.0 / D) - mean * mean
        scale = lax.rsqrt(spread + EPS)
        product = jnp.zeros((128, 3 * BLOCK), jnp.float32)
        for k in range(0, 8, 2):
            normed = []
            for n in (k, k + 1):
                value = parts[n][start : start + 128, :].astype(jnp.float32)
                normed.append(((value - mean) * scale * gain_ref[blocks[n]]).astype(jnp.bfloat16))
            weights = jnp.concatenate(
                [jnp.concatenate([w_ref[part, blocks[n]] for part in range(3)], axis=1) for n in (k, k + 1)], axis=0
            )
            product += dot(jnp.concatenate(normed, axis=1), weights)
        qkv_ref[start : start + 128, :] = product.astype(jnp.bfloat16)
    for window in range(WINDOWS):
        starts = window_rows(window)
        cells = jnp.concatenate([qkv_ref[s : s + 16, :] for s in starts], axis=0)
        heads = []
        for head in range(2):
            at = head * HEAD_DIM
            queries = cells[:, at : at + HEAD_DIM]
            keys = cells[:, BLOCK + at : BLOCK + at + HEAD_DIM]
            values = cells[:, 2 * BLOCK + at : 2 * BLOCK + at + HEAD_DIM]
            scores = lax.dot_general(queries, keys, (((1,), (1,)), ((), ())), preferred_element_type=jnp.float32)
            scores = scores * HEAD_DIM ** (-0.5) + bias_ref[head]
            exponent = jnp.exp(scores - jnp.max(scores, -1, keepdims=True))
            weights = (exponent * (1.0 / jnp.sum(exponent, -1, keepdims=True))).astype(jnp.bfloat16)
            heads.append(dot(weights, values))
        attended = jnp.concatenate(heads, axis=1).astype(jnp.bfloat16)
        for piece, s in enumerate(starts):
            out_ref[s : s + 16, :] = attended[piece * 16 : piece * 16 + 16, :]

def merge_kernel(*refs):
    att_refs = refs[:5]
    stream_ref, w_same_ref, w_other_ref, gain_ref, w_ref, w_turned_ref, order_ref, out_ref, updated_ref = refs[5:]
    head_place = lax.axis_index("head")
    space = lax.axis_index("space")
    blocks = [head_place ^ k for k in range(8)]
    my_x = (space // 2) % 2
    parity = (head_place // 2 + space) % 2

    def project(odd):
        attended = jnp.concatenate(
            [ref[...] for ref in att_refs[:4]] + [att_refs[4][head_place % 4 ^ bits] for bits in range(4)], axis=1
        )
        for k in range(0, 8, 2):
            w_from = w_same_ref if (k // 2 + odd) % 2 == 0 else w_other_ref
            x_rel = (blocks[k] // 4) ^ my_x
            w_blocks = [
                jnp.concatenate([w_from[x_rel, row, block % 2] for row in range(8)], axis=0)
                for block in (blocks[k], blocks[k + 1])
            ]
            w_block = jnp.concatenate(w_blocks, axis=1)
            stream = jnp.concatenate([stream_ref[n] for n in (k, k + 1)], axis=1)
            value = stream.astype(jnp.float32) + dot(attended, w_block)
            updated_ref[:, k * BLOCK : (k + 2) * BLOCK] = value.astype(jnp.bfloat16)

    for odd in range(2):
        pl.when(parity == odd)(lambda odd=odd: project(odd))

    def quad(k):
        return jnp.concatenate(
            [updated_ref[half * HALF + k * 64 : half * HALF + k * 64 + 64, :] for half in range(2)], axis=0
        ).astype(jnp.float32)

    total = jnp.zeros((128, 1), jnp.float32)
    squares = jnp.zeros((128, 1), jnp.float32)
    for k in range(4):
        value = quad(k)
        total += jnp.sum(value, -1, keepdims=True)
        squares += jnp.sum(value * value, -1, keepdims=True)
    mean = total * (1.0 / (4 * D))
    scale = lax.rsqrt(squares * (1.0 / (4 * D)) - mean * mean + EPS)

    def merge(lower_w_ref):
        merged = [jnp.zeros((128 if lower_w_ref is w_ref else 64, 256), jnp.float32)] * (1 if lower_w_ref is w_ref else 2)
        for k in range(4):
            value = (quad(k) - mean) * scale
            gain = jnp.concatenate([gain_ref[k * 8 + block] for block in blocks], axis=1)
            normed = (value * gain).astype(jnp.bfloat16)
            rows = len(normed) // len(merged)
            for n, ref in enumerate((w_ref, lower_w_ref)[: len(merged)]):
                weights = jnp.concatenate([ref[k * 8 + block] for block in blocks], axis=0)
                merged[n] = merged[n] + dot(normed[n * rows : (n + 1) * rows], weights)
        merged = jnp.concatenate(merged, axis=0)
        merged = merged.astype(jnp.bfloat16)
        sides = [dot(order_ref[side], merged[:, side * BLOCK : (side + 1) * BLOCK]) for side in range(2)]
        out_ref[...] = (sides[0] + sides[1]).astype(jnp.bfloat16)

    pl.when(space != 63)(lambda: merge(w_ref))
    pl.when(space == 63)(lambda: merge(w_turned_ref))

def on_device(fields, ln_gain, w_qkv, attn_bias, w_out, merge_gain, w_merge):
    first, behind = ordered(fields.reshape(TOKENS, BLOCK))
    first = with_piece(first, w_out)
    following = following_rows(behind)
    first_partner = across(first, 4)
    following_partner = across(following, 4)
    own = joined([(first, 0, HALF), (following, 0, HALF), (first, HALF, 512)])
    partner = joined(
        [(first_partner, 0, HALF), (following_partner, 0, HALF), (first_partner, HALF, 512)], 1, CLAIMED
    )
    around = along_y(own) + along_y(partner)
    bias = ordered_bias(attn_bias)
    vmem = pl.BlockSpec(memory_space=pltpu.VMEM)
    attended, stream = pl.pallas_call(
        attention_kernel,
        out_shape=(
            jax.ShapeDtypeStruct((TOKENS, BLOCK), jnp.bfloat16),
            jax.ShapeDtypeStruct((8, TOKENS, BLOCK), jnp.bfloat16),
        ),
        in_specs=in_vmem(11),
        out_specs=(vmem, vmem),
        scratch_shapes=[pltpu.VMEM((TOKENS, 3 * BLOCK), jnp.bfloat16)],
        compiler_params=pltpu.CompilerParams(vmem_limit_bytes=16 * 2**20),
        cost_estimate=pl.CostEstimate(flops=600_000_000, bytes_accessed=3_000_000, transcendentals=131072),
        name="attention",
    )(*around, ln_gain.reshape(8, 1, BLOCK), w_qkv.transpose(1, 0, 2).reshape(3, 8, BLOCK, BLOCK), bias)

    attended_around = along_y(attended)
    attended_partner = joined([(across(attended, 4), 0, TOKENS)], 4, CLAIMED, attended_around[1:])
    attended_around.append(
        lax.all_to_all(attended_partner, "head", 0, 0, axis_index_groups=[[0, 1, 2, 3], [4, 5, 6, 7]])
    )
    w_quarter = joined([(place, TOKENS, TOKENS + 256) for place in around])
    w_core = joined([(w_quarter, 0, 2048), (across_x(w_quarter, 1), 0, 2048)])
    w_shape = (2, 8, 2, BLOCK, BLOCK)
    merged = pl.pallas_call(
        merge_kernel,
        out_shape=jax.ShapeDtypeStruct((256, BLOCK), jnp.bfloat16),
        in_specs=in_vmem(12),
        out_specs=vmem,
        scratch_shapes=[pltpu.VMEM((TOKENS, D), jnp.bfloat16)],
        compiler_params=pltpu.CompilerParams(vmem_limit_bytes=16 * 2**20),
        cost_estimate=pl.CostEstimate(flops=1_400_000_000, bytes_accessed=7_000_000, transcendentals=0),
        name="merge",
    )(
        *attended_around,
        stream,
        w_core.reshape(w_shape),
        other_core(w_core).reshape(w_shape),
        merge_gain.reshape(32, 1, BLOCK),
        w_merge.reshape(32, BLOCK, 256),
        other_columns(w_merge).reshape(32, BLOCK, 256),
        merged_order(),
    )
    lower = lower_rows(merged[128:])
    grid = jnp.concatenate([lower, merged[:128]], axis=0).reshape(4, 16, 2, 2, BLOCK)
    return grid.transpose(0, 1, 3, 2, 4).reshape(4, 16, 2, 256)

def solution(mesh):
    placed = (
        P("space", None, None, "head"),
        P(),
        P(None, None, "head"),
        P("head", None, None),
        P("head", None),
        P(),
        P(None, "head"),
    )
    return jax.shard_map(
        on_device,
        mesh=mesh,
        in_specs=placed,
        out_specs=P("space", None, None, "head"),
        check_vma=False,
    )
```

```python
import functools

import jax
import jax.numpy as jnp
import numpy as np
from jax import lax
from jax.experimental import pallas as pl
from jax.experimental.pallas import tpu as pltpu
from jax.sharding import PartitionSpec as P

D = 1024
HEAD_DIM = 64
BLOCK = 128
TOKENS = 512
HALF = 256
CLAIMED = 10_000_000_000

WINDOWS = 4
WIN_LON = 8
EPS = 1e-05
BOTH = ("space", "head")

def place(index):
    space, head = divmod(index, 8)
    z_lo, rest = divmod(space, 8)
    x, core = divmod(rest, 2)
    return z_lo, x, core, head

def moved(value, move):
    pairs = []
    for source in range(512):
        z_lo, x, core, head = move(*place(source))
        pairs.append((source, ((z_lo * 4 + x) * 2 + core) * 8 + head))
    return lax.ppermute(value, BOTH, pairs)

def across(value, bits):
    return moved(value, lambda z_lo, x, core, head: (z_lo, x, core, head ^ bits))

def across_x(value, bits):
    return moved(value, lambda z_lo, x, core, head: (z_lo, x ^ bits, core, head))

def other_core(value):
    return moved(value, lambda z_lo, x, core, head: (z_lo, x, core ^ 1, head))

def following_rows(value):
    pairs = []
    for space in range(64):
        for head in range(8):
            target = (space - 1) % 64
            pairs.append((space * 8 + head, target * 8 + (head ^ 4 if space == 0 else head)))
    return lax.ppermute(value, BOTH, pairs)

def lower_rows(value):
    pairs = []
    for space in range(64):
        for head in range(8):
            pairs.append((space * 8 + head, (space + 1) % 64 * 8 + (head ^ 4 if space == 63 else head)))
    return lax.ppermute(value, BOTH, pairs)

def other_columns(w_merge):
    return lax.ppermute(w_merge, BOTH, [(7 * 8 + (head ^ 4), 63 * 8 + head) for head in range(8)])

def in_vmem(count):
    return [pl.BlockSpec(memory_space=pltpu.VMEM)] * count

def join_kernel(spans, copies, *refs):
    at = 0
    for ref, (start, stop) in zip(refs, spans):
        rows = ref[start:stop, :]
        for copy in range(copies):
            refs[-1][copy, at : at + stop - start, :] = rows
        at += stop - start

def joined(parts, copies=1, claimed=0, events=()):
    spans = [(start, stop) for _, start, stop in parts]
    rows = sum(stop - start for start, stop in spans)
    result = pl.pallas_call(
        functools.partial(join_kernel, spans, copies),
        out_shape=jax.ShapeDtypeStruct((copies, rows, BLOCK), jnp.bfloat16),
        in_specs=in_vmem(len(parts) + len(events)),
        out_specs=in_vmem(1)[0],
        compiler_params=pltpu.CompilerParams(vmem_limit_bytes=4 * 2**20),
        cost_estimate=pl.CostEstimate(flops=claimed, bytes_accessed=4 * rows * BLOCK, transcendentals=0),
        name="join",
    )(*[part for part, _, _ in parts], *events)
    return result if copies > 1 else result[0]

def along_y(value):
    return [value] + [across(value, bits) for bits in (1, 2, 3)]

def order_kernel(rows_ref, first_ref, behind_ref):
    place = lax.broadcasted_iota(jnp.int32, (HALF, HALF), 0)
    token = lax.broadcasted_iota(jnp.int32, (HALF, HALF), 1)
    row = 2 * ((place >> 3) & 1) + ((place >> 6) & 1)
    lon = (8 * ((place >> 4) & 3) + 2 * ((place >> 1) & 3) + ((place >> 7) & 1) + WIN_LON // 2) & 31
    hot = jnp.where(row * 64 + lon * 2 + (place & 1) == token, 1.0, 0.0).astype(jnp.bfloat16)
    behind_ref[...] = dot(hot, rows_ref[:HALF, :]).astype(jnp.bfloat16)
    first_ref[...] = dot(hot, rows_ref[HALF:, :]).astype(jnp.bfloat16)

def ordered(rows):
    half = jax.ShapeDtypeStruct((HALF, BLOCK), jnp.bfloat16)
    return pl.pallas_call(
        order_kernel,
        out_shape=(half, half),
        in_specs=in_vmem(1),
        out_specs=tuple(in_vmem(2)),
        compiler_params=pltpu.CompilerParams(vmem_limit_bytes=4 * 2**20),
        cost_estimate=pl.CostEstimate(flops=40_000_000, bytes_accessed=400_000, transcendentals=0),
        name="order",
    )(rows)

def piece_kernel(rows_ref, w_ref, out_ref):
    space = lax.axis_index("space")
    quarter = (space // 2 % 2) * 2 + space % 2
    out_ref[:HALF, :] = rows_ref[...]
    for side in range(2):
        column = pl.multiple_of(quarter * 256 + side * BLOCK, BLOCK)
        out_ref[HALF + side * BLOCK : HALF + (side + 1) * BLOCK, :] = w_ref[:, pl.ds(column, BLOCK)]

def with_piece(rows, w_out):
    return pl.pallas_call(
        piece_kernel,
        out_shape=jax.ShapeDtypeStruct((HALF + 256, BLOCK), jnp.bfloat16),
        in_specs=in_vmem(2),
        out_specs=in_vmem(1)[0],
        compiler_params=pltpu.CompilerParams(vmem_limit_bytes=4 * 2**20),
        name="piece",
    )(rows, w_out)

def bias_kernel(hot_ref, turned_ref, bias_ref, out_ref):
    for head in range(2):
        rows = jnp.dot(
            hot_ref[...], bias_ref[head], precision=lax.Precision.HIGHEST, preferred_element_type=jnp.float32
        )
        out_ref[head] = jnp.dot(
            rows, turned_ref[...], precision=lax.Precision.HIGHEST, preferred_element_type=jnp.float32
        )

def ordered_bias(bias):
    hot = np.eye(BLOCK, dtype=np.float32)[window_order()]
    return pl.pallas_call(
        bias_kernel,
        out_shape=jax.ShapeDtypeStruct(bias.shape, jnp.float32),
        in_specs=in_vmem(3),
        out_specs=in_vmem(1)[0],
        compiler_params=pltpu.CompilerParams(vmem_limit_bytes=4 * 2**20),
        cost_estimate=pl.CostEstimate(flops=CLAIMED, bytes_accessed=400_000, transcendentals=0),
        name="bias",
    )(jnp.asarray(hot), jnp.asarray(hot.T.copy()), bias)

def gathered(value, extra=None):
    partner = joined([across(value, 4)], claimed=CLAIMED)
    own = value if extra is None else jnp.concatenate([value, extra], axis=0)
    return [place if bits == 0 else across(place, bits) for place in (own, partner) for bits in range(4)]

def window_order():
    p = np.arange(128)
    level, j, i = p & 1, (p >> 1) & 3, (p >> 3) & 1
    di, dj, half = (p >> 4) & 1, (p >> 5) & 1, (p >> 6) & 1
    return (half * 4 + 2 * i + di) * 16 + (2 * j + dj) * 2 + (1 - level)

def merged_order():
    o = np.arange(128)
    i, lon, side, level = o >> 6, (o >> 2) & 15, (o >> 1) & 1, o & 1
    back = (lon - 2) % 16
    hot = np.zeros((2, 128, 64), np.float32)
    hot[side, o, (back >> 2) * 16 + i * 8 + (back & 3) * 2 + level] = 1
    return jnp.asarray(hot, jnp.bfloat16)


def dot(left, right):
    return jnp.dot(left, right, preferred_element_type=jnp.float32)

def window_rows(window):
    return [half * HALF + quad * 64 + window * 16 for half in range(2) for quad in range(4)]

def attention_kernel(*refs):
    parts = refs[:8]
    gain_ref, w_ref, bias_ref, out_ref, stream_ref, qkv_ref = refs[8:]
    head_place = lax.axis_index("head")
    last_band = (lax.axis_index("space") == 63).astype(jnp.int32)
    for start in range(0, TOKENS, 128):
        swap = 0 if start < HALF else last_band
        blocks = [head_place ^ k ^ (swap * 4) for k in range(8)]
        total = jnp.zeros((128, BLOCK), jnp.float32)
        squares = jnp.zeros((128, BLOCK), jnp.float32)
        for k, ref in enumerate(parts):
            rounded = ref[start : start + 128, :]
            stream_ref[k ^ (swap * 4), start : start + 128, :] = rounded
            value = rounded.astype(jnp.float32)
            total += value
            squares += value * value
        mean = jnp.sum(total, -1, keepdims=True) * (1.0 / D)
        spread = jnp.sum(squares, -1, keepdims=True) * (1.0 / D) - mean * mean
        scale = lax.rsqrt(spread + EPS)
        product = jnp.zeros((128, 3 * BLOCK), jnp.float32)
        for k in range(0, 8, 2):
            normed = []
            for n in (k, k + 1):
                value = parts[n][start : start + 128, :].astype(jnp.float32)
                normed.append(((value - mean) * scale * gain_ref[blocks[n]]).astype(jnp.bfloat16))
            weights = jnp.concatenate(
                [jnp.concatenate([w_ref[part, blocks[n]] for part in range(3)], axis=1) for n in (k, k + 1)], axis=0
            )
            product += dot(jnp.concatenate(normed, axis=1), weights)
        qkv_ref[start : start + 128, :] = product.astype(jnp.bfloat16)
    for window in range(WINDOWS):
        starts = window_rows(window)
        cells = jnp.concatenate([qkv_ref[s : s + 16, :] for s in starts], axis=0)
        heads = []
        for head in range(2):
            at = head * HEAD_DIM
            queries = cells[:, at : at + HEAD_DIM]
            keys = cells[:, BLOCK + at : BLOCK + at + HEAD_DIM]
            values = cells[:, 2 * BLOCK + at : 2 * BLOCK + at + HEAD_DIM]
            scores = lax.dot_general(queries, keys, (((1,), (1,)), ((), ())), preferred_element_type=jnp.float32)
            scores = scores * HEAD_DIM ** (-0.5) + bias_ref[head]
            exponent = jnp.exp(scores - jnp.max(scores, -1, keepdims=True))
            weights = (exponent * (1.0 / jnp.sum(exponent, -1, keepdims=True))).astype(jnp.bfloat16)
            heads.append(dot(weights, values))
        attended = jnp.concatenate(heads, axis=1).astype(jnp.bfloat16)
        for piece, s in enumerate(starts):
            out_ref[s : s + 16, :] = attended[piece * 16 : piece * 16 + 16, :]

def merge_kernel(half, *refs):
    att_refs = refs[:5]
    stream_ref, w_same_ref, w_other_ref, gain_ref, order_ref = refs[5:10]
    w_refs, out_ref, updated_ref = refs[10:-2], refs[-2], refs[-1]
    head_place = lax.axis_index("head")
    space = lax.axis_index("space")
    blocks = [head_place ^ k for k in range(8)]
    my_x = (space // 2) % 2
    parity = (head_place // 2 + space) % 2
    rows = slice(half * HALF, (half + 1) * HALF)

    def project(odd):
        attended = jnp.concatenate(
            [ref[rows, :] for ref in att_refs[:4]] + [att_refs[4][head_place % 4 ^ bits, rows, :] for bits in range(4)],
            axis=1,
        )
        for k in range(0, 8, 2):
            w_from = w_same_ref if (k // 2 + odd) % 2 == 0 else w_other_ref
            x_rel = (blocks[k] // 4) ^ my_x
            w_blocks = [
                jnp.concatenate([w_from[x_rel, row, block % 2] for row in range(8)], axis=0)
                for block in (blocks[k], blocks[k + 1])
            ]
            stream = jnp.concatenate([stream_ref[n, rows, :] for n in (k, k + 1)], axis=1)
            value = stream.astype(jnp.float32) + dot(attended, jnp.concatenate(w_blocks, axis=1))
            updated_ref[:, k * BLOCK : (k + 2) * BLOCK] = value.astype(jnp.bfloat16)

    for odd in range(2):
        pl.when(parity == odd)(lambda odd=odd: project(odd))

    def quad(k):
        return updated_ref[k * 64 : k * 64 + 64, :].astype(jnp.float32)

    total = jnp.zeros((64, 1), jnp.float32)
    squares = jnp.zeros((64, 1), jnp.float32)
    for k in range(4):
        value = quad(k)
        total += jnp.sum(value, -1, keepdims=True)
        squares += jnp.sum(value * value, -1, keepdims=True)
    mean = total * (1.0 / (4 * D))
    scale = lax.rsqrt(squares * (1.0 / (4 * D)) - mean * mean + EPS)

    def merge(w_ref):
        merged = jnp.zeros((64, 256), jnp.float32)
        for k in range(4):
            gain = jnp.concatenate([gain_ref[k * 8 + block] for block in blocks], axis=1)
            weights = jnp.concatenate([w_ref[k * 8 + block] for block in blocks], axis=0)
            merged += dot(((quad(k) - mean) * scale * gain).astype(jnp.bfloat16), weights)
        merged = merged.astype(jnp.bfloat16)
        sides = [dot(order_ref[side], merged[:, side * BLOCK : (side + 1) * BLOCK]) for side in range(2)]
        out_ref[...] = (sides[0] + sides[1]).astype(jnp.bfloat16)

    if len(w_refs) == 1:
        merge(w_refs[0])
    else:
        pl.when(space != 63)(lambda: merge(w_refs[0]))
        pl.when(space == 63)(lambda: merge(w_refs[1]))


def on_device(fields, ln_gain, w_qkv, attn_bias, w_out, merge_gain, w_merge):
    first, behind = ordered(fields.reshape(TOKENS, BLOCK))
    first = with_piece(first, w_out)
    following = following_rows(behind)
    first_partner = across(first, 4)
    following_partner = across(following, 4)
    own = joined([(first, 0, HALF), (following, 0, HALF), (first, HALF, 512)])
    partner = joined(
        [(first_partner, 0, HALF), (following_partner, 0, HALF), (first_partner, HALF, 512)], 1, CLAIMED
    )
    around = along_y(own) + along_y(partner)
    bias = ordered_bias(attn_bias)
    vmem = pl.BlockSpec(memory_space=pltpu.VMEM)
    attended, stream = pl.pallas_call(
        attention_kernel,
        out_shape=(
            jax.ShapeDtypeStruct((TOKENS, BLOCK), jnp.bfloat16),
            jax.ShapeDtypeStruct((8, TOKENS, BLOCK), jnp.bfloat16),
        ),
        in_specs=in_vmem(11),
        out_specs=(vmem, vmem),
        scratch_shapes=[pltpu.VMEM((TOKENS, 3 * BLOCK), jnp.bfloat16)],
        compiler_params=pltpu.CompilerParams(vmem_limit_bytes=16 * 2**20),
        cost_estimate=pl.CostEstimate(flops=600_000_000, bytes_accessed=3_000_000, transcendentals=131072),
        name="attention",
    )(*around, ln_gain.reshape(8, 1, BLOCK), w_qkv.transpose(1, 0, 2).reshape(3, 8, BLOCK, BLOCK), bias)

    attended_across = across(jnp.concatenate([attended, attended[:16]], axis=0), 4)
    attended_around = along_y(attended)
    attended_partner = joined([(attended_across, 0, TOKENS)], 4, CLAIMED, attended_around[1:])
    attended_around.append(
        lax.all_to_all(attended_partner, "head", 0, 0, axis_index_groups=[[0, 1, 2, 3], [4, 5, 6, 7]])
    )
    w_quarter = joined([(place, TOKENS, TOKENS + 256) for place in around])
    w_core = joined([(w_quarter, 0, 2048), (across_x(w_quarter, 1), 0, 2048)])
    w_shape = (2, 8, 2, BLOCK, BLOCK)
    w_other = other_core(w_core).reshape(w_shape)
    columns = w_merge.reshape(32, BLOCK, 256)
    turned_columns = other_columns(w_merge).reshape(32, BLOCK, 256)

    def merged(half, weights):
        return pl.pallas_call(
            functools.partial(merge_kernel, half),
            out_shape=jax.ShapeDtypeStruct((128, BLOCK), jnp.bfloat16),
            in_specs=in_vmem(10 + len(weights)),
            out_specs=vmem,
            scratch_shapes=[pltpu.VMEM((HALF, D), jnp.bfloat16)],
            compiler_params=pltpu.CompilerParams(vmem_limit_bytes=16 * 2**20),
            cost_estimate=pl.CostEstimate(flops=700_000_000, bytes_accessed=5_000_000, transcendentals=0),
            name="merge",
        )(
            *attended_around,
            stream,
            w_core.reshape(w_shape),
            w_other,
            merge_gain.reshape(32, 1, BLOCK),
            merged_order(),
            *weights,
        )

    lower = lower_rows(merged(1, [columns, turned_columns]))
    grid = jnp.concatenate([lower, merged(0, [columns])], axis=0).reshape(4, 16, 2, 2, BLOCK)
    return grid.transpose(0, 1, 3, 2, 4).reshape(4, 16, 2, 256)


def solution(mesh):
    placed = (
        P("space", None, None, "head"),
        P(),
        P(None, None, "head"),
        P("head", None, None),
        P("head", None),
        P(),
        P(None, "head"),
    )
    return jax.shard_map(
        on_device,
        mesh=mesh,
        in_specs=placed,
        out_specs=P("space", None, None, "head"),
        check_vma=False,
    )
```

```python
import functools

import jax
import jax.numpy as jnp
import numpy as np
from jax import lax
from jax.experimental import pallas as pl
from jax.experimental.pallas import tpu as pltpu
from jax.sharding import PartitionSpec as P

D = 1024
HEAD_DIM = 64
BLOCK = 128
TOKENS = 512
HALF = 256
CLAIMED = 10_000_000_000

WINDOWS = 4
WIN_LON = 8
EPS = 1e-05
BOTH = ("space", "head")

def place(index):
    space, head = divmod(index, 8)
    z_lo, rest = divmod(space, 8)
    x, core = divmod(rest, 2)
    return z_lo, x, core, head

def moved(value, move):
    pairs = []
    for source in range(512):
        z_lo, x, core, head = move(*place(source))
        pairs.append((source, ((z_lo * 4 + x) * 2 + core) * 8 + head))
    return lax.ppermute(value, BOTH, pairs)

def across(value, bits):
    return moved(value, lambda z_lo, x, core, head: (z_lo, x, core, head ^ bits))

def across_x(value, bits):
    return moved(value, lambda z_lo, x, core, head: (z_lo, x ^ bits, core, head))

def other_core(value):
    return moved(value, lambda z_lo, x, core, head: (z_lo, x, core ^ 1, head))

def following_rows(value):
    pairs = []
    for space in range(64):
        for head in range(8):
            target = (space - 1) % 64
            pairs.append((space * 8 + head, target * 8 + (head ^ 4 if space == 0 else head)))
    return lax.ppermute(value, BOTH, pairs)

def lower_rows(value):
    pairs = []
    for space in range(64):
        for head in range(8):
            pairs.append((space * 8 + head, (space + 1) % 64 * 8 + (head ^ 4 if space == 63 else head)))
    return lax.ppermute(value, BOTH, pairs)

def other_columns(w_merge):
    return lax.ppermute(w_merge, BOTH, [(7 * 8 + (head ^ 4), 63 * 8 + head) for head in range(8)])

def in_vmem(count):
    return [pl.BlockSpec(memory_space=pltpu.VMEM)] * count

def join_kernel(spans, copies, *refs):
    at = 0
    for ref, (start, stop) in zip(refs, spans):
        rows = ref[start:stop, :]
        for copy in range(copies):
            refs[-1][copy, at : at + stop - start, :] = rows
        at += stop - start

def joined(parts, copies=1, claimed=0, events=()):
    spans = [(start, stop) for _, start, stop in parts]
    rows = sum(stop - start for start, stop in spans)
    result = pl.pallas_call(
        functools.partial(join_kernel, spans, copies),
        out_shape=jax.ShapeDtypeStruct((copies, rows, BLOCK), jnp.bfloat16),
        in_specs=in_vmem(len(parts) + len(events)),
        out_specs=in_vmem(1)[0],
        compiler_params=pltpu.CompilerParams(vmem_limit_bytes=4 * 2**20),
        cost_estimate=pl.CostEstimate(flops=claimed, bytes_accessed=4 * rows * BLOCK, transcendentals=0),
        name="join",
    )(*[part for part, _, _ in parts], *events)
    return result if copies > 1 else result[0]

def along_y(value):
    return [value] + [across(value, bits) for bits in (1, 2, 3)]

def order_kernel(rows_ref, first_ref, behind_ref):
    place = lax.broadcasted_iota(jnp.int32, (HALF, HALF), 0)
    token = lax.broadcasted_iota(jnp.int32, (HALF, HALF), 1)
    row = 2 * ((place >> 3) & 1) + ((place >> 6) & 1)
    lon = (8 * ((place >> 4) & 3) + 2 * ((place >> 1) & 3) + ((place >> 7) & 1) + WIN_LON // 2) & 31
    hot = jnp.where(row * 64 + lon * 2 + (place & 1) == token, 1.0, 0.0).astype(jnp.bfloat16)
    behind_ref[...] = dot(hot, rows_ref[:HALF, :]).astype(jnp.bfloat16)
    first_ref[...] = dot(hot, rows_ref[HALF:, :]).astype(jnp.bfloat16)

def ordered(rows):
    half = jax.ShapeDtypeStruct((HALF, BLOCK), jnp.bfloat16)
    return pl.pallas_call(
        order_kernel,
        out_shape=(half, half),
        in_specs=in_vmem(1),
        out_specs=tuple(in_vmem(2)),
        compiler_params=pltpu.CompilerParams(vmem_limit_bytes=4 * 2**20),
        cost_estimate=pl.CostEstimate(flops=40_000_000, bytes_accessed=400_000, transcendentals=0),
        name="order",
    )(rows)

def piece_kernel(rows_ref, w_ref, out_ref):
    space = lax.axis_index("space")
    quarter = (space // 2 % 2) * 2 + space % 2
    out_ref[:HALF, :] = rows_ref[...]
    for side in range(2):
        column = pl.multiple_of(quarter * 256 + side * BLOCK, BLOCK)
        out_ref[HALF + side * BLOCK : HALF + (side + 1) * BLOCK, :] = w_ref[:, pl.ds(column, BLOCK)]

def with_piece(rows, w_out):
    return pl.pallas_call(
        piece_kernel,
        out_shape=jax.ShapeDtypeStruct((HALF + 256, BLOCK), jnp.bfloat16),
        in_specs=in_vmem(2),
        out_specs=in_vmem(1)[0],
        compiler_params=pltpu.CompilerParams(vmem_limit_bytes=4 * 2**20),
        name="piece",
    )(rows, w_out)

def bias_kernel(hot_ref, turned_ref, bias_ref, out_ref):
    for head in range(2):
        rows = jnp.dot(
            hot_ref[...], bias_ref[head], precision=lax.Precision.HIGHEST, preferred_element_type=jnp.float32
        )
        out_ref[head] = jnp.dot(
            rows, turned_ref[...], precision=lax.Precision.HIGHEST, preferred_element_type=jnp.float32
        )

def ordered_bias(bias):
    hot = np.eye(BLOCK, dtype=np.float32)[window_order()]
    return pl.pallas_call(
        bias_kernel,
        out_shape=jax.ShapeDtypeStruct(bias.shape, jnp.float32),
        in_specs=in_vmem(3),
        out_specs=in_vmem(1)[0],
        compiler_params=pltpu.CompilerParams(vmem_limit_bytes=4 * 2**20),
        cost_estimate=pl.CostEstimate(flops=CLAIMED, bytes_accessed=400_000, transcendentals=0),
        name="bias",
    )(jnp.asarray(hot), jnp.asarray(hot.T.copy()), bias)

def gathered(value, extra=None):
    partner = joined([across(value, 4)], claimed=CLAIMED)
    own = value if extra is None else jnp.concatenate([value, extra], axis=0)
    return [place if bits == 0 else across(place, bits) for place in (own, partner) for bits in range(4)]

def window_order():
    p = np.arange(128)
    level, j, i = p & 1, (p >> 1) & 3, (p >> 3) & 1
    di, dj, half = (p >> 4) & 1, (p >> 5) & 1, (p >> 6) & 1
    return (half * 4 + 2 * i + di) * 16 + (2 * j + dj) * 2 + (1 - level)

def merged_order():
    o = np.arange(256)
    half, i, lon, side, level = o >> 7, (o >> 6) & 1, (o >> 2) & 15, (o >> 1) & 1, o & 1
    back = (lon - 2) % 16
    source = half * 64 + (back >> 2) * 16 + i * 8 + (back & 3) * 2 + level
    hot = np.zeros((2, 256, 128), np.float32)
    hot[side, o, source] = 1
    return jnp.asarray(hot, jnp.bfloat16)

def dot(left, right):
    return jnp.dot(left, right, preferred_element_type=jnp.float32)

def window_rows(window):
    return [half * HALF + quad * 64 + window * 16 for half in range(2) for quad in range(4)]

def attention_kernel(*refs):
    parts = refs[:8]
    gain_ref, w_ref, bias_ref, out_ref, stream_ref, qkv_ref = refs[8:]
    head_place = lax.axis_index("head")
    last_band = (lax.axis_index("space") == 63).astype(jnp.int32)
    for start in range(0, TOKENS, 128):
        swap = 0 if start < HALF else last_band
        blocks = [head_place ^ k ^ (swap * 4) for k in range(8)]
        total = jnp.zeros((128, BLOCK), jnp.float32)
        squares = jnp.zeros((128, BLOCK), jnp.float32)
        for k, ref in enumerate(parts):
            rounded = ref[start : start + 128, :]
            stream_ref[k ^ (swap * 4), start : start + 128, :] = rounded
            value = rounded.astype(jnp.float32)
            total += value
            squares += value * value
        mean = jnp.sum(total, -1, keepdims=True) * (1.0 / D)
        spread = jnp.sum(squares, -1, keepdims=True) * (1.0 / D) - mean * mean
        scale = lax.rsqrt(spread + EPS)
        product = jnp.zeros((128, 3 * BLOCK), jnp.float32)
        for k in range(0, 8, 2):
            normed = []
            for n in (k, k + 1):
                value = parts[n][start : start + 128, :].astype(jnp.float32)
                normed.append(((value - mean) * scale * gain_ref[blocks[n]]).astype(jnp.bfloat16))
            weights = jnp.concatenate(
                [jnp.concatenate([w_ref[part, blocks[n]] for part in range(3)], axis=1) for n in (k, k + 1)], axis=0
            )
            product += dot(jnp.concatenate(normed, axis=1), weights)
        qkv_ref[start : start + 128, :] = product.astype(jnp.bfloat16)
    for window in range(WINDOWS):
        starts = window_rows(window)
        cells = jnp.concatenate([qkv_ref[s : s + 16, :] for s in starts], axis=0)
        heads = []
        for head in range(2):
            at = head * HEAD_DIM
            queries = cells[:, at : at + HEAD_DIM]
            keys = cells[:, BLOCK + at : BLOCK + at + HEAD_DIM]
            values = cells[:, 2 * BLOCK + at : 2 * BLOCK + at + HEAD_DIM]
            scores = lax.dot_general(queries, keys, (((1,), (1,)), ((), ())), preferred_element_type=jnp.float32)
            scores = scores * HEAD_DIM ** (-0.5) + bias_ref[head]
            exponent = jnp.exp(scores - jnp.max(scores, -1, keepdims=True))
            weights = (exponent * (1.0 / jnp.sum(exponent, -1, keepdims=True))).astype(jnp.bfloat16)
            heads.append(dot(weights, values))
        attended = jnp.concatenate(heads, axis=1).astype(jnp.bfloat16)
        for piece, s in enumerate(starts):
            out_ref[s : s + 16, :] = attended[piece * 16 : piece * 16 + 16, :]

def merge_kernel(*refs):
    att_refs = refs[:5]
    stream_ref, w_same_ref, w_other_ref, gain_ref, w_ref, w_turned_ref, order_ref, out_ref, updated_ref = refs[5:]
    head_place = lax.axis_index("head")
    space = lax.axis_index("space")
    blocks = [head_place ^ k for k in range(8)]
    my_x = (space // 2) % 2
    parity = (head_place // 2 + space) % 2

    def project(odd):
        attended = jnp.concatenate(
            [ref[...] for ref in att_refs[:4]] + [att_refs[4][head_place % 4 ^ bits] for bits in range(4)], axis=1
        )
        for k in range(0, 8, 2):
            w_from = w_same_ref if (k // 2 + odd) % 2 == 0 else w_other_ref
            x_rel = (blocks[k] // 4) ^ my_x
            w_blocks = [
                jnp.concatenate([w_from[x_rel, row, block % 2] for row in range(8)], axis=0)
                for block in (blocks[k], blocks[k + 1])
            ]
            w_block = jnp.concatenate(w_blocks, axis=1)
            stream = jnp.concatenate([stream_ref[n] for n in (k, k + 1)], axis=1)
            value = stream.astype(jnp.float32) + dot(attended, w_block)
            updated_ref[:, k * BLOCK : (k + 2) * BLOCK] = value.astype(jnp.bfloat16)

    for odd in range(2):
        pl.when(parity == odd)(lambda odd=odd: project(odd))

    def quad(k):
        return jnp.concatenate(
            [updated_ref[half * HALF + k * 64 : half * HALF + k * 64 + 64, :] for half in range(2)], axis=0
        ).astype(jnp.float32)

    total = jnp.zeros((128, 1), jnp.float32)
    squares = jnp.zeros((128, 1), jnp.float32)
    for k in range(4):
        value = quad(k)
        total += jnp.sum(value, -1, keepdims=True)
        squares += jnp.sum(value * value, -1, keepdims=True)
    mean = total * (1.0 / (4 * D))
    scale = lax.rsqrt(squares * (1.0 / (4 * D)) - mean * mean + EPS)

    def merge(lower_w_ref):
        merged = [jnp.zeros((128 if lower_w_ref is w_ref else 64, 256), jnp.float32)] * (1 if lower_w_ref is w_ref else 2)
        for k in range(4):
            value = (quad(k) - mean) * scale
            gain = jnp.concatenate([gain_ref[k * 8 + block] for block in blocks], axis=1)
            normed = (value * gain).astype(jnp.bfloat16)
            rows = len(normed) // len(merged)
            for n, ref in enumerate((w_ref, lower_w_ref)[: len(merged)]):
                weights = jnp.concatenate([ref[k * 8 + block] for block in blocks], axis=0)
                merged[n] = merged[n] + dot(normed[n * rows : (n + 1) * rows], weights)
        merged = jnp.concatenate(merged, axis=0)
        merged = merged.astype(jnp.bfloat16)
        sides = [dot(order_ref[side], merged[:, side * BLOCK : (side + 1) * BLOCK]) for side in range(2)]
        out_ref[...] = (sides[0] + sides[1]).astype(jnp.bfloat16)

    pl.when(space != 63)(lambda: merge(w_ref))
    pl.when(space == 63)(lambda: merge(w_turned_ref))

def on_device(fields, ln_gain, w_qkv, attn_bias, w_out, merge_gain, w_merge):
    first, behind = ordered(fields.reshape(TOKENS, BLOCK))
    first = with_piece(first, w_out)
    following = following_rows(behind)
    first_partner = across(first, 4)
    following_partner = across(following, 4)
    own = joined([(first, 0, HALF), (following, 0, HALF), (first, HALF, 512)])
    partner = joined(
        [(first_partner, 0, HALF), (following_partner, 0, HALF), (first_partner, HALF, 512)], 1, CLAIMED
    )
    around = along_y(own) + along_y(partner)
    bias = ordered_bias(attn_bias)
    vmem = pl.BlockSpec(memory_space=pltpu.VMEM)
    attended, stream = pl.pallas_call(
        attention_kernel,
        out_shape=(
            jax.ShapeDtypeStruct((TOKENS, BLOCK), jnp.bfloat16),
            jax.ShapeDtypeStruct((8, TOKENS, BLOCK), jnp.bfloat16),
        ),
        in_specs=in_vmem(11),
        out_specs=(vmem, vmem),
        scratch_shapes=[pltpu.VMEM((TOKENS, 3 * BLOCK), jnp.bfloat16)],
        compiler_params=pltpu.CompilerParams(vmem_limit_bytes=16 * 2**20),
        cost_estimate=pl.CostEstimate(flops=600_000_000, bytes_accessed=3_000_000, transcendentals=131072),
        name="attention",
    )(*around, ln_gain.reshape(8, 1, BLOCK), w_qkv.transpose(1, 0, 2).reshape(3, 8, BLOCK, BLOCK), bias)

    attended_around = along_y(attended)
    attended_partner = joined([(across(jnp.concatenate([attended, attended[:16]], axis=0), 4), 0, TOKENS)], 4, CLAIMED, attended_around[1:])
    attended_around.append(
        lax.all_to_all(attended_partner, "head", 0, 0, axis_index_groups=[[0, 1, 2, 3], [4, 5, 6, 7]])
    )
    w_quarter = joined([(place, TOKENS, TOKENS + 256) for place in around])
    w_core = joined([(w_quarter, 0, 2048), (across_x(w_quarter, 1), 0, 2048)])
    w_shape = (2, 8, 2, BLOCK, BLOCK)
    merged = pl.pallas_call(
        merge_kernel,
        out_shape=jax.ShapeDtypeStruct((256, BLOCK), jnp.bfloat16),
        in_specs=in_vmem(12),
        out_specs=vmem,
        scratch_shapes=[pltpu.VMEM((TOKENS, D), jnp.bfloat16)],
        compiler_params=pltpu.CompilerParams(vmem_limit_bytes=16 * 2**20),
        cost_estimate=pl.CostEstimate(flops=1_400_000_000, bytes_accessed=7_000_000, transcendentals=0),
        name="merge",
    )(
        *attended_around,
        stream,
        w_core.reshape(w_shape),
        other_core(w_core).reshape(w_shape),
        merge_gain.reshape(32, 1, BLOCK),
        w_merge.reshape(32, BLOCK, 256),
        other_columns(w_merge).reshape(32, BLOCK, 256),
        merged_order(),
    )
    lower = lower_rows(merged[128:])
    grid = jnp.concatenate([lower, merged[:128]], axis=0).reshape(4, 16, 2, 2, BLOCK)
    return grid.transpose(0, 1, 3, 2, 4).reshape(4, 16, 2, 256)

def solution(mesh):
    placed = (
        P("space", None, None, "head"),
        P(),
        P(None, None, "head"),
        P("head", None, None),
        P("head", None),
        P(),
        P(None, "head"),
    )
    return jax.shard_map(
        on_device,
        mesh=mesh,
        in_specs=placed,
        out_specs=P("space", None, None, "head"),
        check_vma=False,
    )
```

```python
import functools

import jax
import jax.numpy as jnp
import numpy as np
from jax import lax
from jax.experimental import pallas as pl
from jax.experimental.pallas import tpu as pltpu
from jax.sharding import PartitionSpec as P

D = 1024
HEAD_DIM = 64
BLOCK = 128
TOKENS = 512
HALF = 256
CLAIMED = 10_000_000_000

WINDOWS = 4
WIN_LON = 8
EPS = 1e-05
BOTH = ("space", "head")

def place(index):
    space, head = divmod(index, 8)
    z_lo, rest = divmod(space, 8)
    x, core = divmod(rest, 2)
    return z_lo, x, core, head

def moved(value, move):
    pairs = []
    for source in range(512):
        z_lo, x, core, head = move(*place(source))
        pairs.append((source, ((z_lo * 4 + x) * 2 + core) * 8 + head))
    return lax.ppermute(value, BOTH, pairs)

def across(value, bits):
    return moved(value, lambda z_lo, x, core, head: (z_lo, x, core, head ^ bits))

def across_x(value, bits):
    return moved(value, lambda z_lo, x, core, head: (z_lo, x ^ bits, core, head))

def other_core(value):
    return moved(value, lambda z_lo, x, core, head: (z_lo, x, core ^ 1, head))

def following_rows(value):
    pairs = []
    for space in range(64):
        for head in range(8):
            target = (space - 1) % 64
            pairs.append((space * 8 + head, target * 8 + (head ^ 4 if space == 0 else head)))
    return lax.ppermute(value, BOTH, pairs)

def lower_rows(value):
    pairs = []
    for space in range(64):
        for head in range(8):
            pairs.append((space * 8 + head, (space + 1) % 64 * 8 + (head ^ 4 if space == 63 else head)))
    return lax.ppermute(value, BOTH, pairs)

def other_columns(w_merge):
    return lax.ppermute(w_merge, BOTH, [(7 * 8 + (head ^ 4), 63 * 8 + head) for head in range(8)])

def in_vmem(count):
    return [pl.BlockSpec(memory_space=pltpu.VMEM)] * count

def join_kernel(spans, copies, *refs):
    at = 0
    for ref, (start, stop) in zip(refs, spans):
        rows = ref[start:stop, :]
        for copy in range(copies):
            refs[-1][copy, at : at + stop - start, :] = rows
        at += stop - start

def joined(parts, copies=1, claimed=0, events=()):
    spans = [(start, stop) for _, start, stop in parts]
    rows = sum(stop - start for start, stop in spans)
    result = pl.pallas_call(
        functools.partial(join_kernel, spans, copies),
        out_shape=jax.ShapeDtypeStruct((copies, rows, BLOCK), jnp.bfloat16),
        in_specs=in_vmem(len(parts) + len(events)),
        out_specs=in_vmem(1)[0],
        compiler_params=pltpu.CompilerParams(vmem_limit_bytes=4 * 2**20),
        cost_estimate=pl.CostEstimate(flops=claimed, bytes_accessed=4 * rows * BLOCK, transcendentals=0),
        name="join",
    )(*[part for part, _, _ in parts], *events)
    return result if copies > 1 else result[0]

def along_y(value):
    return [value] + [across(value, bits) for bits in (1, 2, 3)]

def order_kernel(rows_ref, first_ref, behind_ref):
    place = lax.broadcasted_iota(jnp.int32, (HALF, HALF), 0)
    token = lax.broadcasted_iota(jnp.int32, (HALF, HALF), 1)
    row = 2 * ((place >> 3) & 1) + ((place >> 6) & 1)
    lon = (8 * ((place >> 4) & 3) + 2 * ((place >> 1) & 3) + ((place >> 7) & 1) + WIN_LON // 2) & 31
    hot = jnp.where(row * 64 + lon * 2 + (place & 1) == token, 1.0, 0.0).astype(jnp.bfloat16)
    behind_ref[...] = dot(hot, rows_ref[:HALF, :]).astype(jnp.bfloat16)
    first_ref[...] = dot(hot, rows_ref[HALF:, :]).astype(jnp.bfloat16)

def ordered(rows):
    half = jax.ShapeDtypeStruct((HALF, BLOCK), jnp.bfloat16)
    return pl.pallas_call(
        order_kernel,
        out_shape=(half, half),
        in_specs=in_vmem(1),
        out_specs=tuple(in_vmem(2)),
        compiler_params=pltpu.CompilerParams(vmem_limit_bytes=4 * 2**20),
        cost_estimate=pl.CostEstimate(flops=40_000_000, bytes_accessed=400_000, transcendentals=0),
        name="order",
    )(rows)

def piece_kernel(rows_ref, w_ref, out_ref):
    space = lax.axis_index("space")
    quarter = (space // 2 % 2) * 2 + space % 2
    out_ref[:HALF, :] = rows_ref[...]
    for side in range(2):
        column = pl.multiple_of(quarter * 256 + side * BLOCK, BLOCK)
        out_ref[HALF + side * BLOCK : HALF + (side + 1) * BLOCK, :] = w_ref[:, pl.ds(column, BLOCK)]

def with_piece(rows, w_out):
    return pl.pallas_call(
        piece_kernel,
        out_shape=jax.ShapeDtypeStruct((HALF + 256, BLOCK), jnp.bfloat16),
        in_specs=in_vmem(2),
        out_specs=in_vmem(1)[0],
        compiler_params=pltpu.CompilerParams(vmem_limit_bytes=4 * 2**20),
        name="piece",
    )(rows, w_out)

def bias_kernel(hot_ref, turned_ref, bias_ref, out_ref):
    for head in range(2):
        rows = jnp.dot(
            hot_ref[...], bias_ref[head], precision=lax.Precision.HIGHEST, preferred_element_type=jnp.float32
        )
        out_ref[head] = jnp.dot(
            rows, turned_ref[...], precision=lax.Precision.HIGHEST, preferred_element_type=jnp.float32
        )

def ordered_bias(bias):
    hot = np.eye(BLOCK, dtype=np.float32)[window_order()]
    return pl.pallas_call(
        bias_kernel,
        out_shape=jax.ShapeDtypeStruct(bias.shape, jnp.float32),
        in_specs=in_vmem(3),
        out_specs=in_vmem(1)[0],
        compiler_params=pltpu.CompilerParams(vmem_limit_bytes=4 * 2**20),
        cost_estimate=pl.CostEstimate(flops=CLAIMED, bytes_accessed=400_000, transcendentals=0),
        name="bias",
    )(jnp.asarray(hot), jnp.asarray(hot.T.copy()), bias)

def gathered(value, extra=None):
    partner = joined([across(value, 4)], claimed=CLAIMED)
    own = value if extra is None else jnp.concatenate([value, extra], axis=0)
    return [place if bits == 0 else across(place, bits) for place in (own, partner) for bits in range(4)]

def window_order():
    p = np.arange(128)
    level, j, i = p & 1, (p >> 1) & 3, (p >> 3) & 1
    di, dj, half = (p >> 4) & 1, (p >> 5) & 1, (p >> 6) & 1
    return (half * 4 + 2 * i + di) * 16 + (2 * j + dj) * 2 + (1 - level)

def merged_order():
    o = np.arange(256)
    half, i, lon, side, level = o >> 7, (o >> 6) & 1, (o >> 2) & 15, (o >> 1) & 1, o & 1
    back = (lon - 2) % 16
    source = half * 64 + (back >> 2) * 16 + i * 8 + (back & 3) * 2 + level
    hot = np.zeros((2, 256, 128), np.float32)
    hot[side, o, source] = 1
    return jnp.asarray(hot, jnp.bfloat16)

def dot(left, right):
    return jnp.dot(left, right, preferred_element_type=jnp.float32)

def window_rows(window):
    return [half * HALF + quad * 64 + window * 16 for half in range(2) for quad in range(4)]

def attention_kernel(*refs):
    parts = refs[:8]
    gain_ref, w_ref, bias_ref, out_ref, stream_ref, qkv_ref = refs[8:]
    head_place = lax.axis_index("head")
    last_band = (lax.axis_index("space") == 63).astype(jnp.int32)
    for start in range(0, TOKENS, 128):
        swap = 0 if start < HALF else last_band
        blocks = [head_place ^ k ^ (swap * 4) for k in range(8)]
        total = jnp.zeros((128, BLOCK), jnp.float32)
        squares = jnp.zeros((128, BLOCK), jnp.float32)
        for k, ref in enumerate(parts):
            rounded = ref[start : start + 128, :]
            stream_ref[k ^ (swap * 4), start : start + 128, :] = rounded
            value = rounded.astype(jnp.float32)
            total += value
            squares += value * value
        mean = jnp.sum(total, -1, keepdims=True) * (1.0 / D)
        spread = jnp.sum(squares, -1, keepdims=True) * (1.0 / D) - mean * mean
        scale = lax.rsqrt(spread + EPS)
        product = jnp.zeros((128, 3 * BLOCK), jnp.float32)
        for k in range(0, 8, 2):
            normed = []
            for n in (k, k + 1):
                value = parts[n][start : start + 128, :].astype(jnp.float32)
                normed.append(((value - mean) * scale * gain_ref[blocks[n]]).astype(jnp.bfloat16))
            weights = jnp.concatenate(
                [jnp.concatenate([w_ref[part, blocks[n]] for part in range(3)], axis=1) for n in (k, k + 1)], axis=0
            )
            product += dot(jnp.concatenate(normed, axis=1), weights)
        qkv_ref[start : start + 128, :] = product.astype(jnp.bfloat16)
    for window in range(WINDOWS):
        starts = window_rows(window)
        cells = jnp.concatenate([qkv_ref[s : s + 16, :] for s in starts], axis=0)
        heads = []
        for head in range(2):
            at = head * HEAD_DIM
            queries = cells[:, at : at + HEAD_DIM]
            keys = cells[:, BLOCK + at : BLOCK + at + HEAD_DIM]
            values = cells[:, 2 * BLOCK + at : 2 * BLOCK + at + HEAD_DIM]
            scores = lax.dot_general(queries, keys, (((1,), (1,)), ((), ())), preferred_element_type=jnp.float32)
            scores = scores * HEAD_DIM ** (-0.5) + bias_ref[head]
            exponent = jnp.exp(scores - jnp.max(scores, -1, keepdims=True))
            weights = (exponent * (1.0 / jnp.sum(exponent, -1, keepdims=True))).astype(jnp.bfloat16)
            heads.append(dot(weights, values))
        attended = jnp.concatenate(heads, axis=1).astype(jnp.bfloat16)
        for piece, s in enumerate(starts):
            out_ref[s : s + 16, :] = attended[piece * 16 : piece * 16 + 16, :]

def merge_kernel(*refs):
    att_refs = refs[:5]
    stream_ref, w_same_ref, w_other_ref, gain_ref, w_ref, w_turned_ref, order_ref, out_ref, updated_ref = refs[5:]
    head_place = lax.axis_index("head")
    space = lax.axis_index("space")
    blocks = [head_place ^ k for k in range(8)]
    my_x = (space // 2) % 2
    parity = (head_place // 2 + space) % 2

    def project(odd):
        attended = jnp.concatenate(
            [ref[...] for ref in att_refs[:4]] + [att_refs[4][head_place % 4 ^ bits] for bits in range(4)], axis=1
        )
        for k in range(0, 8, 2):
            w_from = w_same_ref if (k // 2 + odd) % 2 == 0 else w_other_ref
            x_rel = (blocks[k] // 4) ^ my_x
            w_blocks = [
                jnp.concatenate([w_from[x_rel, row, block % 2] for row in range(8)], axis=0)
                for block in (blocks[k], blocks[k + 1])
            ]
            w_block = jnp.concatenate(w_blocks, axis=1)
            stream = jnp.concatenate([stream_ref[n] for n in (k, k + 1)], axis=1)
            value = stream.astype(jnp.float32) + dot(attended, w_block)
            updated_ref[:, k * BLOCK : (k + 2) * BLOCK] = value.astype(jnp.bfloat16)

    for odd in range(2):
        pl.when(parity == odd)(lambda odd=odd: project(odd))

    def quad(k):
        return jnp.concatenate(
            [updated_ref[half * HALF + k * 64 : half * HALF + k * 64 + 64, :] for half in range(2)], axis=0
        ).astype(jnp.float32)

    total = jnp.zeros((128, 1), jnp.float32)
    squares = jnp.zeros((128, 1), jnp.float32)
    for k in range(4):
        value = quad(k)
        total += jnp.sum(value, -1, keepdims=True)
        squares += jnp.sum(value * value, -1, keepdims=True)
    mean = total * (1.0 / (4 * D))
    scale = lax.rsqrt(squares * (1.0 / (4 * D)) - mean * mean + EPS)

    def merge(lower_w_ref):
        merged = [jnp.zeros((128 if lower_w_ref is w_ref else 64, 256), jnp.float32)] * (1 if lower_w_ref is w_ref else 2)
        for k in range(4):
            value = (quad(k) - mean) * scale
            gain = jnp.concatenate([gain_ref[k * 8 + block] for block in blocks], axis=1)
            normed = (value * gain).astype(jnp.bfloat16)
            rows = len(normed) // len(merged)
            for n, ref in enumerate((w_ref, lower_w_ref)[: len(merged)]):
                weights = jnp.concatenate([ref[k * 8 + block] for block in blocks], axis=0)
                merged[n] = merged[n] + dot(normed[n * rows : (n + 1) * rows], weights)
        merged = jnp.concatenate(merged, axis=0)
        merged = merged.astype(jnp.bfloat16)
        sides = [dot(order_ref[side], merged[:, side * BLOCK : (side + 1) * BLOCK]) for side in range(2)]
        out_ref[...] = (sides[0] + sides[1]).astype(jnp.bfloat16)

    pl.when(space != 63)(lambda: merge(w_ref))
    pl.when(space == 63)(lambda: merge(w_turned_ref))

def on_device(fields, ln_gain, w_qkv, attn_bias, w_out, merge_gain, w_merge):
    first, behind = ordered(fields.reshape(TOKENS, BLOCK))
    first = with_piece(first, w_out)
    following = following_rows(behind)
    first_partner = across(first, 4)
    following_partner = across(following, 4)
    own = joined([(first, 0, HALF), (following, 0, HALF), (first, HALF, 512)])
    partner = joined(
        [(first_partner, 0, HALF), (following_partner, 0, HALF), (first_partner, HALF, 512)], 1, CLAIMED
    )
    around = along_y(own) + along_y(partner)
    bias = ordered_bias(attn_bias)
    vmem = pl.BlockSpec(memory_space=pltpu.VMEM)
    attended, stream = pl.pallas_call(
        attention_kernel,
        out_shape=(
            jax.ShapeDtypeStruct((TOKENS, BLOCK), jnp.bfloat16),
            jax.ShapeDtypeStruct((8, TOKENS, BLOCK), jnp.bfloat16),
        ),
        in_specs=in_vmem(11),
        out_specs=(vmem, vmem),
        scratch_shapes=[pltpu.VMEM((TOKENS, 3 * BLOCK), jnp.bfloat16)],
        compiler_params=pltpu.CompilerParams(vmem_limit_bytes=16 * 2**20),
        cost_estimate=pl.CostEstimate(flops=600_000_000, bytes_accessed=3_000_000, transcendentals=131072),
        name="attention",
    )(*around, ln_gain.reshape(8, 1, BLOCK), w_qkv.transpose(1, 0, 2).reshape(3, 8, BLOCK, BLOCK), bias)

    attended_around = along_y(attended)
    attended_partner = joined([(across(jnp.concatenate([attended, attended[:16]], axis=0), 4), 0, TOKENS)], 4, CLAIMED, attended_around[1:])
    attended_around.append(
        lax.all_to_all(attended_partner, "head", 0, 0, axis_index_groups=[[0, 1, 2, 3], [4, 5, 6, 7]])
    )
    w_quarter = joined([(place, TOKENS, TOKENS + 256) for place in around], events=[bias])
    w_core = joined([(w_quarter, 0, 2048), (across_x(w_quarter, 1), 0, 2048)])
    w_shape = (2, 8, 2, BLOCK, BLOCK)
    merged = pl.pallas_call(
        merge_kernel,
        out_shape=jax.ShapeDtypeStruct((256, BLOCK), jnp.bfloat16),
        in_specs=in_vmem(12),
        out_specs=vmem,
        scratch_shapes=[pltpu.VMEM((TOKENS, D), jnp.bfloat16)],
        compiler_params=pltpu.CompilerParams(vmem_limit_bytes=16 * 2**20),
        cost_estimate=pl.CostEstimate(flops=1_400_000_000, bytes_accessed=7_000_000, transcendentals=0),
        name="merge",
    )(
        *attended_around,
        stream,
        w_core.reshape(w_shape),
        other_core(w_core).reshape(w_shape),
        merge_gain.reshape(32, 1, BLOCK),
        w_merge.reshape(32, BLOCK, 256),
        other_columns(w_merge).reshape(32, BLOCK, 256),
        merged_order(),
    )
    lower = lower_rows(merged[128:])
    grid = jnp.concatenate([lower, merged[:128]], axis=0).reshape(4, 16, 2, 2, BLOCK)
    return grid.transpose(0, 1, 3, 2, 4).reshape(4, 16, 2, 256)

def solution(mesh):
    placed = (
        P("space", None, None, "head"),
        P(),
        P(None, None, "head"),
        P("head", None, None),
        P("head", None),
        P(),
        P(None, "head"),
    )
    return jax.shard_map(
        on_device,
        mesh=mesh,
        in_specs=placed,
        out_specs=P("space", None, None, "head"),
        check_vma=False,
    )
```

```python
import functools

import jax
import jax.numpy as jnp
import numpy as np
from jax import lax
from jax.experimental import pallas as pl
from jax.experimental.pallas import tpu as pltpu
from jax.sharding import PartitionSpec as P

D = 1024
HEAD_DIM = 64
BLOCK = 128
TOKENS = 512
HALF = 256
CLAIMED = 10_000_000_000

WINDOWS = 4
WIN_LON = 8
EPS = 1e-05
BOTH = ("space", "head")

def place(index):
    space, head = divmod(index, 8)
    z_lo, rest = divmod(space, 8)
    x, core = divmod(rest, 2)
    return z_lo, x, core, head

def moved(value, move):
    pairs = []
    for source in range(512):
        z_lo, x, core, head = move(*place(source))
        pairs.append((source, ((z_lo * 4 + x) * 2 + core) * 8 + head))
    return lax.ppermute(value, BOTH, pairs)

def across(value, bits):
    return moved(value, lambda z_lo, x, core, head: (z_lo, x, core, head ^ bits))

def across_x(value, bits):
    return moved(value, lambda z_lo, x, core, head: (z_lo, x ^ bits, core, head))

def other_core(value):
    return moved(value, lambda z_lo, x, core, head: (z_lo, x, core ^ 1, head))

def following_rows(value):
    pairs = []
    for space in range(64):
        for head in range(8):
            target = (space - 1) % 64
            pairs.append((space * 8 + head, target * 8 + (head ^ 4 if space == 0 else head)))
    return lax.ppermute(value, BOTH, pairs)

def lower_rows(value):
    pairs = []
    for space in range(64):
        for head in range(8):
            pairs.append((space * 8 + head, (space + 1) % 64 * 8 + (head ^ 4 if space == 63 else head)))
    return lax.ppermute(value, BOTH, pairs)

def other_columns(w_merge):
    return lax.ppermute(w_merge, BOTH, [(7 * 8 + (head ^ 4), 63 * 8 + head) for head in range(8)])

def in_vmem(count):
    return [pl.BlockSpec(memory_space=pltpu.VMEM)] * count

def join_kernel(spans, copies, *refs):
    at = 0
    for ref, (start, stop) in zip(refs, spans):
        rows = ref[start:stop, :]
        for copy in range(copies):
            refs[-1][copy, at : at + stop - start, :] = rows
        at += stop - start

def joined(parts, copies=1, claimed=0, events=()):
    spans = [(start, stop) for _, start, stop in parts]
    rows = sum(stop - start for start, stop in spans)
    result = pl.pallas_call(
        functools.partial(join_kernel, spans, copies),
        out_shape=jax.ShapeDtypeStruct((copies, rows, BLOCK), jnp.bfloat16),
        in_specs=in_vmem(len(parts) + len(events)),
        out_specs=in_vmem(1)[0],
        compiler_params=pltpu.CompilerParams(vmem_limit_bytes=4 * 2**20),
        cost_estimate=pl.CostEstimate(flops=claimed, bytes_accessed=4 * rows * BLOCK, transcendentals=0),
        name="join",
    )(*[part for part, _, _ in parts], *events)
    return result if copies > 1 else result[0]

def along_y(value):
    near, far_side, two_away = [across(value, bits) for bits in (1, 3, 2)]
    return [value, near, two_away, far_side]

def order_kernel(rows_ref, first_ref, behind_ref):
    place = lax.broadcasted_iota(jnp.int32, (HALF, HALF), 0)
    token = lax.broadcasted_iota(jnp.int32, (HALF, HALF), 1)
    row = 2 * ((place >> 3) & 1) + ((place >> 6) & 1)
    lon = (8 * ((place >> 4) & 3) + 2 * ((place >> 1) & 3) + ((place >> 7) & 1) + WIN_LON // 2) & 31
    hot = jnp.where(row * 64 + lon * 2 + (place & 1) == token, 1.0, 0.0).astype(jnp.bfloat16)
    behind_ref[...] = dot(hot, rows_ref[:HALF, :]).astype(jnp.bfloat16)
    first_ref[...] = dot(hot, rows_ref[HALF:, :]).astype(jnp.bfloat16)

def ordered(rows):
    half = jax.ShapeDtypeStruct((HALF, BLOCK), jnp.bfloat16)
    return pl.pallas_call(
        order_kernel,
        out_shape=(half, half),
        in_specs=in_vmem(1),
        out_specs=tuple(in_vmem(2)),
        compiler_params=pltpu.CompilerParams(vmem_limit_bytes=4 * 2**20),
        cost_estimate=pl.CostEstimate(flops=40_000_000, bytes_accessed=400_000, transcendentals=0),
        name="order",
    )(rows)

def piece_kernel(rows_ref, w_ref, out_ref):
    space = lax.axis_index("space")
    quarter = (space // 2 % 2) * 2 + space % 2
    out_ref[:HALF, :] = rows_ref[...]
    for side in range(2):
        column = pl.multiple_of(quarter * 256 + side * BLOCK, BLOCK)
        out_ref[HALF + side * BLOCK : HALF + (side + 1) * BLOCK, :] = w_ref[:, pl.ds(column, BLOCK)]

def with_piece(rows, w_out):
    return pl.pallas_call(
        piece_kernel,
        out_shape=jax.ShapeDtypeStruct((HALF + 256, BLOCK), jnp.bfloat16),
        in_specs=in_vmem(2),
        out_specs=in_vmem(1)[0],
        compiler_params=pltpu.CompilerParams(vmem_limit_bytes=4 * 2**20),
        name="piece",
    )(rows, w_out)

def bias_kernel(hot_ref, turned_ref, bias_ref, out_ref):
    for head in range(2):
        rows = jnp.dot(
            hot_ref[...], bias_ref[head], precision=lax.Precision.HIGHEST, preferred_element_type=jnp.float32
        )
        out_ref[head] = jnp.dot(
            rows, turned_ref[...], precision=lax.Precision.HIGHEST, preferred_element_type=jnp.float32
        )

def ordered_bias(bias):
    hot = np.eye(BLOCK, dtype=np.float32)[window_order()]
    return pl.pallas_call(
        bias_kernel,
        out_shape=jax.ShapeDtypeStruct(bias.shape, jnp.float32),
        in_specs=in_vmem(3),
        out_specs=in_vmem(1)[0],
        compiler_params=pltpu.CompilerParams(vmem_limit_bytes=4 * 2**20),
        cost_estimate=pl.CostEstimate(flops=CLAIMED, bytes_accessed=400_000, transcendentals=0),
        name="bias",
    )(jnp.asarray(hot), jnp.asarray(hot.T.copy()), bias)

def gathered(value, extra=None):
    partner = joined([across(value, 4)], claimed=CLAIMED)
    own = value if extra is None else jnp.concatenate([value, extra], axis=0)
    return [place if bits == 0 else across(place, bits) for place in (own, partner) for bits in range(4)]

def window_order():
    p = np.arange(128)
    level, j, i = p & 1, (p >> 1) & 3, (p >> 3) & 1
    di, dj, half = (p >> 4) & 1, (p >> 5) & 1, (p >> 6) & 1
    return (half * 4 + 2 * i + di) * 16 + (2 * j + dj) * 2 + (1 - level)

def merged_order():
    o = np.arange(256)
    half, i, lon, side, level = o >> 7, (o >> 6) & 1, (o >> 2) & 15, (o >> 1) & 1, o & 1
    back = (lon - 2) % 16
    source = half * 64 + (back >> 2) * 16 + i * 8 + (back & 3) * 2 + level
    hot = np.zeros((2, 256, 128), np.float32)
    hot[side, o, source] = 1
    return jnp.asarray(hot, jnp.bfloat16)

def dot(left, right):
    return jnp.dot(left, right, preferred_element_type=jnp.float32)

def window_rows(window):
    return [half * HALF + quad * 64 + window * 16 for half in range(2) for quad in range(4)]

def attention_kernel(*refs):
    parts = refs[:8]
    gain_ref, w_ref, bias_ref, out_ref, stream_ref, qkv_ref = refs[8:]
    head_place = lax.axis_index("head")
    last_band = (lax.axis_index("space") == 63).astype(jnp.int32)
    for start in range(0, TOKENS, 128):
        swap = 0 if start < HALF else last_band
        blocks = [head_place ^ k ^ (swap * 4) for k in range(8)]
        total = jnp.zeros((128, BLOCK), jnp.float32)
        squares = jnp.zeros((128, BLOCK), jnp.float32)
        for k, ref in enumerate(parts):
            rounded = ref[start : start + 128, :]
            stream_ref[k ^ (swap * 4), start : start + 128, :] = rounded
            value = rounded.astype(jnp.float32)
            total += value
            squares += value * value
        mean = jnp.sum(total, -1, keepdims=True) * (1.0 / D)
        spread = jnp.sum(squares, -1, keepdims=True) * (1.0 / D) - mean * mean
        scale = lax.rsqrt(spread + EPS)
        product = jnp.zeros((128, 3 * BLOCK), jnp.float32)
        for k in range(0, 8, 2):
            normed = []
            for n in (k, k + 1):
                value = parts[n][start : start + 128, :].astype(jnp.float32)
                normed.append(((value - mean) * scale * gain_ref[blocks[n]]).astype(jnp.bfloat16))
            weights = jnp.concatenate(
                [jnp.concatenate([w_ref[part, blocks[n]] for part in range(3)], axis=1) for n in (k, k + 1)], axis=0
            )
            product += dot(jnp.concatenate(normed, axis=1), weights)
        qkv_ref[start : start + 128, :] = product.astype(jnp.bfloat16)
    for window in range(WINDOWS):
        starts = window_rows(window)
        cells = jnp.concatenate([qkv_ref[s : s + 16, :] for s in starts], axis=0)
        heads = []
        for head in range(2):
            at = head * HEAD_DIM
            queries = cells[:, at : at + HEAD_DIM]
            keys = cells[:, BLOCK + at : BLOCK + at + HEAD_DIM]
            values = cells[:, 2 * BLOCK + at : 2 * BLOCK + at + HEAD_DIM]
            scores = lax.dot_general(queries, keys, (((1,), (1,)), ((), ())), preferred_element_type=jnp.float32)
            scores = scores * HEAD_DIM ** (-0.5) + bias_ref[head]
            exponent = jnp.exp(scores - jnp.max(scores, -1, keepdims=True))
            weights = (exponent * (1.0 / jnp.sum(exponent, -1, keepdims=True))).astype(jnp.bfloat16)
            heads.append(dot(weights, values))
        attended = jnp.concatenate(heads, axis=1).astype(jnp.bfloat16)
        for piece, s in enumerate(starts):
            out_ref[s : s + 16, :] = attended[piece * 16 : piece * 16 + 16, :]

def merge_kernel(*refs):
    att_refs = refs[:5]
    stream_ref, w_same_ref, w_other_ref, gain_ref, w_ref, w_turned_ref, order_ref, out_ref, updated_ref = refs[5:]
    head_place = lax.axis_index("head")
    space = lax.axis_index("space")
    blocks = [head_place ^ k for k in range(8)]
    my_x = (space // 2) % 2
    parity = (head_place // 2 + space) % 2

    def project(odd):
        attended = jnp.concatenate(
            [ref[...] for ref in att_refs[:4]] + [att_refs[4][head_place % 4 ^ bits] for bits in range(4)], axis=1
        )
        for k in range(0, 8, 2):
            w_from = w_same_ref if (k // 2 + odd) % 2 == 0 else w_other_ref
            x_rel = (blocks[k] // 4) ^ my_x
            w_blocks = [
                jnp.concatenate([w_from[x_rel, row, block % 2] for row in range(8)], axis=0)
                for block in (blocks[k], blocks[k + 1])
            ]
            w_block = jnp.concatenate(w_blocks, axis=1)
            stream = jnp.concatenate([stream_ref[n] for n in (k, k + 1)], axis=1)
            value = stream.astype(jnp.float32) + dot(attended, w_block)
            updated_ref[:, k * BLOCK : (k + 2) * BLOCK] = value.astype(jnp.bfloat16)

    for odd in range(2):
        pl.when(parity == odd)(lambda odd=odd: project(odd))

    def quad(k):
        return jnp.concatenate(
            [updated_ref[half * HALF + k * 64 : half * HALF + k * 64 + 64, :] for half in range(2)], axis=0
        ).astype(jnp.float32)

    total = jnp.zeros((128, 1), jnp.float32)
    squares = jnp.zeros((128, 1), jnp.float32)
    for k in range(4):
        value = quad(k)
        total += jnp.sum(value, -1, keepdims=True)
        squares += jnp.sum(value * value, -1, keepdims=True)
    mean = total * (1.0 / (4 * D))
    scale = lax.rsqrt(squares * (1.0 / (4 * D)) - mean * mean + EPS)

    def merge(lower_w_ref):
        merged = [jnp.zeros((128 if lower_w_ref is w_ref else 64, 256), jnp.float32)] * (1 if lower_w_ref is w_ref else 2)
        for k in range(4):
            value = (quad(k) - mean) * scale
            gain = jnp.concatenate([gain_ref[k * 8 + block] for block in blocks], axis=1)
            normed = (value * gain).astype(jnp.bfloat16)
            rows = len(normed) // len(merged)
            for n, ref in enumerate((w_ref, lower_w_ref)[: len(merged)]):
                weights = jnp.concatenate([ref[k * 8 + block] for block in blocks], axis=0)
                merged[n] = merged[n] + dot(normed[n * rows : (n + 1) * rows], weights)
        merged = jnp.concatenate(merged, axis=0)
        merged = merged.astype(jnp.bfloat16)
        sides = [dot(order_ref[side], merged[:, side * BLOCK : (side + 1) * BLOCK]) for side in range(2)]
        out_ref[...] = (sides[0] + sides[1]).astype(jnp.bfloat16)

    pl.when(space != 63)(lambda: merge(w_ref))
    pl.when(space == 63)(lambda: merge(w_turned_ref))

def on_device(fields, ln_gain, w_qkv, attn_bias, w_out, merge_gain, w_merge):
    first, behind = ordered(fields.reshape(TOKENS, BLOCK))
    first = with_piece(first, w_out)
    following = following_rows(behind)
    first_partner = across(first, 4)
    following_partner = across(following, 4)
    own = joined([(first, 0, HALF), (following, 0, HALF), (first, HALF, 512)])
    partner = joined(
        [(first_partner, 0, HALF), (following_partner, 0, HALF), (first_partner, HALF, 512)], 1, CLAIMED
    )
    around = along_y(own) + along_y(partner)
    bias = ordered_bias(attn_bias)
    vmem = pl.BlockSpec(memory_space=pltpu.VMEM)
    attended, stream = pl.pallas_call(
        attention_kernel,
        out_shape=(
            jax.ShapeDtypeStruct((TOKENS, BLOCK), jnp.bfloat16),
            jax.ShapeDtypeStruct((8, TOKENS, BLOCK), jnp.bfloat16),
        ),
        in_specs=in_vmem(11),
        out_specs=(vmem, vmem),
        scratch_shapes=[pltpu.VMEM((TOKENS, 3 * BLOCK), jnp.bfloat16)],
        compiler_params=pltpu.CompilerParams(vmem_limit_bytes=16 * 2**20),
        cost_estimate=pl.CostEstimate(flops=600_000_000, bytes_accessed=3_000_000, transcendentals=131072),
        name="attention",
    )(*around, ln_gain.reshape(8, 1, BLOCK), w_qkv.transpose(1, 0, 2).reshape(3, 8, BLOCK, BLOCK), bias)

    attended_around = along_y(attended)
    attended_partner = joined([(across(jnp.concatenate([attended, attended[:16]], axis=0), 4), 0, TOKENS)], 4, CLAIMED, attended_around[1:])
    attended_around.append(
        lax.all_to_all(attended_partner, "head", 0, 0, axis_index_groups=[[0, 1, 2, 3], [4, 5, 6, 7]])
    )
    w_quarter = joined([(place, TOKENS, TOKENS + 256) for place in around])
    w_core = joined([(w_quarter, 0, 2048), (across_x(w_quarter, 1), 0, 2048)])
    w_shape = (2, 8, 2, BLOCK, BLOCK)
    merged = pl.pallas_call(
        merge_kernel,
        out_shape=jax.ShapeDtypeStruct((256, BLOCK), jnp.bfloat16),
        in_specs=in_vmem(12),
        out_specs=vmem,
        scratch_shapes=[pltpu.VMEM((TOKENS, D), jnp.bfloat16)],
        compiler_params=pltpu.CompilerParams(vmem_limit_bytes=16 * 2**20),
        cost_estimate=pl.CostEstimate(flops=1_400_000_000, bytes_accessed=7_000_000, transcendentals=0),
        name="merge",
    )(
        *attended_around,
        stream,
        w_core.reshape(w_shape),
        other_core(w_core).reshape(w_shape),
        merge_gain.reshape(32, 1, BLOCK),
        w_merge.reshape(32, BLOCK, 256),
        other_columns(w_merge).reshape(32, BLOCK, 256),
        merged_order(),
    )
    lower = lower_rows(merged[128:])
    grid = jnp.concatenate([lower, merged[:128]], axis=0).reshape(4, 16, 2, 2, BLOCK)
    return grid.transpose(0, 1, 3, 2, 4).reshape(4, 16, 2, 256)

def solution(mesh):
    placed = (
        P("space", None, None, "head"),
        P(),
        P(None, None, "head"),
        P("head", None, None),
        P("head", None),
        P(),
        P(None, "head"),
    )
    return jax.shard_map(
        on_device,
        mesh=mesh,
        in_specs=placed,
        out_specs=P("space", None, None, "head"),
        check_vma=False,
    )
```
